32 devices in a mesh: dp: 8 (over y, x, core), ctx: 4 (over z).
Axes of the slice: x: 2, y: 2, z: 4, core: 2. Of those that a mesh axis runs over, the one named last changes fastest.
Arguments:
- hidden_in: bfloat16 [2, 8, 1024, 1024], P(None, 'dp', 'ctx'), may hold values from -6 to 6
- out_grad: bfloat16 [2, 8, 1024, 1024], P(None, 'dp', 'ctx'), may hold values from -6 to 6
- segment_ids: int32 [2, 8, 1024], P(None, 'dp', 'ctx'), may hold values from 0 to 5, as said below
- doc_positions: int32 [2, 8, 1024], P(None, 'dp', 'ctx'), may hold values from 0 to 1021, as said below
- attn_gain: bfloat16 [1024], P(('dp', 'ctx')), may hold values from 0.5 to 1.5
- head_gains: bfloat16 [128], P(('dp', 'ctx')), may hold values from 0.5 to 1.5
- w_query: bfloat16 [1024, 1024], P(('dp', 'ctx')), may hold values from -0.1875 to 0.1875
- w_key: bfloat16 [1024, 512], P(('dp', 'ctx')), may hold values from -0.1875 to 0.1875
- w_value: bfloat16 [1024, 512], P(('dp', 'ctx')), may hold values from -0.1875 to 0.1875
- w_out: bfloat16 [1024, 1024], P(('dp', 'ctx')), may hold values from -1.5 to 1.5
- ffn_gain: bfloat16 [1024], P(('dp', 'ctx')), may hold values from 0.5 to 1.5
- w_gate: bfloat16 [1024, 4608], P(('dp', 'ctx')), may hold values from -0.1875 to 0.1875
- w_up: bfloat16 [1024, 4608], P(('dp', 'ctx')), may hold values from -0.1875 to 0.1875
- w_down: bfloat16 [4608, 1024], P(('dp', 'ctx')), may hold values from -0.09375 to 0.09375
Outputs:
- block_out: bfloat16 [2, 8, 1024, 1024], P(None, 'dp', 'ctx')
- in_grad: bfloat16 [2, 8, 1024, 1024], P(None, 'dp', 'ctx')
- attn_gain_grad: float32 [1024], P(('dp', 'ctx'))
- head_gains_grad: float32 [128], P(('dp', 'ctx'))
- w_query_grad: float32 [1024, 1024], P(('dp', 'ctx'))
- w_key_grad: float32 [1024, 512], P(('dp', 'ctx'))
- w_value_grad: float32 [1024, 512], P(('dp', 'ctx'))
- w_out_grad: float32 [1024, 1024], P(('dp', 'ctx'))
- ffn_gain_grad: float32 [1024], P(('dp', 'ctx'))
- w_gate_grad: float32 [1024, 4608], P(('dp', 'ctx'))
- w_up_grad: float32 [1024, 4608], P(('dp', 'ctx'))
- w_down_grad: float32 [4608, 1024], P(('dp', 'ctx'))
The draws below stay inside these ranges and needn't reach their ends.
Inputs may be any that keep to these rules, and one draw needn't show every extreme that they name: `segment_ids`: in each sequence the ids start at 0, rise by one at each new document and never fall. In one sequence of each index of the second dimension a single document starts within the first 256 tokens and ends within the last 256, the tokens before and after it forming one document each; in the sequence at index 0 of the second dimension that document runs from token 1 to token 1022, and the other sequence there packs documents of 200 tokens. The other sequences pack documents of 200 to 2000 tokens and at most 1022, the last one cut at the sequence's end. `doc_positions`: each token's place within its document, counting from 0 at the document's first token.
All inputs are finite; a program needn't handle non-finite values.
Results may differ from the reference program's by a relative error of at most 0.022.
Values may be sent and summed in bfloat16 or wider, within the bound.
No kernel may reach another device: no remote copies, remote signals or barrier semaphores. Data moves between devices by JAX's collectives and lax.ppermute only.
A program may use at most 320 MiB of HBM per device.

```python
import math
import jax
import jax.numpy as jnp
from jax import lax

D = 1024
HEADS = 16
KV_HEADS = 8
HEAD = 64
FF = 4608
TOK_DEV = 256
MICRO = 2
DOC_LO = 200
DOC_HI = 2000
BATCH = 8
SEQ = 1024


def packed_layout(key):
    count = SEQ // DOC_LO + 3
    longest = min(DOC_HI, SEQ - 2)
    lengths = jax.random.randint(jax.random.fold_in(key, 11), (MICRO, BATCH, count), DOC_LO, longest + 1)
    first_row = (jnp.arange(BATCH) == 0)[None, :, None]
    lengths = jnp.where(first_row, DOC_LO, lengths)
    bounds = jnp.cumsum(lengths, -1) - lengths
    front = jax.random.randint(jax.random.fold_in(key, 12), (MICRO, BATCH), 1, TOK_DEV)
    tail = jax.random.randint(jax.random.fold_in(key, 13), (MICRO, BATCH), 1, TOK_DEV)
    first_col = (jnp.arange(BATCH) == 0)[None, :]
    front = jnp.where(first_col, 1, front)
    tail = jnp.where(first_col, 1, tail)
    spanning = jnp.concatenate([jnp.zeros((MICRO, BATCH, 1), jnp.int32), front[..., None], (SEQ - tail)[..., None], jnp.full((MICRO, BATCH, count - 3), SEQ, jnp.int32)], -1)
    chosen = jax.random.randint(jax.random.fold_in(key, 14), (BATCH,), 0, MICRO)
    picked = (jnp.arange(MICRO)[:, None] == chosen[None, :])[..., None]
    bounds = jnp.where(picked, spanning, bounds)
    places = jnp.arange(SEQ, dtype=jnp.int32)
    inside = bounds[..., None, :] <= places[:, None]
    segments = jnp.sum(inside.astype(jnp.int32), -1) - 1
    starts = jnp.max(jnp.where(inside, bounds[..., None, :], 0), -1)
    return (segments.astype(jnp.int32), (places - starts).astype(jnp.int32))


def draw_segment_ids(key, part):
    segments, places = packed_layout(key)
    return segments


def draw_doc_positions(key, part):
    segments, places = packed_layout(key)
    return places


def block_scale(own_key, dims, split, smallest, largest):
    loudness = 1.0
    for dim, parts in split:
        steps = jax.random.uniform(jax.random.fold_in(jax.random.fold_in(own_key, 6), dim), (parts,), jnp.float32, smallest / len(split), largest / len(split))
        loudness = loudness * jnp.repeat(jnp.exp(steps), dims[dim] // parts).reshape((-1,) + (1,) * (len(dims) - 1 - dim))
    return loudness


def centred(stream_key, extent, scale, bound, cuts=(), held_as=jnp.bfloat16):
    result = jax.random.normal(stream_key, extent, jnp.float32) * scale
    if len(cuts) > 0:
        result = block_scale(stream_key, extent, cuts, -0.22, 0.18) * result
    return jnp.clip(result, min=-bound, max=bound).astype(held_as)


def setup_inputs(seed: int = 0) -> dict:
    splits = jax.random.split(jax.random.key(seed), 15)
    hidden_in = centred(splits[0], (MICRO, BATCH, SEQ, D), 1.0, 6.0, ((1, 8), (2, 4)))
    out_grad = centred(splits[1], (MICRO, BATCH, SEQ, D), 1.0, 6.0, ((1, 8), (2, 4)))
    segment_ids = draw_segment_ids(jax.random.fold_in(splits[14], 71), 0)
    doc_positions = draw_doc_positions(jax.random.fold_in(splits[14], 71), 0)
    attn_gain = jnp.clip(1.0 + 0.1 * jax.random.normal(splits[4], (D,), jnp.float32), 0.5, 1.5).astype(jnp.bfloat16)
    head_gains = jnp.clip(1.0 + 0.1 * jax.random.normal(splits[5], (2 * HEAD,), jnp.float32), 0.5, 1.5).astype(jnp.bfloat16)
    w_query = centred(splits[6], (D, HEADS * HEAD), D ** -0.5, 0.1875, ((0, 32),))
    w_key = centred(splits[7], (D, KV_HEADS * HEAD), D ** -0.5, 0.1875, ((0, 32),))
    w_value = centred(splits[8], (D, KV_HEADS * HEAD), D ** -0.5, 0.1875, ((0, 32),))
    w_out = centred(splits[9], (HEADS * HEAD, D), (D // 64) ** -0.5, 1.5, ((0, 32),))
    ffn_gain = jnp.clip(1.0 + 0.1 * jax.random.normal(splits[10], (D,), jnp.float32), 0.5, 1.5).astype(jnp.bfloat16)
    w_gate = centred(splits[11], (D, FF), D ** -0.5, 0.1875, ((0, 32),))
    w_up = centred(splits[12], (D, FF), D ** -0.5, 0.1875, ((0, 32),))
    w_down = centred(splits[13], (FF, D), FF ** -0.5, 0.09375, ((0, 32),))
    return {"hidden_in": hidden_in, "out_grad": out_grad, "segment_ids": segment_ids, "doc_positions": doc_positions, "attn_gain": attn_gain, "head_gains": head_gains, "w_query": w_query, "w_key": w_key, "w_value": w_value, "w_out": w_out, "ffn_gain": ffn_gain, "w_gate": w_gate, "w_up": w_up, "w_down": w_down}


@jax.custom_vjp
def low(v):
    return lax.optimization_barrier(v.astype(jnp.bfloat16)).astype(jnp.float32)

@jax.custom_vjp
def low_back(v):
    return v

def low_keep(v):
    return (low(v), None)

def low_pass(kept, grad):
    return (grad,)

def back_keep(v):
    return (v, None)

def back_low(kept, grad):
    return (low(grad),)
low.defvjp(low_keep, low_pass)
low_back.defvjp(back_keep, back_low)
EPS = 1e-05
THETA = 1000000.0

def matmul(left, right):
    return jnp.dot(left, right, precision=lax.Precision.HIGHEST)

def rms_norm(values, gain):
    return values * lax.rsqrt(lax.optimization_barrier(jnp.mean(values * values, -1, keepdims=True)) + EPS) * gain

def angles(places, half):
    freq = THETA ** (-(jnp.arange(half, dtype=jnp.float32) * 2.0 / (2 * half)))
    turn = places.astype(jnp.float32)[:, None] * freq[None, :]
    return (jnp.cos(turn)[:, None, :], jnp.sin(turn)[:, None, :])

def rotate(values, cosine, sine):
    half = values.shape[-1] // 2
    first = values[..., :half]
    second = values[..., half:]
    return jnp.concatenate([first * cosine - second * sine, second * cosine + first * sine], -1)

def sequence_forward(values, segments, places, attn_gain, head_gains, w_query, w_key, w_value, w_out, ffn_gain, w_gate, w_up, w_down):
    length = values.shape[0]
    group = HEADS // KV_HEADS
    a_low = low(rms_norm(values, attn_gain))
    query = low_back(matmul(a_low, w_query)).reshape(length, HEADS, HEAD)
    keys = low_back(matmul(a_low, w_key)).reshape(length, KV_HEADS, HEAD)
    vals = low(low_back(matmul(a_low, w_value))).reshape(length, KV_HEADS, HEAD)
    cosine, sine = angles(places, HEAD // 2)
    query = low(rotate(rms_norm(query, head_gains[:HEAD]), cosine, sine))
    keys = low(rotate(rms_norm(keys, head_gains[HEAD:]), cosine, sine))
    grouped = query.reshape(length, KV_HEADS, group, HEAD)
    block = math.gcd(length, 512)
    index = jnp.arange(length, dtype=jnp.int32)

    def attend(start):
        part_query = lax.dynamic_slice_in_dim(grouped, start, block, 0)
        part_segments = lax.dynamic_slice_in_dim(segments, start, block, 0)
        rows_here = start + jnp.arange(block, dtype=jnp.int32)
        scores = jnp.einsum('qkgd,skd->kgqs', part_query, keys, precision=lax.Precision.HIGHEST) * HEAD ** (-0.5)
        scores = low_back(scores)
        allowed = (part_segments[:, None] == segments[None, :]) & (rows_here[:, None] >= index[None, :])
        scores = jnp.where(allowed, scores, -1e+30)
        peak = lax.optimization_barrier(jnp.max(scores, -1, keepdims=True))
        expo = jnp.exp(scores - peak)
        probs = low(expo / lax.optimization_barrier(jnp.sum(expo, -1, keepdims=True)))
        return jnp.einsum('kgqs,skd->qkgd', probs, vals, precision=lax.Precision.HIGHEST)
    starts = jnp.arange(length // block, dtype=jnp.int32) * block
    attended = lax.map(jax.checkpoint(attend), starts).reshape(length, HEADS * HEAD)
    attended = low(low_back(attended))
    hidden = values + low_back(matmul(attended, w_out))
    b_low = low(rms_norm(hidden, ffn_gain))
    gate = low_back(matmul(b_low, w_gate))
    upper = low_back(matmul(b_low, w_up))
    act = low(jax.nn.silu(gate) * upper)
    return hidden + low_back(matmul(act, w_down))

def reference(hidden_in, out_grad, segment_ids, doc_positions, attn_gain, head_gains, w_query, w_key, w_value, w_out, ffn_gain, w_gate, w_up, w_down):
    weights = tuple((w.astype(jnp.float32) for w in (attn_gain, head_gains, w_query, w_key, w_value, w_out, ffn_gain, w_gate, w_up, w_down)))
    count = hidden_in.shape[0] * hidden_in.shape[1]
    inputs = hidden_in.reshape(count, SEQ, D)
    cotangents = out_grad.reshape(count, SEQ, D)
    segments_all = segment_ids.reshape(count, SEQ)
    places_all = doc_positions.reshape(count, SEQ)

    def one_sequence(totals, item):
        values, cotangent, segments, places = item

        def forward(values_f, *params):
            return sequence_forward(values_f, segments, places, *params)
        output, pullback = jax.vjp(forward, values.astype(jnp.float32), *weights)
        grads = pullback(cotangent.astype(jnp.float32))
        totals = tuple((left + right for left, right in zip(totals, grads[1:])))
        return (totals, (output.astype(jnp.bfloat16), grads[0].astype(jnp.bfloat16)))
    zeros = tuple((jnp.zeros_like(w) for w in weights))
    totals, (outputs, in_grads) = lax.scan(one_sequence, zeros, (inputs, cotangents, segments_all, places_all))
    shape = hidden_in.shape
    return (outputs.reshape(shape), in_grads.reshape(shape), totals[0], totals[1], totals[2], totals[3], totals[4], totals[5], totals[6], totals[7], totals[8], totals[9])
```

```python
import functools

import jax
import jax.numpy as jnp
from jax import lax
from jax.experimental import pallas as pl
from jax.experimental.pallas import tpu as pltpu
from jax.sharding import PartitionSpec as P

EPS = 1e-05
THETA = 1000000.0


def matmul(left, right):
    return jnp.dot(left, right, preferred_element_type=jnp.float32)


def left_trans(left, right):
    return lax.dot_general(
        left, right, (((0,), (0,)), ((), ())), preferred_element_type=jnp.float32
    )


def right_trans(left, right):
    return lax.dot_general(
        left, right, (((1,), (1,)), ((), ())), preferred_element_type=jnp.float32
    )


def norm_forward(values, gain):
    factor = lax.rsqrt(jnp.mean(values * values, -1, keepdims=True) + EPS)
    unit = values * factor
    return (unit * gain, unit, factor)


def norm_backward(incoming, unit, factor, gain):
    scaled = incoming * gain
    result = factor * (scaled - unit * jnp.mean(scaled * unit, -1, keepdims=True))
    return (result, incoming * unit)


def angles(places, half):
    freq = THETA ** (-(jnp.arange(half, dtype=jnp.float32) * 2.0 / (2 * half)))
    turn = places.astype(jnp.float32)[:, None] * freq[None, :]
    return (jnp.cos(turn)[:, None, :], jnp.sin(turn)[:, None, :])


def rotate(values, cosine, sine, sign):
    half = values.shape[-1] // 2
    first = values[..., :half]
    second = values[..., half:]
    return jnp.concatenate(
        [first * cosine - sign * second * sine, second * cosine + sign * first * sine], -1
    )


def fetch_weights(shards):
    return (
        lax.all_gather(shards[0], ("dp", "ctx"), axis=0, tiled=True),
        lax.all_gather(shards[1], ("dp", "ctx"), axis=0, tiled=True),
        lax.all_gather(shards[2], ("dp", "ctx"), axis=0, tiled=True),
        lax.all_gather(shards[3], ("dp", "ctx"), axis=0, tiled=True),
        lax.all_gather(shards[4], ("dp", "ctx"), axis=0, tiled=True),
        lax.all_gather(shards[5], ("dp", "ctx"), axis=0, tiled=True),
        lax.all_gather(shards[6], ("dp", "ctx"), axis=0, tiled=True),
        lax.all_gather(shards[7], ("dp", "ctx"), axis=0, tiled=True),
        lax.all_gather(shards[8], ("dp", "ctx"), axis=0, tiled=True),
        lax.all_gather(shards[9], ("dp", "ctx"), axis=0, tiled=True),
    )


def fetch_again(shards):
    return (
        lax.all_gather(shards[0], ("dp", "ctx"), axis=0, tiled=True),
        lax.all_gather(shards[1], ("dp", "ctx"), axis=0, tiled=True),
        lax.all_gather(shards[2], ("dp", "ctx"), axis=0, tiled=True),
        lax.all_gather(shards[3], ("dp", "ctx"), axis=0, tiled=True),
        lax.all_gather(shards[4], ("dp", "ctx"), axis=0, tiled=True),
        lax.all_gather(shards[5], ("dp", "ctx"), axis=0, tiled=True),
        lax.all_gather(shards[6], ("dp", "ctx"), axis=0, tiled=True),
        lax.all_gather(shards[7], ("dp", "ctx"), axis=0, tiled=True),
        lax.all_gather(shards[8], ("dp", "ctx"), axis=0, tiled=True),
        lax.all_gather(shards[9], ("dp", "ctx"), axis=0, tiled=True),
    )


def attention_forward(query_low, key_low, value_low, segments, again):
    rows, heads, head = query_low.shape
    kv_heads = key_low.shape[1] // head
    group = heads // kv_heads
    scale = head ** (-0.5)
    grouped = query_low.reshape(rows, kv_heads, group, head)
    query_index = lax.axis_index("ctx") * rows + jnp.arange(rows, dtype=jnp.int32)

    def visit(carry, piece):
        highest, total, summed = carry
        key_piece, value_piece, segment_piece = piece
        width = key_piece.shape[0]
        key_heads = key_piece.reshape(width, kv_heads, head)
        value_heads = value_piece.reshape(width, kv_heads, head)
        scores = (
            jnp.einsum("qkgd,skd->kgqs", grouped, key_heads, preferred_element_type=jnp.float32)
            * scale
        )
        key_index = jnp.arange(width, dtype=jnp.int32)
        allowed = (segments[:, None] == segment_piece[None, :]) & (
            query_index[:, None] >= key_index[None, :]
        )
        scores = jnp.where(allowed, scores, -1e30)
        peak = jnp.maximum(highest, jnp.max(scores, -1))
        weight = jnp.where(allowed, jnp.exp(scores - peak[..., None]), 0.0)
        total = jnp.sum(weight, -1)
        summed = jnp.einsum(
            "kgqs,skd->qkgd",
            weight.astype(jnp.bfloat16),
            value_heads,
            preferred_element_type=jnp.float32,
        )
        return (peak, total, summed)

    initial = (
        jnp.full((kv_heads, group, rows), -1e30, jnp.float32),
        jnp.zeros((kv_heads, group, rows), jnp.float32),
        jnp.zeros((rows, kv_heads, group, head), jnp.float32),
    )
    if again:
        highest, total, summed = visit(
            initial,
            (
                lax.all_gather(key_low, "ctx", axis=0, tiled=True),
                lax.all_gather(value_low, "ctx", axis=0, tiled=True),
                lax.all_gather(segments, "ctx", axis=0, tiled=True),
            ),
        )
    else:
        highest, total, summed = visit(
            initial,
            (
                lax.all_gather(key_low, "ctx", axis=0, tiled=True),
                lax.all_gather(value_low, "ctx", axis=0, tiled=True),
                lax.all_gather(segments, "ctx", axis=0, tiled=True),
            ),
        )
    attended = (summed / jnp.transpose(total, (2, 0, 1))[..., None]).reshape(rows, heads, head)
    return (attended, highest + jnp.log(total))


def forward(values_row, segments, places, weights, again):
    attn_gain, head_gains, w_query, w_key, w_value, w_out, ffn_gain, w_gate, w_up, w_down = weights
    rows = values_row.shape[0]
    head = head_gains.shape[0] // 2
    heads = w_query.shape[1] // head
    kv_heads = w_key.shape[1] // head
    gains = head_gains.astype(jnp.float32)
    state = {}
    state["values"] = values_row.astype(jnp.float32)
    normed, state["x_unit"], state["x_factor"] = norm_forward(
        state["values"], attn_gain.astype(jnp.float32)
    )
    state["a_low"] = normed.astype(jnp.bfloat16)
    query = matmul(state["a_low"], w_query).reshape(rows, heads, head)
    keys = matmul(state["a_low"], w_key).reshape(rows, kv_heads, head)
    state["value_low"] = matmul(state["a_low"], w_value).astype(jnp.bfloat16)
    state["cosine"], state["sine"] = angles(places, head // 2)
    query_normed, state["q_unit"], state["q_factor"] = norm_forward(query, gains[:head])
    key_normed, state["k_unit"], state["k_factor"] = norm_forward(keys, gains[head:])
    state["query_low"] = rotate(query_normed, state["cosine"], state["sine"], 1.0).astype(
        jnp.bfloat16
    )
    state["key_low"] = (
        rotate(key_normed, state["cosine"], state["sine"], 1.0)
        .astype(jnp.bfloat16)
        .reshape(rows, kv_heads * head)
    )
    state["attended"], state["log_total"] = attention_forward(
        state["query_low"], state["key_low"], state["value_low"], segments, again
    )
    state["attended_low"] = state["attended"].astype(jnp.bfloat16).reshape(rows, heads * head)
    hidden = state["values"] + matmul(state["attended_low"], w_out)
    normed_two, state["h_unit"], state["h_factor"] = norm_forward(
        hidden, ffn_gain.astype(jnp.float32)
    )
    state["b_low"] = normed_two.astype(jnp.bfloat16)
    state["gate"] = matmul(state["b_low"], w_gate)
    state["upper"] = matmul(state["b_low"], w_up)
    state["act_low"] = (jax.nn.silu(state["gate"]) * state["upper"]).astype(jnp.bfloat16)
    state["output"] = hidden + matmul(state["act_low"], w_down)
    return state


def backward(grad_row, segments, weights, state):
    attn_gain, head_gains, w_query, w_key, w_value, w_out, ffn_gain, w_gate, w_up, w_down = weights
    query_low = state["query_low"]
    rows, heads, head = query_low.shape
    kv_heads = state["key_low"].shape[1] // head
    group = heads // kv_heads
    scale = head ** (-0.5)
    gains = head_gains.astype(jnp.float32)
    incoming = grad_row.astype(jnp.float32)
    down_low = incoming.astype(jnp.bfloat16)
    g_down = left_trans(state["act_low"], down_low)
    d_act = right_trans(down_low, w_down)
    sigma = jax.nn.sigmoid(state["gate"])
    d_upper = (d_act * state["gate"] * sigma).astype(jnp.bfloat16)
    d_gate = (d_act * state["upper"] * sigma * (1.0 + state["gate"] * (1.0 - sigma))).astype(
        jnp.bfloat16
    )
    g_gate = left_trans(state["b_low"], d_gate)
    g_up = left_trans(state["b_low"], d_upper)
    d_normed = right_trans(d_gate, w_gate) + right_trans(d_upper, w_up)
    d_hidden, terms = norm_backward(
        d_normed, state["h_unit"], state["h_factor"], ffn_gain.astype(jnp.float32)
    )
    g_ffn = jnp.sum(terms, 0)
    d_hidden = incoming + d_hidden
    branch_low = d_hidden.astype(jnp.bfloat16)
    g_out = left_trans(state["attended_low"], branch_low)
    d_attended = (
        right_trans(branch_low, w_out).astype(jnp.bfloat16).reshape(rows, kv_heads, group, head)
    )
    delta = jnp.sum(
        d_attended.astype(jnp.float32) * state["attended"].reshape(rows, kv_heads, group, head), -1
    )
    delta = jnp.transpose(delta, (1, 2, 0))
    log_total = state["log_total"]
    grouped = query_low.reshape(rows, kv_heads, group, head)
    query_index = lax.axis_index("ctx") * rows + jnp.arange(rows, dtype=jnp.int32)
    key_piece = lax.all_gather(state["key_low"], "ctx", axis=0, tiled=True)
    value_piece = lax.all_gather(state["value_low"], "ctx", axis=0, tiled=True)
    segment_piece = lax.all_gather(segments, "ctx", axis=0, tiled=True)
    width = key_piece.shape[0]
    key_heads = key_piece.reshape(width, kv_heads, head)
    value_heads = value_piece.reshape(width, kv_heads, head)
    scores = (
        jnp.einsum("qkgd,skd->kgqs", grouped, key_heads, preferred_element_type=jnp.float32) * scale
    )
    key_index = jnp.arange(width, dtype=jnp.int32)
    allowed = (segments[:, None] == segment_piece[None, :]) & (
        query_index[:, None] >= key_index[None, :]
    )
    probs = jnp.where(allowed, jnp.exp(scores - log_total[..., None]), 0.0)
    d_probs = jnp.einsum(
        "qkgd,skd->kgqs", d_attended, value_heads, preferred_element_type=jnp.float32
    )
    d_scores = (probs * (d_probs - delta[..., None])).astype(jnp.bfloat16)
    d_query = (
        jnp.einsum("kgqs,skd->qkgd", d_scores, key_heads, preferred_element_type=jnp.float32)
        * scale
    )
    key_part = (
        jnp.einsum("kgqs,qkgd->skd", d_scores, grouped, preferred_element_type=jnp.float32) * scale
    )
    value_part = jnp.einsum(
        "kgqs,qkgd->skd", probs.astype(jnp.bfloat16), d_attended, preferred_element_type=jnp.float32
    )
    d_keys = key_part.reshape(width, kv_heads * head)
    d_values = value_part.reshape(width, kv_heads * head)
    d_query, d_keys_all, d_values_all = (d_query, d_keys, d_values)
    d_keys, d_values = (
        lax.psum_scatter(
            d_keys_all.astype(jnp.bfloat16), "ctx", scatter_dimension=0, tiled=True
        ).astype(jnp.float32),
        lax.psum_scatter(
            d_values_all.astype(jnp.bfloat16), "ctx", scatter_dimension=0, tiled=True
        ).astype(jnp.float32),
    )
    d_query = rotate(d_query.reshape(rows, heads, head), state["cosine"], state["sine"], -1.0)
    d_query, query_terms = norm_backward(d_query, state["q_unit"], state["q_factor"], gains[:head])
    d_keys = rotate(d_keys.reshape(rows, kv_heads, head), state["cosine"], state["sine"], -1.0)
    d_keys, key_terms = norm_backward(d_keys, state["k_unit"], state["k_factor"], gains[head:])
    g_heads = jnp.concatenate([jnp.sum(query_terms, (0, 1)), jnp.sum(key_terms, (0, 1))])
    query_grad_low = d_query.astype(jnp.bfloat16).reshape(rows, heads * head)
    key_grad_low = d_keys.astype(jnp.bfloat16).reshape(rows, kv_heads * head)
    value_grad_low = d_values.astype(jnp.bfloat16)
    g_query = left_trans(state["a_low"], query_grad_low)
    g_key = left_trans(state["a_low"], key_grad_low)
    g_value = left_trans(state["a_low"], value_grad_low)
    d_inner = (
        right_trans(query_grad_low, w_query)
        + right_trans(key_grad_low, w_key)
        + right_trans(value_grad_low, w_value)
    )
    d_input, terms = norm_backward(
        d_inner, state["x_unit"], state["x_factor"], attn_gain.astype(jnp.float32)
    )
    g_attn = jnp.sum(terms, 0)
    in_grad = (d_hidden + d_input).astype(jnp.bfloat16)
    return (in_grad, (g_attn, g_heads, g_query, g_key, g_value, g_out, g_ffn, g_gate, g_up, g_down))


def on_device(
    hidden_in,
    out_grad,
    segment_ids,
    doc_positions,
    attn_gain,
    head_gains,
    w_query,
    w_key,
    w_value,
    w_out,
    ffn_gain,
    w_gate,
    w_up,
    w_down,
):
    shards = (attn_gain, head_gains, w_query, w_key, w_value, w_out, ffn_gain, w_gate, w_up, w_down)
    micro = hidden_in.shape[0]
    outputs = []
    for micro_index in range(micro):
        weights = fetch_weights(shards)
        state = forward(
            hidden_in[micro_index, 0],
            segment_ids[micro_index, 0],
            doc_positions[micro_index, 0],
            weights,
            False,
        )
        outputs.append(state["output"].astype(jnp.bfloat16))
    in_grads = []
    totals = None
    for micro_index in range(micro):
        weights = fetch_again(shards)
        state = forward(
            hidden_in[micro_index, 0],
            segment_ids[micro_index, 0],
            doc_positions[micro_index, 0],
            weights,
            True,
        )
        in_grad, grads = backward(
            out_grad[micro_index, 0], segment_ids[micro_index, 0], weights, state
        )
        in_grads.append(in_grad)
        if totals is None:
            totals = grads
        else:
            totals = tuple((left + right for left, right in zip(totals, grads)))
    totals = lax.psum_scatter(totals, ("dp", "ctx"), scatter_dimension=0, tiled=True)
    block_out = jnp.stack(outputs)[:, None]
    input_grads = jnp.stack(in_grads)[:, None]
    return (
        block_out,
        input_grads,
        totals[0],
        totals[1],
        totals[2],
        totals[3],
        totals[4],
        totals[5],
        totals[6],
        totals[7],
        totals[8],
        totals[9],
    )


CORE, SIDE, HIGH = 1, 2, 4


def flip(array, bits):
    count = lax.axis_size("dp")
    return lax.ppermute(array, "dp", [(i, i ^ bits) for i in range(count)])


def spin(array):
    count = lax.axis_size("ctx")
    return lax.ppermute(array, "ctx", [(i, (i + 1) % count) for i in range(count)])


def after(array, *others):
    return lax.optimization_barrier((array,) + others)[0]


def choose(bit, zero, one):
    return jnp.where(bit == 0, zero, one)


def pick(array, index, axis=0):
    return lax.dynamic_index_in_dim(array, index, axis, keepdims=False)


def put(buffer, array, *place):
    index = place + (0,) * (buffer.ndim - len(place))
    shape = (1,) * (buffer.ndim - array.ndim) + array.shape
    return lax.dynamic_update_slice(buffer, array.reshape(shape), index)


def joined(*arrays):
    buffer = jnp.zeros((len(arrays),) + arrays[0].shape, arrays[0].dtype)
    for at, array in enumerate(arrays):
        buffer = put(buffer, array, at)
    return buffer


def order(bit, own, other):
    buffer = jnp.zeros((2,) + own.shape, own.dtype)
    return put(put(buffer, own, bit), other, 1 - bit)


def swap_halves(bit, array, axis):
    low, high = jnp.split(array, 2, axis)
    return choose(bit, array, jnp.concatenate([high, low], axis))


def half_of(bit, array, axis):
    low, high = jnp.split(array, 2, axis)
    return choose(bit, low, high)


def exchange(array, target, index_of, turn):
    dp_count, ctx_count = lax.axis_size("dp"), lax.axis_size("ctx")
    pairs, stay = [], []
    for dp in range(dp_count):
        for z in range(ctx_count):
            to = target(dp, z, turn)
            if to == (dp, z):
                stay.append(dp * ctx_count + z)
            else:
                pairs.append((dp * ctx_count + z, to[0] * ctx_count + to[1]))
    piece = pick(array, index_of(turn))
    got = lax.ppermute(piece, ("dp", "ctx"), pairs)
    if stay:
        me = lax.axis_index("dp") * ctx_count + lax.axis_index("ctx")
        mine = functools.reduce(jnp.logical_or, [me == which for which in stay])
        got = jnp.where(mine, piece, got)
    return got


def spread(array):
    ctx = lax.axis_index("ctx")

    def target(dp, z, turn):
        return dp // 2 * 2 + z // 2, 2 * ((z + turn) % 2) + dp % 2

    got = [exchange(array, target, lambda turn: (ctx + turn) % 2, turn) for turn in range(2)]
    return order(ctx // 2, got[0], got[1])


def unspread(array):
    ctx = lax.axis_index("ctx")

    def target(dp, z, turn):
        return dp // 2 * 2 + z % 2, 2 * (dp % 2) + (z // 2 + turn) % 2

    got = [exchange(array, target, lambda turn: (ctx // 2 + turn) % 2, turn) for turn in range(2)]
    return order(ctx % 2, got[0], got[1])


def swap_gather(array, bit_value, bit):
    return order(bit_value, array, flip(array, bit))


def total_low(left, right):
    return (left.astype(jnp.float32) + right.astype(jnp.float32)).astype(jnp.bfloat16)


def team_gather(array, gate=None):
    side, core = flip(array, SIDE), flip(array, CORE)
    return joined(array, side, core, flip(side, CORE)).reshape((-1,) + array.shape[1:])


def team_reduce(array):
    got = flip(array[2:].astype(jnp.bfloat16), CORE).astype(jnp.float32)
    side = flip((array[1] + got[1]).astype(jnp.bfloat16), SIDE)
    return array[0] + got[0] + side.astype(jnp.float32)


def nt(left, right):
    return lax.dot_general(
        left, right, (((1,), (1,)), ((), ())), preferred_element_type=jnp.float32
    )


def set_bias(bias_ref, seg_row_ref, seg_col_ref, block):
    size = bias_ref.shape[0]
    for first in range(0, size, block):
        for key in range(0, first + block, block):
            allowed = seg_col_ref[key : key + block, :] == seg_row_ref[:, first : first + block]
            if key == first:
                keys = lax.broadcasted_iota(jnp.int32, (block, block), 0)
                queries = lax.broadcasted_iota(jnp.int32, (block, block), 1)
                allowed = jnp.logical_and(allowed, keys <= queries)
            bias_ref[key : key + block, first : first + block] = jnp.where(allowed, 0.0, -1e30)


def turned(values, gain, cosine, sine):
    half = values.shape[0] // 2
    factor = lax.rsqrt(jnp.mean(values * values, 0, keepdims=True) + EPS)
    normed = values * factor * gain
    first, second = normed[:half], normed[half:]
    return jnp.concatenate([first * cosine - second * sine, second * cosine + first * sine], 0)


def turned_back(incoming, values, gain, cosine, sine):
    half = values.shape[0] // 2
    first, second = incoming[:half], incoming[half:]
    incoming = jnp.concatenate(
        [first * cosine + second * sine, second * cosine - first * sine], 0
    )
    factor = lax.rsqrt(jnp.mean(values * values, 0, keepdims=True) + EPS)
    unit = values * factor
    terms = jnp.sum(incoming * unit, 1, keepdims=True)
    scaled = incoming * gain
    return factor * (scaled - unit * jnp.mean(scaled * unit, 0, keepdims=True)), terms


def forward_kernel(
    block, q_ref, kv_ref, cos_ref, sin_ref, gain_ref, row_ref, col_ref,
    o_ref, log_ref, qr_ref, kvr_ref, bias_ref
):
    head = kv_ref.shape[0] // 2
    size = kv_ref.shape[1]
    scale = head ** (-0.5)

    @pl.when(pl.program_id(0) == 0)
    def _():
        set_bias(bias_ref, row_ref, col_ref, block)

    cosine, sine = cos_ref[...], sin_ref[...]
    keys = turned(kv_ref[:head, :], gain_ref[1], cosine, sine)
    kvr_ref[:head, :] = keys
    keys = keys.T.astype(jnp.bfloat16)
    values = kv_ref[head:, :]
    kvr_ref[head:, :] = values
    values = values.astype(jnp.bfloat16)
    for which in range(q_ref.shape[0] // head):
        rows = slice(which * head, (which + 1) * head)
        query = turned(q_ref[rows, :], gain_ref[0], cosine, sine)
        qr_ref[rows, :] = query
        query = query.astype(jnp.bfloat16)
        for first in range(0, size, block):
            here = slice(first, first + block)
            total = jnp.zeros((1, block), jnp.float32)
            summed = jnp.zeros((head, block), jnp.float32)
            for key in range(0, first + block, block):
                there = slice(key, key + block)
                scores = jnp.dot(keys[there], query[:, here], preferred_element_type=jnp.float32)
                weight = jnp.exp(scores * scale + bias_ref[there, here])
                total += jnp.sum(weight, 0, keepdims=True)
                summed += jnp.dot(
                    values[:, there],
                    weight.astype(jnp.bfloat16),
                    preferred_element_type=jnp.float32,
                )
            o_ref[rows, here] = summed / total
            log_ref[0, which : which + 1, here] = jnp.log(total)


def backward_kernel(
    block, q_ref, kv_ref, qr_ref, kvr_ref, do_ref, o_ref, log_ref, cos_ref, sin_ref,
    gain_ref, row_ref, col_ref, dq_ref, dkv_ref, gains_ref, bias_ref, dkey_ref, dvalue_ref
):
    head = kv_ref.shape[0] // 2
    size = kv_ref.shape[1]
    scale = head ** (-0.5)

    @pl.when(pl.program_id(0) == 0)
    def _():
        set_bias(bias_ref, row_ref, col_ref, block)
        gains_ref[...] = jnp.zeros_like(gains_ref)

    cosine, sine = cos_ref[...], sin_ref[...]
    keys_t = kvr_ref[:head, :]
    keys = keys_t.T.astype(jnp.bfloat16)
    keys_t = keys_t.astype(jnp.bfloat16)
    values = kvr_ref[head:, :].T.astype(jnp.bfloat16)
    dkey_ref[...] = jnp.zeros_like(dkey_ref)
    dvalue_ref[...] = jnp.zeros_like(dvalue_ref)
    found = []
    for which in range(q_ref.shape[0] // head):
        rows = slice(which * head, (which + 1) * head)
        query = qr_ref[rows, :].astype(jnp.bfloat16)
        grad = do_ref[rows, :].astype(jnp.bfloat16)
        delta = jnp.sum(grad.astype(jnp.float32) * o_ref[rows, :], 0, keepdims=True)
        pieces = []
        for first in range(0, size, block):
            here = slice(first, first + block)
            dquery = jnp.zeros((head, block), jnp.float32)
            for key in range(0, first + block, block):
                there = slice(key, key + block)
                scores = jnp.dot(keys[there], query[:, here], preferred_element_type=jnp.float32)
                probs = jnp.exp(
                    scores * scale + (bias_ref[there, here] - log_ref[0, which : which + 1, here])
                )
                dprobs = jnp.dot(values[there], grad[:, here], preferred_element_type=jnp.float32)
                dscores = (probs * (dprobs - delta[:, here])).astype(jnp.bfloat16)
                dquery += jnp.dot(keys_t[:, there], dscores, preferred_element_type=jnp.float32)
                dkey_ref[:, there] += nt(query[:, here], dscores)
                dvalue_ref[:, there] += nt(grad[:, here], probs.astype(jnp.bfloat16))
            pieces.append(dquery * scale)
        dquery, terms = turned_back(
            jnp.concatenate(pieces, 1), q_ref[rows, :], gain_ref[0], cosine, sine
        )
        found.append(dquery)
        gains_ref[0] += terms
    dq_ref[...] = jnp.concatenate(found, 0).T
    dkey, terms = turned_back(dkey_ref[...] * scale, kv_ref[:head, :], gain_ref[1], cosine, sine)
    dkv_ref[...] = jnp.concatenate([dkey, dvalue_ref[...]], 0).T
    gains_ref[1] += terms


def whole_spec(*shape):
    return pl.BlockSpec(shape, lambda i: (0,) * len(shape))


def attend(raw, cosine, sine, gains, segments, kv_own, head, block):
    size = raw.shape[1]
    group = raw.shape[0] // head // kv_own - 2
    query = pl.BlockSpec((group * head, size), lambda i: (i, 0))
    kv_at = group * kv_own // 2
    return pl.pallas_call(
        functools.partial(forward_kernel, block),
        grid=(kv_own,),
        in_specs=[
            query,
            pl.BlockSpec((2 * head, size), lambda i: (kv_at + i, 0)),
            whole_spec(head // 2, size),
            whole_spec(head // 2, size),
            whole_spec(2, head, 1),
            whole_spec(1, size),
            whole_spec(size, 1),
        ],
        out_specs=[
            query,
            pl.BlockSpec((1, group, size), lambda i: (i, 0, 0)),
            query,
            pl.BlockSpec((2 * head, size), lambda i: (i, 0)),
        ],
        out_shape=[
            jax.ShapeDtypeStruct((kv_own * group * head, size), jnp.float32),
            jax.ShapeDtypeStruct((kv_own, group, size), jnp.float32),
            jax.ShapeDtypeStruct((kv_own * group * head, size), jnp.float32),
            jax.ShapeDtypeStruct((kv_own * 2 * head, size), jnp.float32),
        ],
        scratch_shapes=[pltpu.VMEM((size, size), jnp.float32)],
        compiler_params=pltpu.CompilerParams(vmem_limit_bytes=40 * 2**20),
        cost_estimate=pl.CostEstimate(
            flops=16 * kv_own * group * size * size * head,
            bytes_accessed=12 * raw.size,
            transcendentals=kv_own * group * size * size,
        ),
    )(raw, raw, cosine, sine, gains, segments[None, :], segments[:, None])


def attend_back(
    raw, turned_q, turned_kv, grad, attended, logs, cosine, sine, gains, segments,
    kv_own, head, block, begin, count
):
    size = raw.shape[1]
    group = raw.shape[0] // head // kv_own - 2
    query = pl.BlockSpec((group * head, size), lambda i: (begin + i, 0))
    kv_at = group * kv_own // 2 + begin
    return pl.pallas_call(
        functools.partial(backward_kernel, block),
        grid=(count,),
        in_specs=[
            query,
            pl.BlockSpec((2 * head, size), lambda i: (kv_at + i, 0)),
            query,
            pl.BlockSpec((2 * head, size), lambda i: (begin + i, 0)),
            query,
            query,
            pl.BlockSpec((1, group, size), lambda i: (begin + i, 0, 0)),
            whole_spec(head // 2, size),
            whole_spec(head // 2, size),
            whole_spec(2, head, 1),
            whole_spec(1, size),
            whole_spec(size, 1),
        ],
        out_specs=[
            pl.BlockSpec((size, group * head), lambda i: (0, i)),
            pl.BlockSpec((size, 2 * head), lambda i: (0, i)),
            whole_spec(2, head, 1),
        ],
        out_shape=[
            jax.ShapeDtypeStruct((size, count * group * head), jnp.float32),
            jax.ShapeDtypeStruct((size, count * 2 * head), jnp.float32),
            jax.ShapeDtypeStruct((2, head, 1), jnp.float32),
        ],
        scratch_shapes=[
            pltpu.VMEM((size, size), jnp.float32),
            pltpu.VMEM((head, size), jnp.float32),
            pltpu.VMEM((head, size), jnp.float32),
        ],
        compiler_params=pltpu.CompilerParams(vmem_limit_bytes=40 * 2**20),
        cost_estimate=pl.CostEstimate(
            flops=40 * count * group * size * size * head,
            bytes_accessed=4 * raw.size * count,
            transcendentals=count * group * size * size,
        ),
    )(
        raw, raw, turned_q, turned_kv, grad, attended, logs, cosine, sine, gains,
        segments[None, :], segments[:, None]
    )


def on_device_fast(
    hidden_in,
    out_grad,
    segment_ids,
    doc_positions,
    attn_gain,
    head_gains,
    w_query,
    w_key,
    w_value,
    w_out,
    ffn_gain,
    w_gate,
    w_up,
    w_down,
):
    low, full = jnp.bfloat16, jnp.float32
    dp, ctx = lax.axis_index("dp"), lax.axis_index("ctx")
    ctx_count = lax.axis_size("ctx")
    core, side, high = dp % 2, dp // 2 % 2, dp // 4
    width = hidden_in.shape[-1]
    rows = w_query.shape[0]
    head = head_gains.shape[0] * lax.axis_size("dp") * ctx_count // 2
    group = w_query.shape[1] // w_key.shape[1]
    kv_own = w_key.shape[1] // head // 2
    units = w_down.shape[0] * ctx_count

    x_half = spread(hidden_in[:, 0]).reshape(-1, width)
    marks = spread(jnp.stack([segment_ids[:, 0], doc_positions[:, 0]], 1))
    marks = swap_gather(marks, core, CORE).reshape(-1, 2, marks.shape[-1])
    segments, places = marks[:, 0].reshape(-1), marks[:, 1].reshape(-1)
    x_all = swap_gather(x_half, core, CORE).reshape(-1, width)

    def of_member(which):
        return jnp.concatenate(
            [
                w[:, (top * 4 + which) * units : (top * 4 + which + 1) * units]
                for w in (w_gate, w_up)
                for top in range(w_gate.shape[1] // units // 4)
            ],
            1,
        )

    def related(zero, one, two, three):
        near, far = choose(side, zero, two), choose(side, two, zero)
        near_far, far_far = choose(side, one, three), choose(side, three, one)
        return (
            choose(core, near, near_far),
            choose(core, far, far_far),
            choose(core, near_far, near),
            choose(core, far_far, far),
        )

    members = related(*[of_member(which) for which in range(4)])
    block_ffn = jnp.zeros((2, 2) + members[0].shape, low)
    block_ffn = put(block_ffn, members[0], side, core)
    block_ffn = put(block_ffn, flip(members[1], SIDE), 1 - side, core)
    block_ffn = put(block_ffn, flip(members[2], CORE), side, 1 - core)
    block_ffn = put(block_ffn, flip(members[3], SIDE | CORE), 1 - side, 1 - core)
    block_ffn = block_ffn.reshape(4, rows, -1)

    head_few = head_gains.shape[0]
    gains = jnp.stack([attn_gain, ffn_gain, jnp.pad(head_gains, (0, rows - head_few))])
    gains = jnp.pad(gains, ((0, rows - 3), (0, 128 - rows)))
    key_value = jnp.stack([w_key.reshape(rows, -1, 2, head), w_value.reshape(rows, -1, 2, head)], 3)
    parities = [
        jnp.concatenate(
            [
                w_query.reshape(rows, -1, 2, group * head)[:, :, which].reshape(rows, -1),
                key_value[:, :, which].reshape(rows, -1),
                gains,
            ],
            1,
        )
        for which in range(2)
    ]
    inner = parities[0].shape[1]
    got = flip(choose(core, parities[1], parities[0]), CORE)
    block = joined(
        choose(core, parities[0], got),
        choose(core, got, parities[1]),
        jnp.pad(w_out, ((0, 0), (0, inner - width))),
    )
    buffer = jnp.zeros((2, 2, 3, ctx_count, rows, inner), low)
    for step in range(ctx_count):
        following = spin(block) if step < ctx_count - 1 else None
        from_side, from_high = flip(block, SIDE), flip(block, HIGH)
        from_both = flip(from_side, HIGH) if step % 2 == 0 else flip(from_high, SIDE)
        place = (ctx - step) % ctx_count
        for up, across, piece in (
            (high, side, block),
            (high, 1 - side, from_side),
            (1 - high, side, from_high),
            (1 - high, 1 - side, from_both),
        ):
            buffer = put(buffer, piece[:, None], up, across, 0, place)
        last_attn = block
        block = following
    w_in = buffer[:, :, :2].reshape(-1, inner)
    w_mine = buffer[:, :, 2].reshape(-1, inner)[:, :width]
    w_theirs = flip(w_mine, CORE)

    features = inner - 128
    gains_all = w_in[:, features:].reshape(-1, rows, 128)[:, :3, :rows].astype(full)
    attn_gain_all, ffn_gain_all = gains_all[:, 0].reshape(-1), gains_all[:, 1].reshape(-1)
    head_gains_all = gains_all[:, 2, :head_few].reshape(2, head, 1)
    w_in = w_in[:, :features]

    ffn_blocks, ffn_far = [after(block_ffn, x_half, last_attn)], []

    def ffn_step(*ready):
        block = ffn_blocks[-1]
        if ready:
            block = after(block, *ready)
            ffn_blocks[-1] = block
        if len(ffn_blocks) < ctx_count:
            ffn_blocks.append(spin(block))
        ffn_far.append(flip(block, HIGH))

    x = x_all.astype(full)
    normed, _, _ = norm_forward(x, attn_gain_all)
    a_low = normed.astype(low)
    ffn_step()
    raw = lax.dot_general(w_in, a_low, (((0,), (1,)), ((), ())), preferred_element_type=full)
    ffn_step(a_low)
    freq = THETA ** (-(jnp.arange(head // 2, dtype=full) * 2.0 / head))
    turn = freq[:, None] * places.astype(full)[None, :]
    cosine, sine = jnp.cos(turn), jnp.sin(turn)
    attended, logs, turned_q, turned_kv = attend(
        raw, cosine, sine, head_gains_all, segments, kv_own, head, 256
    )
    ffn_step(attended)
    attended_low = attended.astype(low)
    o_theirs = flip(half_of(1 - core, attended_low, 1), CORE)
    hidden = (
        x_half.astype(full)
        + left_trans(half_of(core, attended_low, 1), w_mine)
        + left_trans(o_theirs, w_theirs)
    )
    normed_two, h_unit, h_factor = norm_forward(hidden, ffn_gain_all)
    b_own = swap_halves(high, normed_two.astype(low), 1)
    b_side, b_core = flip(b_own, SIDE), flip(b_own, CORE)
    ffn_step(b_own)
    w_ffn = jnp.zeros((2, 4, ctx_count) + block_ffn.shape[1:], low)
    for step in range(ctx_count):
        place = (ctx - step) % ctx_count
        w_ffn = put(w_ffn, ffn_blocks[step][:, None], 0, 0, place)
        w_ffn = put(w_ffn, ffn_far[step][:, None], 1, 0, place)
    w_ffn = w_ffn.reshape(width, -1)
    df = spread(after(out_grad[:, 0], b_own)).reshape(-1, width)
    down_blocks, down_far = [after(w_down, ffn_blocks[-1])], []

    def down_step(*ready):
        block = down_blocks[-1]
        if ready:
            block = after(block, *ready)
            down_blocks[-1] = block
        if len(down_blocks) < ctx_count:
            down_blocks.append(spin(block))
        down_far.append(flip(block, HIGH))

    down_step()
    b_both = flip(b_side, CORE)
    team_b = joined(b_own, b_side, b_core, b_both).reshape(-1, width)
    down_step(b_both)
    down_step(b_both)
    pre = matmul(team_b, w_ffn)
    down_step(pre)
    w_down_all = jnp.zeros((2, ctx_count) + w_down.shape, low)
    for step in range(ctx_count):
        place = (ctx - step) % ctx_count
        w_down_all = put(w_down_all, down_blocks[step], high, place)
        w_down_all = put(w_down_all, down_far[step], 1 - high, place)
    w_down_all = w_down_all.reshape(-1, width)
    team_df = team_gather(df)

    mid = pre.shape[1] // 2
    gate, upper = pre[:, :mid], pre[:, mid:]
    sigma = jax.nn.sigmoid(gate)
    act = (gate * sigma * upper).astype(low)
    d_act = right_trans(team_df, w_down_all)
    d_upper = (d_act * gate * sigma).astype(low)
    d_gate = (d_act * upper * sigma * (1.0 + gate * (1.0 - sigma))).astype(low)
    d_pre = jnp.concatenate([d_gate, d_upper], 1)
    partial_db = right_trans(d_pre, w_ffn)
    db = team_reduce(partial_db.reshape(4, -1, width))
    db = swap_halves(high, db, 1)

    def behind(step):
        return (ctx - 1 - step) % ctx_count

    g_ffn = left_trans(after(team_b, partial_db), d_pre).astype(low)
    g_ffn = g_ffn.reshape(2, 4, ctx_count, rows, -1)
    ffn_got = [flip(pick(g_ffn[1], behind(step), 1), HIGH) for step in range(ctx_count)]
    g_down = left_trans(after(act, g_ffn), team_df).astype(low)
    g_down = g_down.reshape(2, ctx_count, -1, width)
    g_down_near, g_down_far = pick(g_down, high), pick(g_down, 1 - high)
    down_got = [flip(pick(g_down_far, behind(step)), HIGH) for step in range(ctx_count)]
    partial_out = matmul(after(act, g_down), w_down_all)

    def ffn_term(step):
        return total_low(pick(g_ffn[0], behind(step), 1), ffn_got[step])

    def down_term(step):
        return total_low(pick(g_down_near, behind(step)), down_got[step])

    ffn_ring = spin(after(ffn_term(0), partial_out))
    down_ring = spin(after(down_term(0), partial_out))
    d_hidden, ffn_terms = norm_backward(db, h_unit, h_factor, ffn_gain_all)
    d_hidden = df.astype(full) + d_hidden
    dz = d_hidden.astype(low)
    dz_all = swap_gather(dz, core, CORE).reshape(-1, width)
    ffn_ring = spin(total_low(after(ffn_ring, dz), ffn_term(1)))
    down_ring = spin(total_low(after(down_ring, dz), down_term(1)))
    d_attended = right_trans(w_mine, dz_all)
    g_out = matmul(attended_low, dz_all).astype(low).reshape(2, 2, ctx_count, -1, width)
    back = functools.partial(
        attend_back, raw, turned_q, turned_kv, d_attended, attended, logs, cosine, sine,
        head_gains_all, segments, kv_own, head, 256
    )
    dq_one, dkv_one, g_heads_one = back(0, kv_own // 2)
    ffn_ring = spin(total_low(after(ffn_ring, dq_one), ffn_term(2)))
    down_ring = spin(total_low(after(down_ring, dq_one), down_term(2)))
    block_out = hidden + team_reduce(partial_out.reshape(4, -1, width))
    block_out = unspread(after(block_out, dq_one).astype(low).reshape(2, -1, width))

    def squares(array, step):
        part = pick(array, behind(step), 2)
        mine, other = pick(part, high), pick(part, 1 - high)
        if step % 2 == 0:
            got = flip(other, HIGH)
            mine_near, mine_far = pick(mine, side), pick(mine, 1 - side)
            got_near, got_far = pick(got, side), pick(got, 1 - side)
            from_side = flip(total_low(mine_far, got_far), SIDE)
            return total_low(total_low(mine_near, got_near), from_side)
        near, far = pick(part, side, 1), pick(part, 1 - side, 1)
        got = flip(far, SIDE)
        from_high = flip(total_low(pick(near, 1 - high), pick(got, 1 - high)), HIGH)
        return total_low(total_low(pick(near, high), pick(got, high)), from_high)

    out_terms = [squares(after(g_out, dq_one), step) for step in range(ctx_count)]
    out_ring = spin(out_terms[0])
    dq_two, dkv_two, g_heads_two = back(kv_own // 2, kv_own - kv_own // 2)
    d_raw = jnp.concatenate([dq_one, dq_two, dkv_one, dkv_two], 1).astype(low)
    g_heads = g_heads_one + g_heads_two
    g_in = left_trans(a_low, d_raw).astype(low)
    d_theirs = right_trans(half_of(1 - core, d_raw, 0), w_in)
    d_from = flip(d_theirs.astype(low), CORE)
    d_inner = right_trans(half_of(core, d_raw, 0), w_in) + d_from.astype(full)
    _, x_unit, x_factor = norm_forward(x_half.astype(full), attn_gain_all)
    d_input, attn_terms = norm_backward(d_inner, x_unit, x_factor, attn_gain_all)
    in_grad = unspread((d_hidden + d_input).astype(low).reshape(2, -1, width))
    out_ring = spin(total_low(after(out_ring, dq_two), out_terms[1]))
    ffn_total = total_low(after(ffn_ring, dq_two), ffn_term(3)).reshape(2, 2, rows, -1)
    g_down = total_low(after(down_ring, dq_two), down_term(3))

    own_heads = jnp.pad(g_heads.reshape(-1, head_few), ((0, 0), (0, rows - head_few)))
    g_gains = jnp.stack(
        [
            jnp.sum(attn_terms, 0).reshape(-1, rows),
            jnp.sum(ffn_terms, 0).reshape(-1, rows),
            own_heads,
        ],
        1,
    )
    g_gains = jnp.pad(g_gains, ((0, 0), (0, rows - 3), (0, 128 - rows))).reshape(-1, 128)
    g_in = jnp.concatenate([g_in, g_gains.astype(low)], 1)
    g_in = jnp.moveaxis(g_in.reshape(2, 2, 2, ctx_count, rows, inner), 3, 2)
    in_terms = [squares(g_in, step) for step in range(ctx_count)]
    in_ring = spin(in_terms[0])
    out_ring = spin(total_low(out_ring, out_terms[2]))
    in_ring = spin(total_low(in_ring, in_terms[1]))
    g_out = total_low(out_ring, out_terms[3])
    in_ring = spin(total_low(in_ring, in_terms[2]))

    ffn_total = after(ffn_total, in_terms[3])
    found = related(
        pick(pick(ffn_total, side), core),
        flip(pick(pick(ffn_total, side), 1 - core), CORE),
        flip(pick(pick(ffn_total, 1 - side), core), SIDE),
        flip(pick(pick(ffn_total, 1 - side), 1 - core), SIDE | CORE),
    )
    found = (found[0], found[2], found[1], found[3])
    blocks = w_gate.shape[1] // units // 4

    def to_columns(first):
        return jnp.concatenate(
            [
                found[which][:, (first + top) * units : (first + top + 1) * units].astype(full)
                for top in range(blocks)
                for which in range(4)
            ],
            1,
        )

    g_gate, g_up = to_columns(0), to_columns(blocks)

    g_in = total_low(in_ring, in_terms[3])
    own = pick(g_in, core).astype(full)
    got = flip(pick(g_in, 1 - core), CORE).astype(full)
    even, odd = choose(core, own, got), choose(core, got, own)
    first = group * head * kv_own

    def mixed(start, stop, step, size):
        return jnp.concatenate(
            [part[:, at : at + size] for at in range(start, stop, step) for part in (even, odd)], 1
        )

    g_gains = (own + got)[:, features:]

    return (
        block_out[:, None],
        in_grad[:, None],
        g_gains[0, :rows],
        g_gains[2, :head_few],
        mixed(0, first, group * head, group * head),
        mixed(first, features, 2 * head, head),
        mixed(first + head, features, 2 * head, head),
        g_out.astype(full),
        g_gains[1, :rows],
        g_gate,
        g_up,
        g_down.astype(full),
    )


def solution(mesh):
    placed = (
        P(None, "dp", "ctx", None),
        P(None, "dp", "ctx", None),
        P(None, "dp", "ctx"),
        P(None, "dp", "ctx"),
        P(("dp", "ctx")),
        P(("dp", "ctx")),
        P(("dp", "ctx"), None),
        P(("dp", "ctx"), None),
        P(("dp", "ctx"), None),
        P(("dp", "ctx"), None),
        P(("dp", "ctx")),
        P(("dp", "ctx"), None),
        P(("dp", "ctx"), None),
        P(("dp", "ctx"), None),
    )
    fits = mesh.shape["dp"] == 8 and mesh.shape["ctx"] == 4
    return jax.shard_map(
        on_device_fast if fits else on_device,
        mesh=mesh,
        in_specs=placed,
        out_specs=(
            P(None, "dp", "ctx", None),
            P(None, "dp", "ctx", None),
            P(("dp", "ctx")),
            P(("dp", "ctx")),
            P(("dp", "ctx"), None),
            P(("dp", "ctx"), None),
            P(("dp", "ctx"), None),
            P(("dp", "ctx"), None),
            P(("dp", "ctx")),
            P(("dp", "ctx"), None),
            P(("dp", "ctx"), None),
            P(("dp", "ctx"), None),
        ),
        check_vma=False,
    )
```

```python
import functools

import jax
import jax.numpy as jnp
from jax import lax
from jax.experimental import pallas as pl
from jax.experimental.pallas import tpu as pltpu
from jax.sharding import PartitionSpec as P

EPS = 1e-05
THETA = 1000000.0


def matmul(left, right):
    return jnp.dot(left, right, preferred_element_type=jnp.float32)


def left_trans(left, right):
    return lax.dot_general(
        left, right, (((0,), (0,)), ((), ())), preferred_element_type=jnp.float32
    )


def right_trans(left, right):
    return lax.dot_general(
        left, right, (((1,), (1,)), ((), ())), preferred_element_type=jnp.float32
    )


def norm_forward(values, gain):
    factor = lax.rsqrt(jnp.mean(values * values, -1, keepdims=True) + EPS)
    unit = values * factor
    return (unit * gain, unit, factor)


def norm_backward(incoming, unit, factor, gain):
    scaled = incoming * gain
    result = factor * (scaled - unit * jnp.mean(scaled * unit, -1, keepdims=True))
    return (result, incoming * unit)


def angles(places, half):
    freq = THETA ** (-(jnp.arange(half, dtype=jnp.float32) * 2.0 / (2 * half)))
    turn = places.astype(jnp.float32)[:, None] * freq[None, :]
    return (jnp.cos(turn)[:, None, :], jnp.sin(turn)[:, None, :])


def rotate(values, cosine, sine, sign):
    half = values.shape[-1] // 2
    first = values[..., :half]
    second = values[..., half:]
    return jnp.concatenate(
        [first * cosine - sign * second * sine, second * cosine + sign * first * sine], -1
    )


def fetch_weights(shards):
    return (
        lax.all_gather(shards[0], ("dp", "ctx"), axis=0, tiled=True),
        lax.all_gather(shards[1], ("dp", "ctx"), axis=0, tiled=True),
        lax.all_gather(shards[2], ("dp", "ctx"), axis=0, tiled=True),
        lax.all_gather(shards[3], ("dp", "ctx"), axis=0, tiled=True),
        lax.all_gather(shards[4], ("dp", "ctx"), axis=0, tiled=True),
        lax.all_gather(shards[5], ("dp", "ctx"), axis=0, tiled=True),
        lax.all_gather(shards[6], ("dp", "ctx"), axis=0, tiled=True),
        lax.all_gather(shards[7], ("dp", "ctx"), axis=0, tiled=True),
        lax.all_gather(shards[8], ("dp", "ctx"), axis=0, tiled=True),
        lax.all_gather(shards[9], ("dp", "ctx"), axis=0, tiled=True),
    )


def fetch_again(shards):
    return (
        lax.all_gather(shards[0], ("dp", "ctx"), axis=0, tiled=True),
        lax.all_gather(shards[1], ("dp", "ctx"), axis=0, tiled=True),
        lax.all_gather(shards[2], ("dp", "ctx"), axis=0, tiled=True),
        lax.all_gather(shards[3], ("dp", "ctx"), axis=0, tiled=True),
        lax.all_gather(shards[4], ("dp", "ctx"), axis=0, tiled=True),
        lax.all_gather(shards[5], ("dp", "ctx"), axis=0, tiled=True),
        lax.all_gather(shards[6], ("dp", "ctx"), axis=0, tiled=True),
        lax.all_gather(shards[7], ("dp", "ctx"), axis=0, tiled=True),
        lax.all_gather(shards[8], ("dp", "ctx"), axis=0, tiled=True),
        lax.all_gather(shards[9], ("dp", "ctx"), axis=0, tiled=True),
    )


def attention_forward(query_low, key_low, value_low, segments, again):
    rows, heads, head = query_low.shape
    kv_heads = key_low.shape[1] // head
    group = heads // kv_heads
    scale = head ** (-0.5)
    grouped = query_low.reshape(rows, kv_heads, group, head)
    query_index = lax.axis_index("ctx") * rows + jnp.arange(rows, dtype=jnp.int32)

    def visit(carry, piece):
        highest, total, summed = carry
        key_piece, value_piece, segment_piece = piece
        width = key_piece.shape[0]
        key_heads = key_piece.reshape(width, kv_heads, head)
        value_heads = value_piece.reshape(width, kv_heads, head)
        scores = (
            jnp.einsum("qkgd,skd->kgqs", grouped, key_heads, preferred_element_type=jnp.float32)
            * scale
        )
        key_index = jnp.arange(width, dtype=jnp.int32)
        allowed = (segments[:, None] == segment_piece[None, :]) & (
            query_index[:, None] >= key_index[None, :]
        )
        scores = jnp.where(allowed, scores, -1e30)
        peak = jnp.maximum(highest, jnp.max(scores, -1))
        weight = jnp.where(allowed, jnp.exp(scores - peak[..., None]), 0.0)
        total = jnp.sum(weight, -1)
        summed = jnp.einsum(
            "kgqs,skd->qkgd",
            weight.astype(jnp.bfloat16),
            value_heads,
            preferred_element_type=jnp.float32,
        )
        return (peak, total, summed)

    initial = (
        jnp.full((kv_heads, group, rows), -1e30, jnp.float32),
        jnp.zeros((kv_heads, group, rows), jnp.float32),
        jnp.zeros((rows, kv_heads, group, head), jnp.float32),
    )
    if again:
        highest, total, summed = visit(
            initial,
            (
                lax.all_gather(key_low, "ctx", axis=0, tiled=True),
                lax.all_gather(value_low, "ctx", axis=0, tiled=True),
                lax.all_gather(segments, "ctx", axis=0, tiled=True),
            ),
        )
    else:
        highest, total, summed = visit(
            initial,
            (
                lax.all_gather(key_low, "ctx", axis=0, tiled=True),
                lax.all_gather(value_low, "ctx", axis=0, tiled=True),
                lax.all_gather(segments, "ctx", axis=0, tiled=True),
            ),
        )
    attended = (summed / jnp.transpose(total, (2, 0, 1))[..., None]).reshape(rows, heads, head)
    return (attended, highest + jnp.log(total))


def forward(values_row, segments, places, weights, again):
    attn_gain, head_gains, w_query, w_key, w_value, w_out, ffn_gain, w_gate, w_up, w_down = weights
    rows = values_row.shape[0]
    head = head_gains.shape[0] // 2
    heads = w_query.shape[1] // head
    kv_heads = w_key.shape[1] // head
    gains = head_gains.astype(jnp.float32)
    state = {}
    state["values"] = values_row.astype(jnp.float32)
    normed, state["x_unit"], state["x_factor"] = norm_forward(
        state["values"], attn_gain.astype(jnp.float32)
    )
    state["a_low"] = normed.astype(jnp.bfloat16)
    query = matmul(state["a_low"], w_query).reshape(rows, heads, head)
    keys = matmul(state["a_low"], w_key).reshape(rows, kv_heads, head)
    state["value_low"] = matmul(state["a_low"], w_value).astype(jnp.bfloat16)
    state["cosine"], state["sine"] = angles(places, head // 2)
    query_normed, state["q_unit"], state["q_factor"] = norm_forward(query, gains[:head])
    key_normed, state["k_unit"], state["k_factor"] = norm_forward(keys, gains[head:])
    state["query_low"] = rotate(query_normed, state["cosine"], state["sine"], 1.0).astype(
        jnp.bfloat16
    )
    state["key_low"] = (
        rotate(key_normed, state["cosine"], state["sine"], 1.0)
        .astype(jnp.bfloat16)
        .reshape(rows, kv_heads * head)
    )
    state["attended"], state["log_total"] = attention_forward(
        state["query_low"], state["key_low"], state["value_low"], segments, again
    )
    state["attended_low"] = state["attended"].astype(jnp.bfloat16).reshape(rows, heads * head)
    hidden = state["values"] + matmul(state["attended_low"], w_out)
    normed_two, state["h_unit"], state["h_factor"] = norm_forward(
        hidden, ffn_gain.astype(jnp.float32)
    )
    state["b_low"] = normed_two.astype(jnp.bfloat16)
    state["gate"] = matmul(state["b_low"], w_gate)
    state["upper"] = matmul(state["b_low"], w_up)
    state["act_low"] = (jax.nn.silu(state["gate"]) * state["upper"]).astype(jnp.bfloat16)
    state["output"] = hidden + matmul(state["act_low"], w_down)
    return state


def backward(grad_row, segments, weights, state):
    attn_gain, head_gains, w_query, w_key, w_value, w_out, ffn_gain, w_gate, w_up, w_down = weights
    query_low = state["query_low"]
    rows, heads, head = query_low.shape
    kv_heads = state["key_low"].shape[1] // head
    group = heads // kv_heads
    scale = head ** (-0.5)
    gains = head_gains.astype(jnp.float32)
    incoming = grad_row.astype(jnp.float32)
    down_low = incoming.astype(jnp.bfloat16)
    g_down = left_trans(state["act_low"], down_low)
    d_act = right_trans(down_low, w_down)
    sigma = jax.nn.sigmoid(state["gate"])
    d_upper = (d_act * state["gate"] * sigma).astype(jnp.bfloat16)
    d_gate = (d_act * state["upper"] * sigma * (1.0 + state["gate"] * (1.0 - sigma))).astype(
        jnp.bfloat16
    )
    g_gate = left_trans(state["b_low"], d_gate)
    g_up = left_trans(state["b_low"], d_upper)
    d_normed = right_trans(d_gate, w_gate) + right_trans(d_upper, w_up)
    d_hidden, terms = norm_backward(
        d_normed, state["h_unit"], state["h_factor"], ffn_gain.astype(jnp.float32)
    )
    g_ffn = jnp.sum(terms, 0)
    d_hidden = incoming + d_hidden
    branch_low = d_hidden.astype(jnp.bfloat16)
    g_out = left_trans(state["attended_low"], branch_low)
    d_attended = (
        right_trans(branch_low, w_out).astype(jnp.bfloat16).reshape(rows, kv_heads, group, head)
    )
    delta = jnp.sum(
        d_attended.astype(jnp.float32) * state["attended"].reshape(rows, kv_heads, group, head), -1
    )
    delta = jnp.transpose(delta, (1, 2, 0))
    log_total = state["log_total"]
    grouped = query_low.reshape(rows, kv_heads, group, head)
    query_index = lax.axis_index("ctx") * rows + jnp.arange(rows, dtype=jnp.int32)
    key_piece = lax.all_gather(state["key_low"], "ctx", axis=0, tiled=True)
    value_piece = lax.all_gather(state["value_low"], "ctx", axis=0, tiled=True)
    segment_piece = lax.all_gather(segments, "ctx", axis=0, tiled=True)
    width = key_piece.shape[0]
    key_heads = key_piece.reshape(width, kv_heads, head)
    value_heads = value_piece.reshape(width, kv_heads, head)
    scores = (
        jnp.einsum("qkgd,skd->kgqs", grouped, key_heads, preferred_element_type=jnp.float32) * scale
    )
    key_index = jnp.arange(width, dtype=jnp.int32)
    allowed = (segments[:, None] == segment_piece[None, :]) & (
        query_index[:, None] >= key_index[None, :]
    )
    probs = jnp.where(allowed, jnp.exp(scores - log_total[..., None]), 0.0)
    d_probs = jnp.einsum(
        "qkgd,skd->kgqs", d_attended, value_heads, preferred_element_type=jnp.float32
    )
    d_scores = (probs * (d_probs - delta[..., None])).astype(jnp.bfloat16)
    d_query = (
        jnp.einsum("kgqs,skd->qkgd", d_scores, key_heads, preferred_element_type=jnp.float32)
        * scale
    )
    key_part = (
        jnp.einsum("kgqs,qkgd->skd", d_scores, grouped, preferred_element_type=jnp.float32) * scale
    )
    value_part = jnp.einsum(
        "kgqs,qkgd->skd", probs.astype(jnp.bfloat16), d_attended, preferred_element_type=jnp.float32
    )
    d_keys = key_part.reshape(width, kv_heads * head)
    d_values = value_part.reshape(width, kv_heads * head)
    d_query, d_keys_all, d_values_all = (d_query, d_keys, d_values)
    d_keys, d_values = (
        lax.psum_scatter(
            d_keys_all.astype(jnp.bfloat16), "ctx", scatter_dimension=0, tiled=True
        ).astype(jnp.float32),
        lax.psum_scatter(
            d_values_all.astype(jnp.bfloat16), "ctx", scatter_dimension=0, tiled=True
        ).astype(jnp.float32),
    )
    d_query = rotate(d_query.reshape(rows, heads, head), state["cosine"], state["sine"], -1.0)
    d_query, query_terms = norm_backward(d_query, state["q_unit"], state["q_factor"], gains[:head])
    d_keys = rotate(d_keys.reshape(rows, kv_heads, head), state["cosine"], state["sine"], -1.0)
    d_keys, key_terms = norm_backward(d_keys, state["k_unit"], state["k_factor"], gains[head:])
    g_heads = jnp.concatenate([jnp.sum(query_terms, (0, 1)), jnp.sum(key_terms, (0, 1))])
    query_grad_low = d_query.astype(jnp.bfloat16).reshape(rows, heads * head)
    key_grad_low = d_keys.astype(jnp.bfloat16).reshape(rows, kv_heads * head)
    value_grad_low = d_values.astype(jnp.bfloat16)
    g_query = left_trans(state["a_low"], query_grad_low)
    g_key = left_trans(state["a_low"], key_grad_low)
    g_value = left_trans(state["a_low"], value_grad_low)
    d_inner = (
        right_trans(query_grad_low, w_query)
        + right_trans(key_grad_low, w_key)
        + right_trans(value_grad_low, w_value)
    )
    d_input, terms = norm_backward(
        d_inner, state["x_unit"], state["x_factor"], attn_gain.astype(jnp.float32)
    )
    g_attn = jnp.sum(terms, 0)
    in_grad = (d_hidden + d_input).astype(jnp.bfloat16)
    return (in_grad, (g_attn, g_heads, g_query, g_key, g_value, g_out, g_ffn, g_gate, g_up, g_down))


def on_device(
    hidden_in,
    out_grad,
    segment_ids,
    doc_positions,
    attn_gain,
    head_gains,
    w_query,
    w_key,
    w_value,
    w_out,
    ffn_gain,
    w_gate,
    w_up,
    w_down,
):
    shards = (attn_gain, head_gains, w_query, w_key, w_value, w_out, ffn_gain, w_gate, w_up, w_down)
    micro = hidden_in.shape[0]
    outputs = []
    for micro_index in range(micro):
        weights = fetch_weights(shards)
        state = forward(
            hidden_in[micro_index, 0],
            segment_ids[micro_index, 0],
            doc_positions[micro_index, 0],
            weights,
            False,
        )
        outputs.append(state["output"].astype(jnp.bfloat16))
    in_grads = []
    totals = None
    for micro_index in range(micro):
        weights = fetch_again(shards)
        state = forward(
            hidden_in[micro_index, 0],
            segment_ids[micro_index, 0],
            doc_positions[micro_index, 0],
            weights,
            True,
        )
        in_grad, grads = backward(
            out_grad[micro_index, 0], segment_ids[micro_index, 0], weights, state
        )
        in_grads.append(in_grad)
        if totals is None:
            totals = grads
        else:
            totals = tuple((left + right for left, right in zip(totals, grads)))
    totals = lax.psum_scatter(totals, ("dp", "ctx"), scatter_dimension=0, tiled=True)
    block_out = jnp.stack(outputs)[:, None]
    input_grads = jnp.stack(in_grads)[:, None]
    return (
        block_out,
        input_grads,
        totals[0],
        totals[1],
        totals[2],
        totals[3],
        totals[4],
        totals[5],
        totals[6],
        totals[7],
        totals[8],
        totals[9],
    )


CORE, SIDE, HIGH = 1, 2, 4


def flip(array, bits):
    count = lax.axis_size("dp")
    return lax.ppermute(array, "dp", [(i, i ^ bits) for i in range(count)])


def spin(array):
    count = lax.axis_size("ctx")
    return lax.ppermute(array, "ctx", [(i, (i + 1) % count) for i in range(count)])


def hold(*arrays):
    return lax.optimization_barrier(arrays)


def choose(bit, zero, one):
    return jnp.where(bit == 0, zero, one)


def pick(array, index, axis=0):
    return lax.dynamic_index_in_dim(array, index, axis, keepdims=False)


def put(buffer, array, *place):
    index = place + (0,) * (buffer.ndim - len(place))
    shape = (1,) * (buffer.ndim - array.ndim) + array.shape
    return lax.dynamic_update_slice(buffer, array.reshape(shape), index)


def place_kernel(splits, count, slots_ref, *refs):
    pieces, outs = refs[:count], refs[count:]
    at = 0
    for piece in pieces:
        for part in range(len(splits)):
            outs[splits[part]][slots_ref[at]] = piece[part]
            at += 1


def placed(pieces, splits, slots, counts):
    shape = pieces[0].shape
    return pl.pallas_call(
        functools.partial(place_kernel, splits, len(pieces)),
        in_specs=[pl.BlockSpec(memory_space=pltpu.SMEM)]
        + [pl.BlockSpec(memory_space=pltpu.VMEM)] * len(pieces),
        out_specs=[pl.BlockSpec(memory_space=pltpu.VMEM)] * len(counts),
        out_shape=[
            jax.ShapeDtypeStruct((count,) + shape[1:], pieces[0].dtype) for count in counts
        ],
        compiler_params=pltpu.CompilerParams(vmem_limit_bytes=40 * 2**20),
    )(jnp.stack(slots).astype(jnp.int32), *pieces)


def block_kernel(slots_ref, own_ref, core_ref, side_ref, down_ref, out_ref):
    rows = own_ref.shape[1]
    for member, ref, first in ((0, own_ref, 0), (1, core_ref, 1), (2, side_ref, 0), (3, side_ref, 2)):
        for part in range(2):
            start = pl.multiple_of((part * 4 + slots_ref[member]) * rows, rows)
            out_ref[pl.ds(start, rows), :] = ref[first + part]
    out_ref[8 * rows :, : down_ref.shape[1]] = down_ref[...]
    out_ref[8 * rows :, down_ref.shape[1] :] = jnp.zeros_like(
        out_ref[8 * rows :, down_ref.shape[1] :]
    )


def unit_block(slots, own, from_core, from_side, down):
    rows, columns = own.shape[1:]
    shape = (8 * rows + down.shape[0], columns)
    return pl.pallas_call(
        block_kernel,
        in_specs=[pl.BlockSpec(memory_space=pltpu.SMEM)]
        + [pl.BlockSpec(memory_space=pltpu.VMEM)] * 4,
        out_specs=pl.BlockSpec(memory_space=pltpu.VMEM),
        out_shape=jax.ShapeDtypeStruct(shape, own.dtype),
    )(jnp.stack(slots).astype(jnp.int32), own, from_core, from_side, down)


def unit_kernel(chunk, ctx_count, tiles, rows, slots_ref, *refs):
    pieces, refs = refs[: 2 * ctx_count], refs[2 * ctx_count :]
    b_refs, df_refs = refs[:2], refs[2:4]
    act_ref, pre_ref, all_b_ref, all_df_ref = refs[-12:-8]
    db_refs, out_refs, (w_ref, down_ref, b_ref, df_ref) = refs[-8:-6], refs[-6:-4], refs[-4:]
    mid = pieces[0].shape[1]
    width = down_ref.shape[1]
    down_rows = pieces[0].shape[0] - 8 * rows
    tile = pl.program_id(0)

    @pl.when(tile == 0)
    def _():
        high = slots_ref[ctx_count]
        for step in range(ctx_count):
            place = slots_ref[step]
            for far in range(2):
                piece = pieces[2 * step + far]
                for member in range(4):
                    first = ((far * 4 + member) * ctx_count + place) * rows
                    to = pl.ds(pl.multiple_of(first, rows), rows)
                    w_ref[to, :mid] = piece[member * rows : (member + 1) * rows, :]
                    w_ref[to, mid:] = piece[(4 + member) * rows : (5 + member) * rows, :]
                half = high if far == 0 else 1 - high
                first = (half * ctx_count + place) * down_rows
                to = pl.ds(pl.multiple_of(first, 16), down_rows)
                down_ref[to, :] = piece[8 * rows :, :width]

    for which in range(2):

        @pl.when(tile // tiles == which)
        def _(which=which):
            b_ref[...] = b_refs[which][...]
            df_ref[...] = df_refs[which][...]

    b, df = b_ref[...], df_ref[...]
    all_b_ref[...] = b
    all_df_ref[...] = df
    db, out = 0.0, 0.0
    for first in range(0, mid, chunk):
        here, there = slice(first, first + chunk), slice(mid + first, mid + first + chunk)
        gate = jnp.dot(b, w_ref[:, here], preferred_element_type=jnp.float32)
        upper = jnp.dot(b, w_ref[:, there], preferred_element_type=jnp.float32)
        d_act = nt(df, down_ref[here, :])
        sigma = 1.0 / (1.0 + jnp.exp(-gate))
        silu = gate * sigma
        act = (silu * upper).astype(jnp.bfloat16)
        d_upper = (d_act * silu).astype(jnp.bfloat16)
        d_gate = (d_act * upper * sigma * (1.0 + gate * (1.0 - sigma))).astype(jnp.bfloat16)
        act_ref[:, here] = act
        pre_ref[:, here] = d_gate
        pre_ref[:, there] = d_upper
        db += nt(d_gate, w_ref[:, here]) + nt(d_upper, w_ref[:, there])
        out += jnp.dot(act, down_ref[here, :], preferred_element_type=jnp.float32)
    for which in range(2):

        @pl.when(tile // tiles == which)
        def _(which=which):
            db_refs[which][...] = db.astype(jnp.bfloat16)
            out_refs[which][...] = out.astype(jnp.bfloat16)


def feed_forward(slots, pieces, rows, b_parts, df_parts, size, begin, left):
    tokens, width = b_parts[0].shape
    mid = pieces[0].shape[1]
    down_rows = pieces[0].shape[0] - 8 * rows
    tiles = tokens // size
    once = lambda array: pl.BlockSpec(
        array.shape, lambda t: (0,) * array.ndim, pipeline_mode=pl.Buffered(1)
    )

    def part(which):
        return pl.BlockSpec((size, width), lambda t: (jnp.clip(t - which * tiles, 0, tiles - 1), 0))

    def tiled(count, first):
        return pl.BlockSpec((size, count), lambda t: (first + t, 0))

    first = begin * tiles
    first_left = 1 + len(pieces) + 4
    full = lambda count: jax.ShapeDtypeStruct((4 * tokens, count), jnp.bfloat16)
    half = jax.ShapeDtypeStruct((tokens, width), jnp.bfloat16)
    return pl.pallas_call(
        functools.partial(unit_kernel, mid // 3, len(pieces) // 2, tiles, rows),
        grid=(2 * tiles,),
        in_specs=[pl.BlockSpec(memory_space=pltpu.SMEM)]
        + [once(array) for array in pieces]
        + [part(which) for which in range(2)] * 2
        + [pl.BlockSpec(memory_space=pl.ANY)] * len(left),
        out_specs=[tiled(mid, first), tiled(2 * mid, first), tiled(width, first), tiled(width, first)]
        + [part(which) for which in range(2)] * 2,
        out_shape=[full(mid), full(2 * mid), full(width), full(width)] + [half] * 4,
        input_output_aliases={first_left + at: at for at in range(len(left))},
        scratch_shapes=[
            pltpu.VMEM((width, 2 * mid), jnp.bfloat16),
            pltpu.VMEM((len(pieces) * down_rows, width), jnp.bfloat16),
            pltpu.VMEM((size, width), jnp.bfloat16),
            pltpu.VMEM((size, width), jnp.bfloat16),
        ],
        compiler_params=pltpu.CompilerParams(vmem_limit_bytes=52 * 2**20),
        cost_estimate=pl.CostEstimate(flops=10 * tokens * mid * width, bytes_accessed=0, transcendentals=0),
    )(jnp.stack(slots).astype(jnp.int32), *pieces, *b_parts, *df_parts, *left)


def spread_kernel(ctx_count, rows, slots_ref, ffn_ref, down_ref, *outs):
    mid = ffn_ref.shape[1] // 2
    width = down_ref.shape[1]
    down_rows = down_ref.shape[0] // (2 * ctx_count)
    high = slots_ref[ctx_count]
    for far in range(2):
        half = high if far == 0 else 1 - high
        for step in range(ctx_count):
            place = slots_ref[step]
            out = outs[far * ctx_count + step]
            for member in range(4):
                first = ((far * 4 + member) * ctx_count + place) * rows
                here = pl.ds(pl.multiple_of(first, rows), rows)
                out[member * rows : (member + 1) * rows, :] = ffn_ref[here, :mid]
                out[(4 + member) * rows : (5 + member) * rows, :] = ffn_ref[here, mid:]
            first = (half * ctx_count + place) * down_rows
            here = pl.ds(pl.multiple_of(first, 16), down_rows)
            out[8 * rows :, :width] = down_ref[here, :]
            out[8 * rows :, width:] = jnp.zeros_like(out[8 * rows :, width:])


def spread_units(slots, ffn, down, rows, ctx_count):
    shape = (8 * rows + down.shape[0] // (2 * ctx_count), ffn.shape[1] // 2)
    return pl.pallas_call(
        functools.partial(spread_kernel, ctx_count, rows),
        in_specs=[pl.BlockSpec(memory_space=pltpu.SMEM)]
        + [pl.BlockSpec(memory_space=pltpu.VMEM)] * 2,
        out_specs=[pl.BlockSpec(memory_space=pltpu.VMEM)] * (2 * ctx_count),
        out_shape=[jax.ShapeDtypeStruct(shape, ffn.dtype)] * (2 * ctx_count),
        compiler_params=pltpu.CompilerParams(vmem_limit_bytes=40 * 2**20),
        cost_estimate=pl.CostEstimate(flops=3 * 10**9, bytes_accessed=0, transcendentals=0),
    )(jnp.stack(slots).astype(jnp.int32), ffn, down)


def joined(*arrays):
    buffer = jnp.zeros((len(arrays),) + arrays[0].shape, arrays[0].dtype)
    for at, array in enumerate(arrays):
        buffer = put(buffer, array, at)
    return buffer


def order(bit, own, other):
    buffer = jnp.zeros((2,) + own.shape, own.dtype)
    return put(put(buffer, own, bit), other, 1 - bit)


def swap_halves(bit, array, axis):
    low, high = jnp.split(array, 2, axis)
    return choose(bit, array, jnp.concatenate([high, low], axis))


def half_of(bit, array, axis):
    low, high = jnp.split(array, 2, axis)
    return choose(bit, low, high)


def exchange(array, target, index_of):
    dp_count, ctx_count = lax.axis_size("dp"), lax.axis_size("ctx")
    me = lax.axis_index("dp") * ctx_count + lax.axis_index("ctx")
    came, kept = [], []
    for turn in range(2):
        pairs, stay = [], []
        for dp in range(dp_count):
            for z in range(ctx_count):
                to = target(dp, z, turn)
                if to == (dp, z):
                    stay.append(dp * ctx_count + z)
                else:
                    pairs.append((dp * ctx_count + z, to[0] * ctx_count + to[1]))
        piece = pick(array, index_of(turn))
        came.append(lax.ppermute(piece, ("dp", "ctx"), pairs))
        mine = functools.reduce(jnp.logical_or, [me == which for which in stay]) if stay else None
        kept.append((piece, mine))
    return came, kept


def settled(came, kept):
    return [
        got if mine is None else jnp.where(mine, piece, got)
        for got, (piece, mine) in zip(came, kept)
    ]


def spread(array):
    ctx = lax.axis_index("ctx")

    def target(dp, z, turn):
        return dp // 2 * 2 + z // 2, 2 * ((z + turn) % 2) + dp % 2

    return exchange(array, target, lambda turn: (ctx + turn) % 2)


def unspread(array):
    ctx = lax.axis_index("ctx")

    def target(dp, z, turn):
        return dp // 2 * 2 + z % 2, 2 * (dp % 2) + (z // 2 + turn) % 2

    return exchange(array, target, lambda turn: (ctx // 2 + turn) % 2)


def swap_gather(array, bit_value, bit):
    return order(bit_value, array, flip(array, bit))


def total_low(left, right):
    return (left.astype(jnp.float32) + right.astype(jnp.float32)).astype(jnp.bfloat16)


def nt(left, right):
    return lax.dot_general(
        left, right, (((1,), (1,)), ((), ())), preferred_element_type=jnp.float32
    )


def set_bias(bias_ref, seg_row_ref, seg_col_ref, block):
    size = bias_ref.shape[0]
    for first in range(0, size, block):
        for key in range(0, first + block, block):
            allowed = seg_col_ref[key : key + block, :] == seg_row_ref[:, first : first + block]
            if key == first:
                keys = lax.broadcasted_iota(jnp.int32, (block, block), 0)
                queries = lax.broadcasted_iota(jnp.int32, (block, block), 1)
                allowed = jnp.logical_and(allowed, keys <= queries)
            bias_ref[key : key + block, first : first + block] = jnp.where(allowed, 0.0, -1e30)


def turned(values, gain, cosine, sine):
    half = values.shape[0] // 2
    factor = lax.rsqrt(jnp.mean(values * values, 0, keepdims=True) + EPS)
    normed = values * factor * gain
    first, second = normed[:half], normed[half:]
    return jnp.concatenate([first * cosine - second * sine, second * cosine + first * sine], 0)


def turned_back(incoming, values, gain, cosine, sine):
    half = values.shape[0] // 2
    first, second = incoming[:half], incoming[half:]
    incoming = jnp.concatenate(
        [first * cosine + second * sine, second * cosine - first * sine], 0
    )
    factor = lax.rsqrt(jnp.mean(values * values, 0, keepdims=True) + EPS)
    unit = values * factor
    terms = jnp.sum(incoming * unit, 1, keepdims=True)
    scaled = incoming * gain
    return factor * (scaled - unit * jnp.mean(scaled * unit, 0, keepdims=True)), terms


def forward_kernel(
    block, q_ref, kv_ref, cos_ref, sin_ref, gain_ref, row_ref, col_ref,
    o_ref, log_ref, qr_ref, kvr_ref, bias_ref
):
    head = kv_ref.shape[0] // 2
    size = kv_ref.shape[1]
    scale = head ** (-0.5)

    @pl.when(pl.program_id(0) == 0)
    def _():
        set_bias(bias_ref, row_ref, col_ref, block)

    cosine, sine = cos_ref[...], sin_ref[...]
    keys = turned(kv_ref[:head, :], gain_ref[1], cosine, sine)
    kvr_ref[:head, :] = keys.astype(jnp.bfloat16)
    keys = keys.T.astype(jnp.bfloat16)
    values = kv_ref[head:, :].astype(jnp.bfloat16)
    kvr_ref[head:, :] = values
    for which in range(q_ref.shape[0] // head):
        rows = slice(which * head, (which + 1) * head)
        query = turned(q_ref[rows, :], gain_ref[0], cosine, sine).astype(jnp.bfloat16)
        qr_ref[rows, :] = query
        for first in range(0, size, block):
            here = slice(first, first + block)
            total = jnp.zeros((1, block), jnp.float32)
            summed = jnp.zeros((head, block), jnp.float32)
            for key in range(0, first + block, block):
                there = slice(key, key + block)
                scores = jnp.dot(keys[there], query[:, here], preferred_element_type=jnp.float32)
                weight = jnp.exp(scores * scale + bias_ref[there, here])
                total += jnp.sum(weight, 0, keepdims=True)
                summed += jnp.dot(
                    values[:, there],
                    weight.astype(jnp.bfloat16),
                    preferred_element_type=jnp.float32,
                )
            o_ref[rows, here] = summed / total
            log_ref[0, which : which + 1, here] = jnp.log(total)


def backward_kernel(
    block, q_ref, kv_ref, qr_ref, kvr_ref, do_ref, o_ref, log_ref, cos_ref, sin_ref,
    gain_ref, row_ref, col_ref, dq_ref, dkv_ref, gains_ref, bias_ref, dkey_ref, dvalue_ref
):
    head = kv_ref.shape[0] // 2
    size = kv_ref.shape[1]
    scale = head ** (-0.5)

    @pl.when(pl.program_id(0) == 0)
    def _():
        set_bias(bias_ref, row_ref, col_ref, block)
        gains_ref[...] = jnp.zeros_like(gains_ref)

    cosine, sine = cos_ref[...], sin_ref[...]
    keys_t = kvr_ref[:head, :]
    keys = keys_t.astype(jnp.float32).T.astype(jnp.bfloat16)
    values = kvr_ref[head:, :].astype(jnp.float32).T.astype(jnp.bfloat16)
    dkey_ref[...] = jnp.zeros_like(dkey_ref)
    dvalue_ref[...] = jnp.zeros_like(dvalue_ref)
    found = []
    for which in range(q_ref.shape[0] // head):
        rows = slice(which * head, (which + 1) * head)
        query = qr_ref[rows, :]
        grad = do_ref[rows, :]
        delta = jnp.sum(grad.astype(jnp.float32) * o_ref[rows, :], 0, keepdims=True)
        pieces = []
        for first in range(0, size, block):
            here = slice(first, first + block)
            dquery = jnp.zeros((head, block), jnp.float32)
            for key in range(0, first + block, block):
                there = slice(key, key + block)
                scores = jnp.dot(keys[there], query[:, here], preferred_element_type=jnp.float32)
                probs = jnp.exp(
                    scores * scale + (bias_ref[there, here] - log_ref[0, which : which + 1, here])
                )
                dprobs = jnp.dot(values[there], grad[:, here], preferred_element_type=jnp.float32)
                dscores = (probs * (dprobs - delta[:, here])).astype(jnp.bfloat16)
                dquery += jnp.dot(keys_t[:, there], dscores, preferred_element_type=jnp.float32)
                dkey_ref[:, there] += nt(query[:, here], dscores)
                dvalue_ref[:, there] += nt(grad[:, here], probs.astype(jnp.bfloat16))
            pieces.append(dquery * scale)
        dquery, terms = turned_back(
            jnp.concatenate(pieces, 1), q_ref[rows, :], gain_ref[0], cosine, sine
        )
        found.append(dquery)
        gains_ref[0] += terms
    dq_ref[...] = jnp.concatenate(found, 0).T.astype(jnp.bfloat16)
    dkey, terms = turned_back(dkey_ref[...] * scale, kv_ref[:head, :], gain_ref[1], cosine, sine)
    dkv_ref[...] = jnp.concatenate([dkey, dvalue_ref[...]], 0).T.astype(jnp.bfloat16)
    gains_ref[1] += terms


def whole_spec(*shape):
    return pl.BlockSpec(shape, lambda i: (0,) * len(shape))


def attend(raw, cosine, sine, gains, segments, kv_own, head, block):
    size = raw.shape[1]
    group = raw.shape[0] // head // kv_own - 2
    query = pl.BlockSpec((group * head, size), lambda i: (i, 0))
    kv_at = group * kv_own // 2
    return pl.pallas_call(
        functools.partial(forward_kernel, block),
        grid=(kv_own,),
        in_specs=[
            query,
            pl.BlockSpec((2 * head, size), lambda i: (kv_at + i, 0)),
            whole_spec(head // 2, size),
            whole_spec(head // 2, size),
            whole_spec(2, head, 1),
            whole_spec(1, size),
            whole_spec(size, 1),
        ],
        out_specs=[
            query,
            pl.BlockSpec((1, group, size), lambda i: (i, 0, 0)),
            query,
            pl.BlockSpec((2 * head, size), lambda i: (i, 0)),
        ],
        out_shape=[
            jax.ShapeDtypeStruct((kv_own * group * head, size), jnp.float32),
            jax.ShapeDtypeStruct((kv_own, group, size), jnp.float32),
            jax.ShapeDtypeStruct((kv_own * group * head, size), jnp.bfloat16),
            jax.ShapeDtypeStruct((kv_own * 2 * head, size), jnp.bfloat16),
        ],
        scratch_shapes=[pltpu.VMEM((size, size), jnp.float32)],
        compiler_params=pltpu.CompilerParams(vmem_limit_bytes=40 * 2**20),
        cost_estimate=pl.CostEstimate(flops=10**6, bytes_accessed=0, transcendentals=0),
    )(raw, raw, cosine, sine, gains, segments[None, :], segments[:, None])


def attend_back(
    raw, turned_q, turned_kv, grad, attended, logs, cosine, sine, gains, segments,
    kv_own, head, block, begin, count
):
    size = raw.shape[1]
    group = raw.shape[0] // head // kv_own - 2
    query = pl.BlockSpec((group * head, size), lambda i: (begin + i, 0))
    kv_at = group * kv_own // 2 + begin
    return pl.pallas_call(
        functools.partial(backward_kernel, block),
        grid=(count,),
        in_specs=[
            query,
            pl.BlockSpec((2 * head, size), lambda i: (kv_at + i, 0)),
            query,
            pl.BlockSpec((2 * head, size), lambda i: (begin + i, 0)),
            query,
            query,
            pl.BlockSpec((1, group, size), lambda i: (begin + i, 0, 0)),
            whole_spec(head // 2, size),
            whole_spec(head // 2, size),
            whole_spec(2, head, 1),
            whole_spec(1, size),
            whole_spec(size, 1),
        ],
        out_specs=[
            pl.BlockSpec((size, group * head), lambda i: (0, i)),
            pl.BlockSpec((size, 2 * head), lambda i: (0, i)),
            whole_spec(2, head, 1),
        ],
        out_shape=[
            jax.ShapeDtypeStruct((size, count * group * head), jnp.bfloat16),
            jax.ShapeDtypeStruct((size, count * 2 * head), jnp.bfloat16),
            jax.ShapeDtypeStruct((2, head, 1), jnp.float32),
        ],
        scratch_shapes=[
            pltpu.VMEM((size, size), jnp.float32),
            pltpu.VMEM((head, size), jnp.float32),
            pltpu.VMEM((head, size), jnp.float32),
        ],
        compiler_params=pltpu.CompilerParams(vmem_limit_bytes=40 * 2**20),
        cost_estimate=pl.CostEstimate(flops=10**6, bytes_accessed=0, transcendentals=0),
    )(
        raw, raw, turned_q, turned_kv, grad, attended, logs, cosine, sine, gains,
        segments[None, :], segments[:, None]
    )


def on_device_fast(
    hidden_in,
    out_grad,
    segment_ids,
    doc_positions,
    attn_gain,
    head_gains,
    w_query,
    w_key,
    w_value,
    w_out,
    ffn_gain,
    w_gate,
    w_up,
    w_down,
):
    low, full = jnp.bfloat16, jnp.float32
    dp, ctx = lax.axis_index("dp"), lax.axis_index("ctx")
    ctx_count = lax.axis_size("ctx")
    core, side, high = dp % 2, dp // 2 % 2, dp // 4
    width = hidden_in.shape[-1]
    rows = w_query.shape[0]
    head = head_gains.shape[0] * lax.axis_size("dp") * ctx_count // 2
    group = w_query.shape[1] // w_key.shape[1]
    kv_own = w_key.shape[1] // head // 2
    units = w_down.shape[0] * ctx_count

    tokens = hidden_in.shape[2]
    marks = jnp.stack(
        [segment_ids[:, 0], doc_positions[:, 0] // 256, doc_positions[:, 0] % 256], 1
    ).reshape(2, 1, -1)
    marks = jnp.pad(marks, ((0, 0), (0, 15), (0, width - 3 * tokens))).astype(low)
    both_came, both_kept = spread(jnp.concatenate([hidden_in[:, 0], marks, out_grad[:, 0]], 1))

    head_few = head_gains.shape[0]
    gains = jnp.stack([attn_gain, ffn_gain, jnp.pad(head_gains, (0, rows - head_few))])
    gains = jnp.pad(gains, ((0, rows - 3), (0, 128 - rows)))
    key_value = jnp.stack([w_key.reshape(rows, -1, 2, head), w_value.reshape(rows, -1, 2, head)], 3)
    parities = [
        jnp.concatenate(
            [
                w_query.reshape(rows, -1, 2, group * head)[:, :, which].reshape(rows, -1),
                key_value[:, :, which].reshape(rows, -1),
                gains,
            ],
            1,
        )
        for which in range(2)
    ]
    inner = parities[0].shape[1]

    tops = w_gate.shape[1] // units // 4

    def of_member(which):
        return [
            jnp.concatenate(
                [w[:, (top * 4 + which) * units : (top * 4 + which + 1) * units] for top in range(tops)],
                1,
            )
            for w in (w_gate, w_up)
        ]

    def related(zero, one, two, three):
        near, far = choose(side, zero, two), choose(side, two, zero)
        near_far, far_far = choose(side, one, three), choose(side, three, one)
        return (
            choose(core, near, near_far),
            choose(core, far, far_far),
            choose(core, near_far, near),
            choose(core, far_far, far),
        )

    members = [of_member(which) for which in range(4)]
    gate_of = related(*[member[0] for member in members])
    up_of = related(*[member[1] for member in members])
    from_core = flip(
        joined(choose(core, parities[1], parities[0]), gate_of[2], up_of[2], gate_of[3], up_of[3]),
        CORE,
    )
    block = joined(
        choose(core, parities[0], from_core[0]),
        choose(core, from_core[0], parities[1]),
        jnp.pad(w_out, ((0, 0), (0, inner - width))),
    )
    from_side = flip(joined(gate_of[1], up_of[1], from_core[3], from_core[4]), SIDE)
    blocks = [block]
    for step in range(ctx_count - 1):
        blocks.append(spin(blocks[-1]))

    def across(pair):
        return [pair, flip(pair, SIDE), flip(pair, HIGH), flip(pair, SIDE | HIGH)]

    early = across(jnp.concatenate(blocks[:2], 0))
    blocks[3], *rest = hold(blocks[3], *both_came, *early)
    both_came, early = rest[:2], rest[2:]
    late = across(jnp.concatenate(blocks[2:], 0))
    block_ffn = unit_block(
        [side * 2 + core, side * 2 + 1 - core, 2 - side * 2 + core, 2 - side * 2 + 1 - core],
        joined(gate_of[0], up_of[0]), from_core, from_side, w_down,
    )
    ffn_blocks = [block_ffn, spin(block_ffn)]
    got = settled(both_came, both_kept)
    taken = tokens + 16
    x_half = order(ctx // 2, got[0][:taken], got[1][:taken])
    x_other = flip(x_half, CORE)
    x_half, *late = hold(x_half, *late)
    ffn_far = [flip(block_ffn, HIGH)]
    df = order(ctx // 2, got[0][taken:], got[1][taken:]).reshape(-1, width)
    df_side, df_core = flip(df, SIDE), flip(df, CORE)
    pieces = [
        pair[3 * part : 3 * part + 3] for pairs in (early, late) for part in range(2) for pair in pairs
    ]

    slots = []
    for step in range(ctx_count):
        place = (ctx - step) % ctx_count
        for far in range(4):
            up = 1 - high if far >= 2 else high
            across_to = 1 - side if far % 2 == 1 else side
            chip = up * 2 + across_to
            slots += [(chip * 2 + c) * ctx_count + place for c in range(2)]
            slots += [chip * ctx_count + place]
    w_in, w_mine = placed(pieces, (0, 0, 1), slots, (8 * ctx_count, 4 * ctx_count))
    w_in, w_mine = w_in.reshape(-1, inner), w_mine.reshape(-1, inner)[:, :width]
    w_in, w_mine, x_other, ffn_blocks[1], ffn_far[0] = hold(
        w_in, w_mine, x_other, ffn_blocks[1], ffn_far[0]
    )
    ffn_blocks.append(spin(ffn_blocks[1]))
    ffn_far.append(flip(ffn_blocks[1], HIGH))
    w_theirs = flip(w_mine, CORE)
    features = inner - 128
    gains_all = w_in[:, features:].reshape(-1, rows, 128)[:, :3, :rows].astype(full)
    w_in = w_in[:, :features]
    attn_gain_all, ffn_gain_all = gains_all[:, 0].reshape(-1), gains_all[:, 1].reshape(-1)
    head_gains_all = gains_all[:, 2, :head_few].reshape(2, head, 1)

    x_all = order(core, x_half, x_other)
    marks = x_all[:, :, tokens, : 3 * tokens].reshape(-1, 3, tokens)
    x_all, x_half = x_all[:, :, :tokens].reshape(-1, width), x_half[:, :tokens].reshape(-1, width)
    segments = marks[:, 0].reshape(-1).astype(jnp.int32)
    places = (256.0 * marks[:, 1].astype(full) + marks[:, 2].astype(full)).reshape(-1)
    normed, _, _ = norm_forward(x_all.astype(full), attn_gain_all)
    a_low = normed.astype(low)
    raw = lax.dot_general(w_in, a_low, (((0,), (1,)), ((), ())), preferred_element_type=full)
    freq = THETA ** (-(jnp.arange(head // 2, dtype=full) * 2.0 / head))
    turn = freq[:, None] * places[None, :]
    cosine, sine = jnp.cos(turn), jnp.sin(turn)
    attended, logs, turned_q, turned_kv = attend(
        raw, cosine, sine, head_gains_all, segments, kv_own, head, 256
    )
    attended_low = attended.astype(low)
    attended_low, ffn_blocks[2], ffn_far[1], df_side, df_core, w_theirs = hold(
        attended_low, ffn_blocks[2], ffn_far[1], df_side, df_core, w_theirs
    )
    df_both = flip(df_side, CORE)
    ffn_blocks.append(spin(ffn_blocks[2]))
    ffn_far.append(flip(ffn_blocks[2], HIGH))
    o_theirs = flip(half_of(1 - core, attended_low, 1), CORE)
    hidden = (
        x_half.astype(full)
        + left_trans(half_of(core, attended_low, 1), w_mine)
        + left_trans(o_theirs, w_theirs)
    )
    normed_two, h_unit, h_factor = norm_forward(hidden, ffn_gain_all)
    b_own = swap_halves(high, normed_two.astype(low), 1)
    b_own, ffn_blocks[3], ffn_far[2], df_both = hold(b_own, ffn_blocks[3], ffn_far[2], df_both)
    ffn_far.append(flip(ffn_blocks[3], HIGH))
    b_side, b_core = flip(b_own, SIDE), flip(b_own, CORE)
    b_side, b_core, ffn_far[3] = hold(b_side, b_core, ffn_far[3])
    b_both = flip(b_side, CORE)

    units_of = functools.partial(
        feed_forward,
        [(ctx - step) % ctx_count for step in range(ctx_count)] + [high],
        [block for pair in zip(ffn_blocks, ffn_far) for block in pair],
        rows,
    )
    *left, db_side, db_both, out_side, out_both = units_of(
        [b_side, b_both], [df_side, df_both], 256, 2, []
    )
    got_both, got_out_both = flip(db_both, CORE), flip(out_both, CORE)
    db_far = total_low(db_side, got_both)
    db_far, b_own, b_core, got_out_both = hold(db_far, b_own, b_core, got_out_both)
    got_side = flip(db_far, SIDE)
    act, d_pre, team_b, team_df, db_own, db_core, out_own, out_core = units_of(
        [b_own, b_core], [df, df_core], 256, 0, left
    )
    block_side = total_low(out_side, got_out_both)
    db_core, d_pre, act, got_side, block_side = hold(db_core, d_pre, act, got_side, block_side)
    got_core, got_out_core, got_block = flip(db_core, CORE), flip(out_core, CORE), flip(block_side, SIDE)

    def behind(step):
        return (ctx - 1 - step) % ctx_count

    g_down = left_trans(act, team_df).astype(low)
    g_down, team_b = hold(g_down, team_b)
    g_ffn = left_trans(team_b, d_pre).astype(low)
    terms = spread_units(
        [behind(step) for step in range(ctx_count)] + [high], g_ffn, g_down, rows, ctx_count
    )
    *terms, got_core, got_out_core, got_block = hold(*terms, got_core, got_out_core, got_block)
    near_terms = terms[:ctx_count]
    far_got = [flip(term, HIGH) for term in terms[ctx_count:]]
    block_out = hidden + out_own.astype(full) + got_out_core.astype(full) + got_block.astype(full)
    block_came, block_kept = unspread(block_out.astype(low).reshape(2, -1, width))

    db = db_own.astype(full) + got_core.astype(full) + got_side.astype(full)
    db = swap_halves(high, db, 1)
    d_hidden, ffn_terms = norm_backward(db, h_unit, h_factor, ffn_gain_all)
    d_hidden = df.astype(full) + d_hidden
    dz = d_hidden.astype(low)
    dz_other = flip(dz, CORE)
    dz_all = order(core, dz, dz_other).reshape(-1, width)
    d_attended = right_trans(w_mine, dz_all).astype(low)
    g_out = matmul(attended_low, dz_all).astype(low).reshape(2, 2, ctx_count, -1, width)

    def side_square(array):
        near = jnp.where(side == 0, array[:, 0], array[:, 1])
        far = jnp.where(side == 0, array[:, 1], array[:, 0])
        near = joined(pick(near, high), pick(near, 1 - high))
        return near, flip(joined(pick(far, high), pick(far, 1 - high)), SIDE)

    def high_square(near, got):
        sums = near.astype(full) + got.astype(full)
        return sums[0], flip(sums[1].astype(low), HIGH)

    def total(terms):
        return functools.reduce(lambda a, b: a + b, [term.astype(full) for term in terms])

    back = functools.partial(
        attend_back, raw, turned_q, turned_kv, attended=attended, logs=logs, cosine=cosine,
        sine=sine, gains=head_gains_all, segments=segments, kv_own=kv_own, head=head, block=256
    )
    g_out = jnp.stack([pick(g_out, behind(step), 2) for step in range(ctx_count)], 2)
    g_out, d_attended, far_got[0], *block_came = hold(g_out, d_attended, far_got[0], *block_came)
    unit_total = total_low(near_terms[0], far_got[0])
    d_attended, unit_total = hold(d_attended, unit_total)
    unit_ring = spin(unit_total)
    out_near, out_got = side_square(g_out)
    dq, dkv, g_heads = back(grad=d_attended, begin=0, count=kv_own)
    dq, out_got, unit_ring, far_got[1] = hold(dq, out_got, unit_ring, far_got[1])
    out_near, out_got = high_square(out_near, out_got)
    unit_total = total_low(unit_ring, total_low(near_terms[1], far_got[1]))
    unit_ring = spin(unit_total)
    d_raw = jnp.concatenate([dq, dkv], 1)
    d_theirs = right_trans(half_of(1 - core, d_raw, 0), w_in).astype(low)
    d_theirs, d_raw = hold(d_theirs, d_raw)
    d_from = flip(d_theirs, CORE)
    g_in = left_trans(a_low, d_raw).astype(low)
    g_in = g_in.reshape(2, 2, 2, ctx_count, rows, features)
    g_in = jnp.stack([pick(g_in, behind(step), 3) for step in range(ctx_count)], 2)
    g_in, d_raw = hold(g_in, d_raw)
    early_near, early_got = side_square(g_in[:, :, :2])
    late_near, late_got = side_square(g_in[:, :, 2:])
    d_inner = right_trans(half_of(core, d_raw, 0), w_in)
    d_inner, d_from, out_got = hold(d_inner, d_from, out_got)
    d_inner = d_inner + d_from.astype(full)
    _, x_unit, x_factor = norm_forward(x_half.astype(full), attn_gain_all)
    d_input, attn_terms = norm_backward(d_inner, x_unit, x_factor, attn_gain_all)
    in_grad = (d_hidden + d_input).astype(low)
    out_total = out_near + out_got.astype(full)
    g_gains = jnp.concatenate([jnp.sum(attn_terms, 0), jnp.sum(ffn_terms, 0), g_heads.reshape(-1)])
    g_gains = g_gains.reshape(-1, 128)
    g_gains = jnp.pad(g_gains, ((0, 24 - g_gains.shape[0]), (0, 0)))
    in_grad, early_got, g_gains = hold(in_grad, early_got, g_gains)
    early_near, early_got = high_square(early_near, early_got)
    g_gains = g_gains + flip(g_gains, CORE)
    in_came, in_kept = unspread(in_grad.reshape(2, -1, width))
    early_got, late_got, g_gains, unit_ring, far_got[2] = hold(
        early_got, late_got, g_gains, unit_ring, far_got[2]
    )
    unit_total = total_low(unit_ring, total_low(near_terms[2], far_got[2]))
    unit_ring = spin(unit_total)
    late_near, late_got = high_square(late_near, late_got)
    g_gains = g_gains + flip(g_gains, SIDE)
    g_gains = (g_gains + flip(g_gains, HIGH)).reshape(-1)

    def own_of(place):
        which = dp * ctx_count + place
        row = [
            lax.dynamic_slice(g_gains, (start + which * count,), (count,))
            for start, count in ((0, rows), (width, rows), (2 * width, head_few))
        ]
        row = jnp.concatenate(row)[None]
        return jnp.pad(row, ((0, 15), (0, width - row.shape[1])))

    def terms_of(near, got, first):
        terms = near + got.astype(full)
        return [
            jnp.concatenate(
                [
                    terms[at].reshape(2 * rows, width),
                    out_total[first + at],
                    own_of(behind(first + at)),
                ],
                0,
            )
            for at in range(2)
        ]

    in_terms = terms_of(early_near, early_got, 0)
    in_ring = spin(in_terms[0].astype(low))
    in_ring, late_got = hold(in_ring, late_got)
    in_terms += terms_of(late_near, late_got, 2)
    in_ring = spin((in_ring.astype(full) + in_terms[1]).astype(low))
    in_ring, unit_ring = hold(in_ring, unit_ring)
    in_ring = spin((in_ring.astype(full) + in_terms[2]).astype(low))
    in_ring, far_got[3], *in_came = hold(in_ring, far_got[3], *in_came)
    unit_total = total_low(unit_ring, total_low(near_terms[3], far_got[3]))
    ffn_total = jnp.concatenate(
        [unit_total[: 4 * rows], unit_total[4 * rows : 8 * rows]], 1
    ).reshape(2, 2, rows, -1)
    g_down = unit_total[8 * rows :, :width]

    found = related(
        pick(pick(ffn_total, side), core),
        flip(pick(pick(ffn_total, side), 1 - core), CORE),
        flip(pick(pick(ffn_total, 1 - side), core), SIDE),
        flip(pick(pick(ffn_total, 1 - side), 1 - core), SIDE | CORE),
    )
    found = (found[0], found[2], found[1], found[3])

    def to_columns(first):
        return jnp.concatenate(
            [
                found[which][:, (first + top) * units : (first + top + 1) * units].astype(full)
                for top in range(tops)
                for which in range(4)
            ],
            1,
        )

    g_gate, g_up = to_columns(0), to_columns(tops)

    in_sum = in_ring.astype(full) + in_terms[3]
    g_in, g_out = in_sum[: 2 * rows].astype(low).reshape(2, rows, width), in_sum[2 * rows : 3 * rows]
    g_gains = in_sum[3 * rows]
    in_grad = order(ctx % 2, *settled(in_came, in_kept))
    block_out = order(ctx % 2, *settled(block_came, block_kept))
    own = pick(g_in, core).astype(full)
    got = flip(pick(g_in, 1 - core), CORE).astype(full)
    even, odd = choose(core, own, got), choose(core, got, own)
    first = group * head * kv_own

    def mixed(start, stop, step, size):
        return jnp.concatenate(
            [part[:, at : at + size] for at in range(start, stop, step) for part in (even, odd)], 1
        )

    return (
        block_out[:, None],
        in_grad[:, None],
        g_gains[:rows],
        g_gains[2 * rows : 2 * rows + head_few],
        mixed(0, first, group * head, group * head),
        mixed(first, features, 2 * head, head),
        mixed(first + head, features, 2 * head, head),
        g_out,
        g_gains[rows : 2 * rows],
        g_gate,
        g_up,
        g_down.astype(full),
    )


def solution(mesh):
    placed = (
        P(None, "dp", "ctx", None),
        P(None, "dp", "ctx", None),
        P(None, "dp", "ctx"),
        P(None, "dp", "ctx"),
        P(("dp", "ctx")),
        P(("dp", "ctx")),
        P(("dp", "ctx"), None),
        P(("dp", "ctx"), None),
        P(("dp", "ctx"), None),
        P(("dp", "ctx"), None),
        P(("dp", "ctx")),
        P(("dp", "ctx"), None),
        P(("dp", "ctx"), None),
        P(("dp", "ctx"), None),
    )
    fits = mesh.shape["dp"] == 8 and mesh.shape["ctx"] == 4
    return jax.shard_map(
        on_device_fast if fits else on_device,
        mesh=mesh,
        in_specs=placed,
        out_specs=(
            P(None, "dp", "ctx", None),
            P(None, "dp", "ctx", None),
            P(("dp", "ctx")),
            P(("dp", "ctx")),
            P(("dp", "ctx"), None),
            P(("dp", "ctx"), None),
            P(("dp", "ctx"), None),
            P(("dp", "ctx"), None),
            P(("dp", "ctx")),
            P(("dp", "ctx"), None),
            P(("dp", "ctx"), None),
            P(("dp", "ctx"), None),
        ),
        check_vma=False,
    )
```

```python
import functools

import jax
import jax.numpy as jnp
from jax import lax
from jax.experimental import pallas as pl
from jax.experimental.pallas import tpu as pltpu
from jax.sharding import PartitionSpec as P

EPS = 1e-05
THETA = 1000000.0


def matmul(left, right):
    return jnp.dot(left, right, preferred_element_type=jnp.float32)


def left_trans(left, right):
    return lax.dot_general(
        left, right, (((0,), (0,)), ((), ())), preferred_element_type=jnp.float32
    )


def right_trans(left, right):
    return lax.dot_general(
        left, right, (((1,), (1,)), ((), ())), preferred_element_type=jnp.float32
    )


def norm_forward(values, gain):
    factor = lax.rsqrt(jnp.mean(values * values, -1, keepdims=True) + EPS)
    unit = values * factor
    return (unit * gain, unit, factor)


def norm_backward(incoming, unit, factor, gain):
    scaled = incoming * gain
    result = factor * (scaled - unit * jnp.mean(scaled * unit, -1, keepdims=True))
    return (result, incoming * unit)


def angles(places, half):
    freq = THETA ** (-(jnp.arange(half, dtype=jnp.float32) * 2.0 / (2 * half)))
    turn = places.astype(jnp.float32)[:, None] * freq[None, :]
    return (jnp.cos(turn)[:, None, :], jnp.sin(turn)[:, None, :])


def rotate(values, cosine, sine, sign):
    half = values.shape[-1] // 2
    first = values[..., :half]
    second = values[..., half:]
    return jnp.concatenate(
        [first * cosine - sign * second * sine, second * cosine + sign * first * sine], -1
    )


def fetch_weights(shards):
    return (
        lax.all_gather(shards[0], ("dp", "ctx"), axis=0, tiled=True),
        lax.all_gather(shards[1], ("dp", "ctx"), axis=0, tiled=True),
        lax.all_gather(shards[2], ("dp", "ctx"), axis=0, tiled=True),
        lax.all_gather(shards[3], ("dp", "ctx"), axis=0, tiled=True),
        lax.all_gather(shards[4], ("dp", "ctx"), axis=0, tiled=True),
        lax.all_gather(shards[5], ("dp", "ctx"), axis=0, tiled=True),
        lax.all_gather(shards[6], ("dp", "ctx"), axis=0, tiled=True),
        lax.all_gather(shards[7], ("dp", "ctx"), axis=0, tiled=True),
        lax.all_gather(shards[8], ("dp", "ctx"), axis=0, tiled=True),
        lax.all_gather(shards[9], ("dp", "ctx"), axis=0, tiled=True),
    )


def fetch_again(shards):
    return (
        lax.all_gather(shards[0], ("dp", "ctx"), axis=0, tiled=True),
        lax.all_gather(shards[1], ("dp", "ctx"), axis=0, tiled=True),
        lax.all_gather(shards[2], ("dp", "ctx"), axis=0, tiled=True),
        lax.all_gather(shards[3], ("dp", "ctx"), axis=0, tiled=True),
        lax.all_gather(shards[4], ("dp", "ctx"), axis=0, tiled=True),
        lax.all_gather(shards[5], ("dp", "ctx"), axis=0, tiled=True),
        lax.all_gather(shards[6], ("dp", "ctx"), axis=0, tiled=True),
        lax.all_gather(shards[7], ("dp", "ctx"), axis=0, tiled=True),
        lax.all_gather(shards[8], ("dp", "ctx"), axis=0, tiled=True),
        lax.all_gather(shards[9], ("dp", "ctx"), axis=0, tiled=True),
    )


def attention_forward(query_low, key_low, value_low, segments, again):
    rows, heads, head = query_low.shape
    kv_heads = key_low.shape[1] // head
    group = heads // kv_heads
    scale = head ** (-0.5)
    grouped = query_low.reshape(rows, kv_heads, group, head)
    query_index = lax.axis_index("ctx") * rows + jnp.arange(rows, dtype=jnp.int32)

    def visit(carry, piece):
        highest, total, summed = carry
        key_piece, value_piece, segment_piece = piece
        width = key_piece.shape[0]
        key_heads = key_piece.reshape(width, kv_heads, head)
        value_heads = value_piece.reshape(width, kv_heads, head)
        scores = (
            jnp.einsum("qkgd,skd->kgqs", grouped, key_heads, preferred_element_type=jnp.float32)
            * scale
        )
        key_index = jnp.arange(width, dtype=jnp.int32)
        allowed = (segments[:, None] == segment_piece[None, :]) & (
            query_index[:, None] >= key_index[None, :]
        )
        scores = jnp.where(allowed, scores, -1e30)
        peak = jnp.maximum(highest, jnp.max(scores, -1))
        weight = jnp.where(allowed, jnp.exp(scores - peak[..., None]), 0.0)
        total = jnp.sum(weight, -1)
        summed = jnp.einsum(
            "kgqs,skd->qkgd",
            weight.astype(jnp.bfloat16),
            value_heads,
            preferred_element_type=jnp.float32,
        )
        return (peak, total, summed)

    initial = (
        jnp.full((kv_heads, group, rows), -1e30, jnp.float32),
        jnp.zeros((kv_heads, group, rows), jnp.float32),
        jnp.zeros((rows, kv_heads, group, head), jnp.float32),
    )
    if again:
        highest, total, summed = visit(
            initial,
            (
                lax.all_gather(key_low, "ctx", axis=0, tiled=True),
                lax.all_gather(value_low, "ctx", axis=0, tiled=True),
                lax.all_gather(segments, "ctx", axis=0, tiled=True),
            ),
        )
    else:
        highest, total, summed = visit(
            initial,
            (
                lax.all_gather(key_low, "ctx", axis=0, tiled=True),
                lax.all_gather(value_low, "ctx", axis=0, tiled=True),
                lax.all_gather(segments, "ctx", axis=0, tiled=True),
            ),
        )
    attended = (summed / jnp.transpose(total, (2, 0, 1))[..., None]).reshape(rows, heads, head)
    return (attended, highest + jnp.log(total))


def forward(values_row, segments, places, weights, again):
    attn_gain, head_gains, w_query, w_key, w_value, w_out, ffn_gain, w_gate, w_up, w_down = weights
    rows = values_row.shape[0]
    head = head_gains.shape[0] // 2
    heads = w_query.shape[1] // head
    kv_heads = w_key.shape[1] // head
    gains = head_gains.astype(jnp.float32)
    state = {}
    state["values"] = values_row.astype(jnp.float32)
    normed, state["x_unit"], state["x_factor"] = norm_forward(
        state["values"], attn_gain.astype(jnp.float32)
    )
    state["a_low"] = normed.astype(jnp.bfloat16)
    query = matmul(state["a_low"], w_query).reshape(rows, heads, head)
    keys = matmul(state["a_low"], w_key).reshape(rows, kv_heads, head)
    state["value_low"] = matmul(state["a_low"], w_value).astype(jnp.bfloat16)
    state["cosine"], state["sine"] = angles(places, head // 2)
    query_normed, state["q_unit"], state["q_factor"] = norm_forward(query, gains[:head])
    key_normed, state["k_unit"], state["k_factor"] = norm_forward(keys, gains[head:])
    state["query_low"] = rotate(query_normed, state["cosine"], state["sine"], 1.0).astype(
        jnp.bfloat16
    )
    state["key_low"] = (
        rotate(key_normed, state["cosine"], state["sine"], 1.0)
        .astype(jnp.bfloat16)
        .reshape(rows, kv_heads * head)
    )
    state["attended"], state["log_total"] = attention_forward(
        state["query_low"], state["key_low"], state["value_low"], segments, again
    )
    state["attended_low"] = state["attended"].astype(jnp.bfloat16).reshape(rows, heads * head)
    hidden = state["values"] + matmul(state["attended_low"], w_out)
    normed_two, state["h_unit"], state["h_factor"] = norm_forward(
        hidden, ffn_gain.astype(jnp.float32)
    )
    state["b_low"] = normed_two.astype(jnp.bfloat16)
    state["gate"] = matmul(state["b_low"], w_gate)
    state["upper"] = matmul(state["b_low"], w_up)
    state["act_low"] = (jax.nn.silu(state["gate"]) * state["upper"]).astype(jnp.bfloat16)
    state["output"] = hidden + matmul(state["act_low"], w_down)
    return state


def backward(grad_row, segments, weights, state):
    attn_gain, head_gains, w_query, w_key, w_value, w_out, ffn_gain, w_gate, w_up, w_down = weights
    query_low = state["query_low"]
    rows, heads, head = query_low.shape
    kv_heads = state["key_low"].shape[1] // head
    group = heads // kv_heads
    scale = head ** (-0.5)
    gains = head_gains.astype(jnp.float32)
    incoming = grad_row.astype(jnp.float32)
    down_low = incoming.astype(jnp.bfloat16)
    g_down = left_trans(state["act_low"], down_low)
    d_act = right_trans(down_low, w_down)
    sigma = jax.nn.sigmoid(state["gate"])
    d_upper = (d_act * state["gate"] * sigma).astype(jnp.bfloat16)
    d_gate = (d_act * state["upper"] * sigma * (1.0 + state["gate"] * (1.0 - sigma))).astype(
        jnp.bfloat16
    )
    g_gate = left_trans(state["b_low"], d_gate)
    g_up = left_trans(state["b_low"], d_upper)
    d_normed = right_trans(d_gate, w_gate) + right_trans(d_upper, w_up)
    d_hidden, terms = norm_backward(
        d_normed, state["h_unit"], state["h_factor"], ffn_gain.astype(jnp.float32)
    )
    g_ffn = jnp.sum(terms, 0)
    d_hidden = incoming + d_hidden
    branch_low = d_hidden.astype(jnp.bfloat16)
    g_out = left_trans(state["attended_low"], branch_low)
    d_attended = (
        right_trans(branch_low, w_out).astype(jnp.bfloat16).reshape(rows, kv_heads, group, head)
    )
    delta = jnp.sum(
        d_attended.astype(jnp.float32) * state["attended"].reshape(rows, kv_heads, group, head), -1
    )
    delta = jnp.transpose(delta, (1, 2, 0))
    log_total = state["log_total"]
    grouped = query_low.reshape(rows, kv_heads, group, head)
    query_index = lax.axis_index("ctx") * rows + jnp.arange(rows, dtype=jnp.int32)
    key_piece = lax.all_gather(state["key_low"], "ctx", axis=0, tiled=True)
    value_piece = lax.all_gather(state["value_low"], "ctx", axis=0, tiled=True)
    segment_piece = lax.all_gather(segments, "ctx", axis=0, tiled=True)
    width = key_piece.shape[0]
    key_heads = key_piece.reshape(width, kv_heads, head)
    value_heads = value_piece.reshape(width, kv_heads, head)
    scores = (
        jnp.einsum("qkgd,skd->kgqs", grouped, key_heads, preferred_element_type=jnp.float32) * scale
    )
    key_index = jnp.arange(width, dtype=jnp.int32)
    allowed = (segments[:, None] == segment_piece[None, :]) & (
        query_index[:, None] >= key_index[None, :]
    )
    probs = jnp.where(allowed, jnp.exp(scores - log_total[..., None]), 0.0)
    d_probs = jnp.einsum(
        "qkgd,skd->kgqs", d_attended, value_heads, preferred_element_type=jnp.float32
    )
    d_scores = (probs * (d_probs - delta[..., None])).astype(jnp.bfloat16)
    d_query = (
        jnp.einsum("kgqs,skd->qkgd", d_scores, key_heads, preferred_element_type=jnp.float32)
        * scale
    )
    key_part = (
        jnp.einsum("kgqs,qkgd->skd", d_scores, grouped, preferred_element_type=jnp.float32) * scale
    )
    value_part = jnp.einsum(
        "kgqs,qkgd->skd", probs.astype(jnp.bfloat16), d_attended, preferred_element_type=jnp.float32
    )
    d_keys = key_part.reshape(width, kv_heads * head)
    d_values = value_part.reshape(width, kv_heads * head)
    d_query, d_keys_all, d_values_all = (d_query, d_keys, d_values)
    d_keys, d_values = (
        lax.psum_scatter(
            d_keys_all.astype(jnp.bfloat16), "ctx", scatter_dimension=0, tiled=True
        ).astype(jnp.float32),
        lax.psum_scatter(
            d_values_all.astype(jnp.bfloat16), "ctx", scatter_dimension=0, tiled=True
        ).astype(jnp.float32),
    )
    d_query = rotate(d_query.reshape(rows, heads, head), state["cosine"], state["sine"], -1.0)
    d_query, query_terms = norm_backward(d_query, state["q_unit"], state["q_factor"], gains[:head])
    d_keys = rotate(d_keys.reshape(rows, kv_heads, head), state["cosine"], state["sine"], -1.0)
    d_keys, key_terms = norm_backward(d_keys, state["k_unit"], state["k_factor"], gains[head:])
    g_heads = jnp.concatenate([jnp.sum(query_terms, (0, 1)), jnp.sum(key_terms, (0, 1))])
    query_grad_low = d_query.astype(jnp.bfloat16).reshape(rows, heads * head)
    key_grad_low = d_keys.astype(jnp.bfloat16).reshape(rows, kv_heads * head)
    value_grad_low = d_values.astype(jnp.bfloat16)
    g_query = left_trans(state["a_low"], query_grad_low)
    g_key = left_trans(state["a_low"], key_grad_low)
    g_value = left_trans(state["a_low"], value_grad_low)
    d_inner = (
        right_trans(query_grad_low, w_query)
        + right_trans(key_grad_low, w_key)
        + right_trans(value_grad_low, w_value)
    )
    d_input, terms = norm_backward(
        d_inner, state["x_unit"], state["x_factor"], attn_gain.astype(jnp.float32)
    )
    g_attn = jnp.sum(terms, 0)
    in_grad = (d_hidden + d_input).astype(jnp.bfloat16)
    return (in_grad, (g_attn, g_heads, g_query, g_key, g_value, g_out, g_ffn, g_gate, g_up, g_down))


def on_device(
    hidden_in,
    out_grad,
    segment_ids,
    doc_positions,
    attn_gain,
    head_gains,
    w_query,
    w_key,
    w_value,
    w_out,
    ffn_gain,
    w_gate,
    w_up,
    w_down,
):
    shards = (attn_gain, head_gains, w_query, w_key, w_value, w_out, ffn_gain, w_gate, w_up, w_down)
    micro = hidden_in.shape[0]
    outputs = []
    for micro_index in range(micro):
        weights = fetch_weights(shards)
        state = forward(
            hidden_in[micro_index, 0],
            segment_ids[micro_index, 0],
            doc_positions[micro_index, 0],
            weights,
            False,
        )
        outputs.append(state["output"].astype(jnp.bfloat16))
    in_grads = []
    totals = None
    for micro_index in range(micro):
        weights = fetch_again(shards)
        state = forward(
            hidden_in[micro_index, 0],
            segment_ids[micro_index, 0],
            doc_positions[micro_index, 0],
            weights,
            True,
        )
        in_grad, grads = backward(
            out_grad[micro_index, 0], segment_ids[micro_index, 0], weights, state
        )
        in_grads.append(in_grad)
        if totals is None:
            totals = grads
        else:
            totals = tuple((left + right for left, right in zip(totals, grads)))
    totals = lax.psum_scatter(totals, ("dp", "ctx"), scatter_dimension=0, tiled=True)
    block_out = jnp.stack(outputs)[:, None]
    input_grads = jnp.stack(in_grads)[:, None]
    return (
        block_out,
        input_grads,
        totals[0],
        totals[1],
        totals[2],
        totals[3],
        totals[4],
        totals[5],
        totals[6],
        totals[7],
        totals[8],
        totals[9],
    )


CORE, SIDE, HIGH = 1, 2, 4


def flip(array, bits):
    count = lax.axis_size("dp")
    return lax.ppermute(array, "dp", [(i, i ^ bits) for i in range(count)])


def spin(array):
    count = lax.axis_size("ctx")
    return lax.ppermute(array, "ctx", [(i, (i + 1) % count) for i in range(count)])


def hold(*arrays):
    return lax.optimization_barrier(arrays)


def choose(bit, zero, one):
    return jnp.where(bit == 0, zero, one)


def pick(array, index, axis=0):
    return lax.dynamic_index_in_dim(array, index, axis, keepdims=False)


def put(buffer, array, *place):
    index = place + (0,) * (buffer.ndim - len(place))
    shape = (1,) * (buffer.ndim - array.ndim) + array.shape
    return lax.dynamic_update_slice(buffer, array.reshape(shape), index)


def place_kernel(splits, count, slots_ref, *refs):
    pieces, outs = refs[:count], refs[count:]
    at = 0
    for piece in pieces:
        for part in range(len(splits)):
            outs[splits[part]][slots_ref[at]] = piece[part]
            at += 1


def placed(pieces, splits, slots, counts):
    shape = pieces[0].shape
    return pl.pallas_call(
        functools.partial(place_kernel, splits, len(pieces)),
        in_specs=[pl.BlockSpec(memory_space=pltpu.SMEM)]
        + [pl.BlockSpec(memory_space=pltpu.VMEM)] * len(pieces),
        out_specs=[pl.BlockSpec(memory_space=pltpu.VMEM)] * len(counts),
        out_shape=[
            jax.ShapeDtypeStruct((count,) + shape[1:], pieces[0].dtype) for count in counts
        ],
        compiler_params=pltpu.CompilerParams(vmem_limit_bytes=40 * 2**20),
    )(jnp.stack(slots).astype(jnp.int32), *pieces)


def block_kernel(slots_ref, own_ref, core_ref, side_ref, down_ref, out_ref):
    rows = own_ref.shape[1]
    for member, ref, first in ((0, own_ref, 0), (1, core_ref, 1), (2, side_ref, 0), (3, side_ref, 2)):
        for part in range(2):
            start = pl.multiple_of((part * 4 + slots_ref[member]) * rows, rows)
            out_ref[pl.ds(start, rows), :] = ref[first + part]
    out_ref[8 * rows :, : down_ref.shape[1]] = down_ref[...]
    out_ref[8 * rows :, down_ref.shape[1] :] = jnp.zeros_like(
        out_ref[8 * rows :, down_ref.shape[1] :]
    )


def unit_block(slots, own, from_core, from_side, down):
    rows, columns = own.shape[1:]
    shape = (8 * rows + down.shape[0], columns)
    return pl.pallas_call(
        block_kernel,
        in_specs=[pl.BlockSpec(memory_space=pltpu.SMEM)]
        + [pl.BlockSpec(memory_space=pltpu.VMEM)] * 4,
        out_specs=pl.BlockSpec(memory_space=pltpu.VMEM),
        out_shape=jax.ShapeDtypeStruct(shape, own.dtype),
    )(jnp.stack(slots).astype(jnp.int32), own, from_core, from_side, down)


def unit_kernel(chunk, ctx_count, tiles, rows, slots_ref, *refs):
    pieces, refs = refs[: 2 * ctx_count], refs[2 * ctx_count :]
    b_refs, df_refs = refs[:2], refs[2:4]
    act_ref, pre_ref, all_b_ref, all_df_ref = refs[-12:-8]
    db_refs, out_refs, (w_ref, down_ref, b_ref, df_ref) = refs[-8:-6], refs[-6:-4], refs[-4:]
    mid = pieces[0].shape[1]
    width = down_ref.shape[1]
    down_rows = pieces[0].shape[0] - 8 * rows
    tile = pl.program_id(0)

    @pl.when(tile == 0)
    def _():
        high = slots_ref[ctx_count]
        for step in range(ctx_count):
            place = slots_ref[step]
            for far in range(2):
                piece = pieces[2 * step + far]
                for member in range(4):
                    first = ((far * 4 + member) * ctx_count + place) * rows
                    to = pl.ds(pl.multiple_of(first, rows), rows)
                    w_ref[to, :mid] = piece[member * rows : (member + 1) * rows, :]
                    w_ref[to, mid:] = piece[(4 + member) * rows : (5 + member) * rows, :]
                half = high if far == 0 else 1 - high
                first = (half * ctx_count + place) * down_rows
                to = pl.ds(pl.multiple_of(first, 16), down_rows)
                down_ref[to, :] = piece[8 * rows :, :width]

    for which in range(2):

        @pl.when(tile // tiles == which)
        def _(which=which):
            b_ref[...] = b_refs[which][...]
            df_ref[...] = df_refs[which][...]

    b, df = b_ref[...], df_ref[...]
    all_b_ref[...] = b
    all_df_ref[...] = df
    db, out = 0.0, 0.0
    for first, last in ((0, chunk), (chunk, mid)):
        here, there = slice(first, last), slice(mid + first, mid + last)
        gate = jnp.dot(b, w_ref[:, here], preferred_element_type=jnp.float32)
        upper = jnp.dot(b, w_ref[:, there], preferred_element_type=jnp.float32)
        d_act = nt(df, down_ref[here, :])
        sigma = 1.0 / (1.0 + jnp.exp(-gate))
        silu = gate * sigma
        act = (silu * upper).astype(jnp.bfloat16)
        d_upper = (d_act * silu).astype(jnp.bfloat16)
        d_gate = (d_act * upper * sigma * (1.0 + gate * (1.0 - sigma))).astype(jnp.bfloat16)
        act_ref[:, here] = act
        pre_ref[:, here] = d_gate
        pre_ref[:, there] = d_upper
        db += nt(d_gate, w_ref[:, here]) + nt(d_upper, w_ref[:, there])
        out += jnp.dot(act, down_ref[here, :], preferred_element_type=jnp.float32)
    for which in range(2):

        @pl.when(tile // tiles == which)
        def _(which=which):
            db_refs[which][...] = db.astype(jnp.bfloat16)
            out_refs[which][...] = out.astype(jnp.bfloat16)


def feed_forward(slots, pieces, rows, b_parts, df_parts, size, begin, left):
    tokens, width = b_parts[0].shape
    mid = pieces[0].shape[1]
    down_rows = pieces[0].shape[0] - 8 * rows
    tiles = tokens // size
    once = lambda array: pl.BlockSpec(
        array.shape, lambda t: (0,) * array.ndim, pipeline_mode=pl.Buffered(1)
    )

    def part(which):
        return pl.BlockSpec((size, width), lambda t: (jnp.clip(t - which * tiles, 0, tiles - 1), 0))

    def tiled(count, first):
        return pl.BlockSpec((size, count), lambda t: (first + t, 0))

    first = begin * tiles
    first_left = 1 + len(pieces) + 4
    full = lambda count: jax.ShapeDtypeStruct((4 * tokens, count), jnp.bfloat16)
    half = jax.ShapeDtypeStruct((tokens, width), jnp.bfloat16)
    return pl.pallas_call(
        functools.partial(unit_kernel, mid // 512 * 256, len(pieces) // 2, tiles, rows),
        grid=(2 * tiles,),
        in_specs=[pl.BlockSpec(memory_space=pltpu.SMEM)]
        + [once(array) for array in pieces]
        + [part(which) for which in range(2)] * 2
        + [pl.BlockSpec(memory_space=pl.ANY)] * len(left),
        out_specs=[tiled(mid, first), tiled(2 * mid, first), tiled(width, first), tiled(width, first)]
        + [part(which) for which in range(2)] * 2,
        out_shape=[full(mid), full(2 * mid), full(width), full(width)] + [half] * 4,
        input_output_aliases={first_left + at: at for at in range(len(left))},
        scratch_shapes=[
            pltpu.VMEM((width, 2 * mid), jnp.bfloat16),
            pltpu.VMEM((len(pieces) * down_rows, width), jnp.bfloat16),
            pltpu.VMEM((size, width), jnp.bfloat16),
            pltpu.VMEM((size, width), jnp.bfloat16),
        ],
        compiler_params=pltpu.CompilerParams(vmem_limit_bytes=52 * 2**20),
        cost_estimate=pl.CostEstimate(flops=10 * tokens * mid * width, bytes_accessed=0, transcendentals=0),
    )(jnp.stack(slots).astype(jnp.int32), *pieces, *b_parts, *df_parts, *left)


def spread_kernel(ctx_count, rows, slots_ref, ffn_ref, down_ref, *outs):
    mid = ffn_ref.shape[1] // 2
    width = down_ref.shape[1]
    down_rows = down_ref.shape[0] // (2 * ctx_count)
    high = slots_ref[ctx_count]
    for far in range(2):
        half = high if far == 0 else 1 - high
        for step in range(ctx_count):
            place = slots_ref[step]
            out = outs[far * ctx_count + step]
            for member in range(4):
                first = ((far * 4 + member) * ctx_count + place) * rows
                here = pl.ds(pl.multiple_of(first, rows), rows)
                out[member * rows : (member + 1) * rows, :] = ffn_ref[here, :mid]
                out[(4 + member) * rows : (5 + member) * rows, :] = ffn_ref[here, mid:]
            first = (half * ctx_count + place) * down_rows
            here = pl.ds(pl.multiple_of(first, 16), down_rows)
            out[8 * rows :, :width] = down_ref[here, :]
            out[8 * rows :, width:] = jnp.zeros_like(out[8 * rows :, width:])


def spread_units(slots, ffn, down, rows, ctx_count):
    shape = (8 * rows + down.shape[0] // (2 * ctx_count), ffn.shape[1] // 2)
    return pl.pallas_call(
        functools.partial(spread_kernel, ctx_count, rows),
        in_specs=[pl.BlockSpec(memory_space=pltpu.SMEM)]
        + [pl.BlockSpec(memory_space=pltpu.VMEM)] * 2,
        out_specs=[pl.BlockSpec(memory_space=pltpu.VMEM)] * (2 * ctx_count),
        out_shape=[jax.ShapeDtypeStruct(shape, ffn.dtype)] * (2 * ctx_count),
        compiler_params=pltpu.CompilerParams(vmem_limit_bytes=40 * 2**20),
        cost_estimate=pl.CostEstimate(flops=10**6, bytes_accessed=0, transcendentals=0),
    )(jnp.stack(slots).astype(jnp.int32), ffn, down)


def joined(*arrays):
    buffer = jnp.zeros((len(arrays),) + arrays[0].shape, arrays[0].dtype)
    for at, array in enumerate(arrays):
        buffer = put(buffer, array, at)
    return buffer


def order(bit, own, other):
    buffer = jnp.zeros((2,) + own.shape, own.dtype)
    return put(put(buffer, own, bit), other, 1 - bit)


def swap_halves(bit, array, axis):
    low, high = jnp.split(array, 2, axis)
    return choose(bit, array, jnp.concatenate([high, low], axis))


def half_of(bit, array, axis):
    low, high = jnp.split(array, 2, axis)
    return choose(bit, low, high)


def exchange(array, target, index_of):
    dp_count, ctx_count = lax.axis_size("dp"), lax.axis_size("ctx")
    me = lax.axis_index("dp") * ctx_count + lax.axis_index("ctx")
    came, kept = [], []
    for turn in range(2):
        pairs, stay = [], []
        for dp in range(dp_count):
            for z in range(ctx_count):
                to = target(dp, z, turn)
                if to == (dp, z):
                    stay.append(dp * ctx_count + z)
                else:
                    pairs.append((dp * ctx_count + z, to[0] * ctx_count + to[1]))
        piece = pick(array, index_of(turn))
        came.append(lax.ppermute(piece, ("dp", "ctx"), pairs))
        mine = functools.reduce(jnp.logical_or, [me == which for which in stay]) if stay else None
        kept.append((piece, mine))
    return came, kept


def settled(came, kept):
    return [
        got if mine is None else jnp.where(mine, piece, got)
        for got, (piece, mine) in zip(came, kept)
    ]


def spread(array):
    ctx = lax.axis_index("ctx")

    def target(dp, z, turn):
        return dp // 2 * 2 + z // 2, 2 * ((z + turn) % 2) + dp % 2

    return exchange(array, target, lambda turn: (ctx + turn) % 2)


def unspread(array):
    ctx = lax.axis_index("ctx")

    def target(dp, z, turn):
        return dp // 2 * 2 + z % 2, 2 * (dp % 2) + (z // 2 + turn) % 2

    return exchange(array, target, lambda turn: (ctx // 2 + turn) % 2)


def swap_gather(array, bit_value, bit):
    return order(bit_value, array, flip(array, bit))


def total_low(left, right):
    return (left.astype(jnp.float32) + right.astype(jnp.float32)).astype(jnp.bfloat16)


def nt(left, right):
    return lax.dot_general(
        left, right, (((1,), (1,)), ((), ())), preferred_element_type=jnp.float32
    )


def set_bias(bias_ref, seg_row_ref, seg_col_ref, block):
    size = bias_ref.shape[0]
    for first in range(0, size, block):
        for key in range(0, first + block, block):
            allowed = seg_col_ref[key : key + block, :] == seg_row_ref[:, first : first + block]
            if key == first:
                keys = lax.broadcasted_iota(jnp.int32, (block, block), 0)
                queries = lax.broadcasted_iota(jnp.int32, (block, block), 1)
                allowed = jnp.logical_and(allowed, keys <= queries)
            bias_ref[key : key + block, first : first + block] = jnp.where(allowed, 0.0, -1e30)


def turned(values, gain, cosine, sine):
    half = values.shape[0] // 2
    factor = lax.rsqrt(jnp.mean(values * values, 0, keepdims=True) + EPS)
    normed = values * factor * gain
    first, second = normed[:half], normed[half:]
    return jnp.concatenate([first * cosine - second * sine, second * cosine + first * sine], 0)


def turned_back(incoming, values, gain, cosine, sine):
    half = values.shape[0] // 2
    first, second = incoming[:half], incoming[half:]
    incoming = jnp.concatenate(
        [first * cosine + second * sine, second * cosine - first * sine], 0
    )
    factor = lax.rsqrt(jnp.mean(values * values, 0, keepdims=True) + EPS)
    unit = values * factor
    terms = jnp.sum(incoming * unit, 1, keepdims=True)
    scaled = incoming * gain
    return factor * (scaled - unit * jnp.mean(scaled * unit, 0, keepdims=True)), terms


def forward_kernel(
    block, q_ref, kv_ref, cos_ref, sin_ref, gain_ref, row_ref, col_ref,
    o_ref, log_ref, qr_ref, kvr_ref, bias_ref
):
    head = kv_ref.shape[0] // 2
    size = kv_ref.shape[1]
    scale = head ** (-0.5)

    @pl.when(pl.program_id(0) == 0)
    def _():
        set_bias(bias_ref, row_ref, col_ref, block)

    cosine, sine = cos_ref[...], sin_ref[...]
    keys = turned(kv_ref[:head, :], gain_ref[1], cosine, sine)
    kvr_ref[:head, :] = keys.astype(jnp.bfloat16)
    keys = keys.T.astype(jnp.bfloat16)
    values = kv_ref[head:, :].astype(jnp.bfloat16)
    kvr_ref[head:, :] = values
    for which in range(q_ref.shape[0] // head):
        rows = slice(which * head, (which + 1) * head)
        query = turned(q_ref[rows, :], gain_ref[0], cosine, sine).astype(jnp.bfloat16)
        qr_ref[rows, :] = query
        for first in range(0, size, block):
            here = slice(first, first + block)
            total = jnp.zeros((1, block), jnp.float32)
            summed = jnp.zeros((head, block), jnp.float32)
            for key in range(0, first + block, block):
                there = slice(key, key + block)
                scores = jnp.dot(keys[there], query[:, here], preferred_element_type=jnp.float32)
                weight = jnp.exp(scores * scale + bias_ref[there, here])
                total += jnp.sum(weight, 0, keepdims=True)
                summed += jnp.dot(
                    values[:, there],
                    weight.astype(jnp.bfloat16),
                    preferred_element_type=jnp.float32,
                )
            o_ref[rows, here] = summed / total
            log_ref[0, which : which + 1, here] = jnp.log(total)


def backward_kernel(
    block, q_ref, kv_ref, qr_ref, kvr_ref, do_ref, o_ref, log_ref, cos_ref, sin_ref,
    gain_ref, row_ref, col_ref, dq_ref, dkv_ref, gains_ref, bias_ref, dkey_ref, dvalue_ref
):
    head = kv_ref.shape[0] // 2
    size = kv_ref.shape[1]
    scale = head ** (-0.5)

    @pl.when(pl.program_id(0) == 0)
    def _():
        set_bias(bias_ref, row_ref, col_ref, block)
        gains_ref[...] = jnp.zeros_like(gains_ref)

    cosine, sine = cos_ref[...], sin_ref[...]
    keys_t = kvr_ref[:head, :]
    keys = keys_t.astype(jnp.float32).T.astype(jnp.bfloat16)
    values = kvr_ref[head:, :].astype(jnp.float32).T.astype(jnp.bfloat16)
    dkey_ref[...] = jnp.zeros_like(dkey_ref)
    dvalue_ref[...] = jnp.zeros_like(dvalue_ref)
    found = []
    for which in range(q_ref.shape[0] // head):
        rows = slice(which * head, (which + 1) * head)
        query = qr_ref[rows, :]
        grad = do_ref[rows, :]
        delta = jnp.sum(grad.astype(jnp.float32) * o_ref[rows, :], 0, keepdims=True)
        pieces = []
        for first in range(0, size, block):
            here = slice(first, first + block)
            dquery = jnp.zeros((head, block), jnp.float32)
            for key in range(0, first + block, block):
                there = slice(key, key + block)
                scores = jnp.dot(keys[there], query[:, here], preferred_element_type=jnp.float32)
                probs = jnp.exp(
                    scores * scale + (bias_ref[there, here] - log_ref[0, which : which + 1, here])
                )
                dprobs = jnp.dot(values[there], grad[:, here], preferred_element_type=jnp.float32)
                dscores = (probs * (dprobs - delta[:, here])).astype(jnp.bfloat16)
                dquery += jnp.dot(keys_t[:, there], dscores, preferred_element_type=jnp.float32)
                dkey_ref[:, there] += nt(query[:, here], dscores)
                dvalue_ref[:, there] += nt(grad[:, here], probs.astype(jnp.bfloat16))
            pieces.append(dquery * scale)
        dquery, terms = turned_back(
            jnp.concatenate(pieces, 1), q_ref[rows, :], gain_ref[0], cosine, sine
        )
        found.append(dquery)
        gains_ref[0] += terms
    dq_ref[...] = jnp.concatenate(found, 0).T.astype(jnp.bfloat16)
    dkey, terms = turned_back(dkey_ref[...] * scale, kv_ref[:head, :], gain_ref[1], cosine, sine)
    dkv_ref[...] = jnp.concatenate([dkey, dvalue_ref[...]], 0).T.astype(jnp.bfloat16)
    gains_ref[1] += terms


def whole_spec(*shape):
    return pl.BlockSpec(shape, lambda i: (0,) * len(shape))


def attend(raw, cosine, sine, gains, segments, kv_own, head, block):
    size = raw.shape[1]
    group = raw.shape[0] // head // kv_own - 2
    query = pl.BlockSpec((group * head, size), lambda i: (i, 0))
    kv_at = group * kv_own // 2
    return pl.pallas_call(
        functools.partial(forward_kernel, block),
        grid=(kv_own,),
        in_specs=[
            query,
            pl.BlockSpec((2 * head, size), lambda i: (kv_at + i, 0)),
            whole_spec(head // 2, size),
            whole_spec(head // 2, size),
            whole_spec(2, head, 1),
            whole_spec(1, size),
            whole_spec(size, 1),
        ],
        out_specs=[
            query,
            pl.BlockSpec((1, group, size), lambda i: (i, 0, 0)),
            query,
            pl.BlockSpec((2 * head, size), lambda i: (i, 0)),
        ],
        out_shape=[
            jax.ShapeDtypeStruct((kv_own * group * head, size), jnp.float32),
            jax.ShapeDtypeStruct((kv_own, group, size), jnp.float32),
            jax.ShapeDtypeStruct((kv_own * group * head, size), jnp.bfloat16),
            jax.ShapeDtypeStruct((kv_own * 2 * head, size), jnp.bfloat16),
        ],
        scratch_shapes=[pltpu.VMEM((size, size), jnp.float32)],
        compiler_params=pltpu.CompilerParams(vmem_limit_bytes=40 * 2**20),
        cost_estimate=pl.CostEstimate(flops=10**6, bytes_accessed=0, transcendentals=0),
    )(raw, raw, cosine, sine, gains, segments[None, :], segments[:, None])


def attend_back(
    raw, turned_q, turned_kv, grad, attended, logs, cosine, sine, gains, segments,
    kv_own, head, block, begin, count
):
    size = raw.shape[1]
    group = raw.shape[0] // head // kv_own - 2
    query = pl.BlockSpec((group * head, size), lambda i: (begin + i, 0))
    kv_at = group * kv_own // 2 + begin
    return pl.pallas_call(
        functools.partial(backward_kernel, block),
        grid=(count,),
        in_specs=[
            query,
            pl.BlockSpec((2 * head, size), lambda i: (kv_at + i, 0)),
            query,
            pl.BlockSpec((2 * head, size), lambda i: (begin + i, 0)),
            query,
            query,
            pl.BlockSpec((1, group, size), lambda i: (begin + i, 0, 0)),
            whole_spec(head // 2, size),
            whole_spec(head // 2, size),
            whole_spec(2, head, 1),
            whole_spec(1, size),
            whole_spec(size, 1),
        ],
        out_specs=[
            pl.BlockSpec((size, group * head), lambda i: (0, i)),
            pl.BlockSpec((size, 2 * head), lambda i: (0, i)),
            whole_spec(2, head, 1),
        ],
        out_shape=[
            jax.ShapeDtypeStruct((size, count * group * head), jnp.bfloat16),
            jax.ShapeDtypeStruct((size, count * 2 * head), jnp.bfloat16),
            jax.ShapeDtypeStruct((2, head, 1), jnp.float32),
        ],
        scratch_shapes=[
            pltpu.VMEM((size, size), jnp.float32),
            pltpu.VMEM((head, size), jnp.float32),
            pltpu.VMEM((head, size), jnp.float32),
        ],
        compiler_params=pltpu.CompilerParams(vmem_limit_bytes=40 * 2**20),
        cost_estimate=pl.CostEstimate(flops=10**6, bytes_accessed=0, transcendentals=0),
    )(
        raw, raw, turned_q, turned_kv, grad, attended, logs, cosine, sine, gains,
        segments[None, :], segments[:, None]
    )


def on_device_fast(
    hidden_in,
    out_grad,
    segment_ids,
    doc_positions,
    attn_gain,
    head_gains,
    w_query,
    w_key,
    w_value,
    w_out,
    ffn_gain,
    w_gate,
    w_up,
    w_down,
):
    low, full = jnp.bfloat16, jnp.float32
    dp, ctx = lax.axis_index("dp"), lax.axis_index("ctx")
    ctx_count = lax.axis_size("ctx")
    core, side, high = dp % 2, dp // 2 % 2, dp // 4
    width = hidden_in.shape[-1]
    rows = w_query.shape[0]
    head = head_gains.shape[0] * lax.axis_size("dp") * ctx_count // 2
    group = w_query.shape[1] // w_key.shape[1]
    kv_own = w_key.shape[1] // head // 2
    units = w_down.shape[0] * ctx_count

    tokens = hidden_in.shape[2]
    marks = jnp.stack(
        [segment_ids[:, 0], doc_positions[:, 0] // 256, doc_positions[:, 0] % 256], 1
    ).reshape(2, 1, -1)
    marks = jnp.pad(marks, ((0, 0), (0, 15), (0, width - 3 * tokens))).astype(low)
    x_sent = jnp.concatenate([hidden_in[:, 0], marks], 1)

    head_few = head_gains.shape[0]
    gains = jnp.stack([attn_gain, ffn_gain, jnp.pad(head_gains, (0, rows - head_few))])
    gains = jnp.pad(gains, ((0, rows - 3), (0, 128 - rows)))
    key_value = jnp.stack([w_key.reshape(rows, -1, 2, head), w_value.reshape(rows, -1, 2, head)], 3)
    parities = [
        jnp.concatenate(
            [
                w_query.reshape(rows, -1, 2, group * head)[:, :, which].reshape(rows, -1),
                key_value[:, :, which].reshape(rows, -1),
                gains,
            ],
            1,
        )
        for which in range(2)
    ]
    inner = parities[0].shape[1]

    tops = w_gate.shape[1] // units // 4

    def of_member(which):
        return [
            jnp.concatenate(
                [w[:, (top * 4 + which) * units : (top * 4 + which + 1) * units] for top in range(tops)],
                1,
            )
            for w in (w_gate, w_up)
        ]

    def related(zero, one, two, three):
        near, far = choose(side, zero, two), choose(side, two, zero)
        near_far, far_far = choose(side, one, three), choose(side, three, one)
        return (
            choose(core, near, near_far),
            choose(core, far, far_far),
            choose(core, near_far, near),
            choose(core, far_far, far),
        )

    members = [of_member(which) for which in range(4)]
    gate_of = related(*[member[0] for member in members])
    up_of = related(*[member[1] for member in members])
    from_core = flip(
        joined(choose(core, parities[1], parities[0]), gate_of[2], up_of[2], gate_of[3], up_of[3]),
        CORE,
    )
    block = joined(
        choose(core, parities[0], from_core[0]),
        choose(core, from_core[0], parities[1]),
        jnp.pad(w_out, ((0, 0), (0, inner - width))),
    )
    from_side = flip(joined(gate_of[1], up_of[1], from_core[3], from_core[4]), SIDE)
    blocks = [block]
    for step in range(ctx_count - 1):
        blocks.append(spin(blocks[-1]))

    def across(pair):
        return [pair, flip(pair, SIDE), flip(pair, HIGH), flip(pair, SIDE | HIGH)]

    early = across(jnp.concatenate(blocks[:2], 0))
    blocks[3], x_sent, w_down_late, *early = hold(blocks[3], x_sent, w_down, *early)
    late = across(jnp.concatenate(blocks[2:], 0))
    x_came, x_kept = spread(x_sent)
    block_ffn = unit_block(
        [side * 2 + core, side * 2 + 1 - core, 2 - side * 2 + core, 2 - side * 2 + 1 - core],
        joined(gate_of[0], up_of[0]), from_core, from_side, w_down_late,
    )
    block_ffn, out_late, *came = hold(block_ffn, out_grad, *x_came, *late)
    x_came, late = came[:2], came[2:]
    ffn_blocks, ffn_far = [block_ffn, spin(block_ffn)], [flip(block_ffn, HIGH)]
    df_came, df_kept = spread(out_late[:, 0])
    x_half = order(ctx // 2, *settled(x_came, x_kept))
    x_other = flip(x_half, CORE)
    pieces = [
        pair[3 * part : 3 * part + 3] for pairs in (early, late) for part in range(2) for pair in pairs
    ]

    slots = []
    for step in range(ctx_count):
        place = (ctx - step) % ctx_count
        for far in range(4):
            up = 1 - high if far >= 2 else high
            across_to = 1 - side if far % 2 == 1 else side
            chip = up * 2 + across_to
            slots += [(chip * 2 + c) * ctx_count + place for c in range(2)]
            slots += [chip * ctx_count + place]
    w_in, w_mine = placed(pieces, (0, 0, 1), slots, (8 * ctx_count, 4 * ctx_count))
    w_in, w_mine = w_in.reshape(-1, inner), w_mine.reshape(-1, inner)[:, :width]
    w_in, w_mine, x_other = hold(w_in, w_mine, x_other)
    w_theirs = flip(w_mine, CORE)
    features = inner - 128
    gains_all = w_in[:, features:].reshape(-1, rows, 128)[:, :3, :rows].astype(full)
    w_in = w_in[:, :features]
    attn_gain_all, ffn_gain_all = gains_all[:, 0].reshape(-1), gains_all[:, 1].reshape(-1)
    head_gains_all = gains_all[:, 2, :head_few].reshape(2, head, 1)

    x_all = order(core, x_half, x_other)
    marks = x_all[:, :, tokens, : 3 * tokens].reshape(-1, 3, tokens)
    x_all, x_half = x_all[:, :, :tokens].reshape(-1, width), x_half[:, :tokens].reshape(-1, width)
    segments = marks[:, 0].reshape(-1).astype(jnp.int32)
    places = (256.0 * marks[:, 1].astype(full) + marks[:, 2].astype(full)).reshape(-1)
    normed, _, _ = norm_forward(x_all.astype(full), attn_gain_all)
    a_low = normed.astype(low)
    raw = lax.dot_general(w_in, a_low, (((0,), (1,)), ((), ())), preferred_element_type=full)
    raw, ffn_blocks[1], ffn_far[0], w_theirs, *df_came = hold(
        raw, ffn_blocks[1], ffn_far[0], w_theirs, *df_came
    )
    ffn_blocks.append(spin(ffn_blocks[1]))
    ffn_far.append(flip(ffn_blocks[1], HIGH))
    df = order(ctx // 2, *settled(df_came, df_kept)).reshape(-1, width)
    df_side, df_core = flip(df, SIDE), flip(df, CORE)
    freq = THETA ** (-(jnp.arange(head // 2, dtype=full) * 2.0 / head))
    turn = freq[:, None] * places[None, :]
    cosine, sine = jnp.cos(turn), jnp.sin(turn)
    attended, logs, turned_q, turned_kv = attend(
        raw, cosine, sine, head_gains_all, segments, kv_own, head, 256
    )
    attended_low = attended.astype(low)
    o_theirs = flip(half_of(1 - core, attended_low, 1), CORE)
    o_theirs, ffn_blocks[2], ffn_far[1] = hold(o_theirs, ffn_blocks[2], ffn_far[1])
    ffn_blocks.append(spin(ffn_blocks[2]))
    ffn_far.append(flip(ffn_blocks[2], HIGH))
    hidden = (
        x_half.astype(full)
        + left_trans(half_of(core, attended_low, 1), w_mine)
        + left_trans(o_theirs, w_theirs)
    )
    normed_two, h_unit, h_factor = norm_forward(hidden, ffn_gain_all)
    b_own = swap_halves(high, normed_two.astype(low), 1)
    b_own, df_side, df_core, ffn_blocks[3], ffn_far[2] = hold(
        b_own, df_side, df_core, ffn_blocks[3], ffn_far[2]
    )
    ffn_far.append(flip(ffn_blocks[3], HIGH))
    b_side, b_core, df_both = flip(b_own, SIDE), flip(b_own, CORE), flip(df_side, CORE)
    b_side, b_core, df_both, ffn_far[3] = hold(b_side, b_core, df_both, ffn_far[3])
    b_both = flip(b_side, CORE)

    units_of = functools.partial(
        feed_forward,
        [(ctx - step) % ctx_count for step in range(ctx_count)] + [high],
        [block for pair in zip(ffn_blocks, ffn_far) for block in pair],
        rows,
    )
    *left, db_side, db_both, out_side, out_both = units_of(
        [b_side, b_both], [df_side, df_both], 256, 2, []
    )
    got_both, got_out_both = flip(db_both, CORE), flip(out_both, CORE)
    db_far = total_low(db_side, got_both)
    block_side = total_low(out_side, got_out_both)
    to_side, b_own, b_core = hold(joined(db_far, block_side), b_own, b_core)
    from_other = flip(to_side, SIDE)
    act, d_pre, team_b, team_df, db_own, db_core, out_own, out_core = units_of(
        [b_own, b_core], [df, df_core], 256, 0, left
    )
    db_core, d_pre, act = hold(db_core, d_pre, act)
    got_core, got_out_core = flip(db_core, CORE), flip(out_core, CORE)

    def behind(step):
        return (ctx - 1 - step) % ctx_count

    g_down = left_trans(act, team_df).astype(low)
    g_down, team_b, from_other, got_core, got_out_core = hold(
        g_down, team_b, from_other, got_core, got_out_core
    )
    got_side, got_block = from_other[0], from_other[1]
    block_out = hidden + out_own.astype(full) + got_out_core.astype(full) + got_block.astype(full)
    block_came, block_kept = unspread(block_out.astype(low).reshape(2, -1, width))

    db = db_own.astype(full) + got_core.astype(full) + got_side.astype(full)
    db = swap_halves(high, db, 1)
    d_hidden, ffn_terms = norm_backward(db, h_unit, h_factor, ffn_gain_all)
    d_hidden = df.astype(full) + d_hidden
    dz = d_hidden.astype(low)
    dz, team_b = hold(dz, team_b)
    dz_other = flip(dz, CORE)
    g_ffn = left_trans(team_b, d_pre).astype(low)
    terms = spread_units(
        [behind(step) for step in range(ctx_count)] + [high], g_ffn, g_down, rows, ctx_count
    )
    *terms, dz_other = hold(*terms, dz_other)
    near_terms = terms[:ctx_count]
    far_got = [flip(term, HIGH) for term in terms[ctx_count:]]
    dz_all = order(core, dz, dz_other).reshape(-1, width)
    d_attended = right_trans(w_mine, dz_all).astype(low)
    g_out = matmul(attended_low, dz_all).astype(low).reshape(2, 2, ctx_count, -1, width)

    def side_square(array):
        near = jnp.where(side == 0, array[:, 0], array[:, 1])
        far = jnp.where(side == 0, array[:, 1], array[:, 0])
        near = joined(pick(near, high), pick(near, 1 - high))
        return near, flip(joined(pick(far, high), pick(far, 1 - high)), SIDE)

    def high_square(near, got):
        sums = near.astype(full) + got.astype(full)
        return sums[0], flip(sums[1].astype(low), HIGH)

    def total(terms):
        return functools.reduce(lambda a, b: a + b, [term.astype(full) for term in terms])

    back = functools.partial(
        attend_back, raw, turned_q, turned_kv, attended=attended, logs=logs, cosine=cosine,
        sine=sine, gains=head_gains_all, segments=segments, kv_own=kv_own, head=head, block=256
    )
    g_out = jnp.stack([pick(g_out, behind(step), 2) for step in range(ctx_count)], 2)
    g_out, d_attended = hold(g_out, d_attended)
    out_near, out_got = side_square(g_out)
    dq_one, dkv_one, g_heads_one = back(grad=d_attended, begin=0, count=kv_own // 2)
    dq_one, out_got, far_got[0], d_attended, *block_came = hold(
        dq_one, out_got, far_got[0], d_attended, *block_came
    )
    unit_total = total_low(near_terms[0], far_got[0])
    out_near, out_got = high_square(out_near, out_got)
    d_attended, unit_total = hold(d_attended, unit_total)
    unit_ring = spin(unit_total)
    dq_two, dkv_two, g_heads_two = back(
        grad=d_attended, begin=kv_own // 2, count=kv_own - kv_own // 2
    )
    g_heads = g_heads_one + g_heads_two
    dq_two, unit_ring, far_got[1] = hold(dq_two, unit_ring, far_got[1])
    unit_total = total_low(unit_ring, total_low(near_terms[1], far_got[1]))
    dq_two, unit_total = hold(dq_two, unit_total)
    unit_ring = spin(unit_total)
    d_raw = jnp.concatenate([dq_one, dq_two, dkv_one, dkv_two], 1)
    d_theirs = right_trans(half_of(1 - core, d_raw, 0), w_in).astype(low)
    d_theirs, d_raw = hold(d_theirs, d_raw)
    d_from = flip(d_theirs, CORE)
    d_inner = right_trans(half_of(core, d_raw, 0), w_in)
    d_inner, d_raw = hold(d_inner, d_raw)
    g_in = left_trans(a_low, d_raw).astype(low).reshape(2, 2, 2, ctx_count, rows, features)
    g_in, d_inner, d_from = hold(g_in, d_inner, d_from)
    d_inner = d_inner + d_from.astype(full)
    _, x_unit, x_factor = norm_forward(x_half.astype(full), attn_gain_all)
    d_input, attn_terms = norm_backward(d_inner, x_unit, x_factor, attn_gain_all)
    in_grad = (d_hidden + d_input).astype(low)

    g_gains = jnp.concatenate(
        [
            jnp.sum(attn_terms, 0).reshape(2, 2, 2, ctx_count, rows),
            jnp.sum(ffn_terms, 0).reshape(2, 2, 2, ctx_count, rows),
            g_heads.reshape(2, 2, 2, ctx_count, head_few),
        ],
        -1,
    ).astype(low)
    blank = ((0, 0), (0, 0), (0, 0), (0, 14), (0, width - g_gains.shape[-1]))
    g_gains = jnp.pad(jnp.moveaxis(g_gains, 2, 3), blank)
    g_in = jnp.moveaxis(g_in, 3, 2).reshape(2, 2, ctx_count, 2 * rows, features)
    g_in = jnp.concatenate([g_in, g_gains], 3)
    g_in = jnp.stack([pick(g_in, behind(step), 2) for step in range(ctx_count)], 2)
    g_in, in_grad = hold(g_in, in_grad)
    early_near, early_got = side_square(g_in[:, :, :2])
    late_near, late_got = side_square(g_in[:, :, 2:])
    in_came, in_kept = unspread(in_grad.reshape(2, -1, width))
    early_got, unit_ring, far_got[2], out_got = hold(early_got, unit_ring, far_got[2], out_got)
    out_total = out_near + out_got.astype(full)
    unit_total = total_low(unit_ring, total_low(near_terms[2], far_got[2]))
    unit_ring = spin(unit_total)
    early_near, early_got = high_square(early_near, early_got)
    early_got, late_got = hold(early_got, late_got)
    late_near, late_got = high_square(late_near, late_got)

    def terms_of(near, got, first):
        terms = near + got.astype(full)
        return [jnp.concatenate([terms[at], out_total[first + at]], 0) for at in range(2)]

    in_terms = terms_of(early_near, early_got, 0)
    in_ring = spin(in_terms[0].astype(low))
    in_ring, late_got = hold(in_ring, late_got)
    in_terms += terms_of(late_near, late_got, 2)
    in_ring = spin((in_ring.astype(full) + in_terms[1]).astype(low))
    in_ring, unit_ring, far_got[3] = hold(in_ring, unit_ring, far_got[3])
    in_ring = spin((in_ring.astype(full) + in_terms[2]).astype(low))
    unit_total = total_low(unit_ring, total_low(near_terms[3], far_got[3]))
    ffn_total = jnp.concatenate(
        [unit_total[: 4 * rows], unit_total[4 * rows : 8 * rows]], 1
    ).reshape(2, 2, rows, -1)
    g_down = unit_total[8 * rows :, :width]

    found = [
        pick(pick(ffn_total, side), core),
        flip(pick(pick(ffn_total, side), 1 - core), CORE),
        flip(pick(pick(ffn_total, 1 - side), core), SIDE),
        flip(pick(pick(ffn_total, 1 - side), 1 - core), SIDE | CORE),
    ]
    in_ring, *found = hold(in_ring, *found)
    found = related(*found)
    found = (found[0], found[2], found[1], found[3])

    def to_columns(first):
        return jnp.concatenate(
            [
                found[which][:, (first + top) * units : (first + top + 1) * units].astype(full)
                for top in range(tops)
                for which in range(4)
            ],
            1,
        )

    g_gate, g_up = to_columns(0), to_columns(tops)

    in_sum = in_ring.astype(full) + in_terms[3]
    g_in, g_out = in_sum[: 2 * rows].astype(low).reshape(2, rows, width), in_sum[2 * rows + 16 :]
    g_gains = in_sum[2 * rows : 2 * rows + 16]
    g_in, *rest = hold(g_in, *in_came, *block_came)
    in_came, block_came = rest[:2], rest[2:]
    in_grad = order(ctx % 2, *settled(in_came, in_kept))
    block_out = order(ctx % 2, *settled(block_came, block_kept))
    own = pick(g_in, core).astype(full)
    got = flip(jnp.concatenate([pick(g_in, 1 - core), g_gains.astype(low)], 0), CORE).astype(full)
    g_gains = pick(g_gains[:2] + got[rows : rows + 2], core)
    got = got[:rows]
    even, odd = choose(core, own, got), choose(core, got, own)
    first = group * head * kv_own

    def mixed(start, stop, step, size):
        return jnp.concatenate(
            [part[:, at : at + size] for at in range(start, stop, step) for part in (even, odd)], 1
        )

    return (
        block_out[:, None],
        in_grad[:, None],
        g_gains[:rows],
        g_gains[2 * rows : 2 * rows + head_few],
        mixed(0, first, group * head, group * head),
        mixed(first, features, 2 * head, head),
        mixed(first + head, features, 2 * head, head),
        g_out,
        g_gains[rows : 2 * rows],
        g_gate,
        g_up,
        g_down.astype(full),
    )


def solution(mesh):
    placed = (
        P(None, "dp", "ctx", None),
        P(None, "dp", "ctx", None),
        P(None, "dp", "ctx"),
        P(None, "dp", "ctx"),
        P(("dp", "ctx")),
        P(("dp", "ctx")),
        P(("dp", "ctx"), None),
        P(("dp", "ctx"), None),
        P(("dp", "ctx"), None),
        P(("dp", "ctx"), None),
        P(("dp", "ctx")),
        P(("dp", "ctx"), None),
        P(("dp", "ctx"), None),
        P(("dp", "ctx"), None),
    )
    fits = mesh.shape["dp"] == 8 and mesh.shape["ctx"] == 4
    return jax.shard_map(
        on_device_fast if fits else on_device,
        mesh=mesh,
        in_specs=placed,
        out_specs=(
            P(None, "dp", "ctx", None),
            P(None, "dp", "ctx", None),
            P(("dp", "ctx")),
            P(("dp", "ctx")),
            P(("dp", "ctx"), None),
            P(("dp", "ctx"), None),
            P(("dp", "ctx"), None),
            P(("dp", "ctx"), None),
            P(("dp", "ctx")),
            P(("dp", "ctx"), None),
            P(("dp", "ctx"), None),
            P(("dp", "ctx"), None),
        ),
        check_vma=False,
    )
```

```python
import functools

import jax
import jax.numpy as jnp
from jax import lax
from jax.experimental import pallas as pl
from jax.experimental.pallas import tpu as pltpu
from jax.sharding import PartitionSpec as P

EPS = 1e-05
THETA = 1000000.0


def matmul(left, right):
    return jnp.dot(left, right, preferred_element_type=jnp.float32)


def left_trans(left, right):
    return lax.dot_general(
        left, right, (((0,), (0,)), ((), ())), preferred_element_type=jnp.float32
    )


def right_trans(left, right):
    return lax.dot_general(
        left, right, (((1,), (1,)), ((), ())), preferred_element_type=jnp.float32
    )


def norm_forward(values, gain):
    factor = lax.rsqrt(jnp.mean(values * values, -1, keepdims=True) + EPS)
    unit = values * factor
    return (unit * gain, unit, factor)


def norm_backward(incoming, unit, factor, gain):
    scaled = incoming * gain
    result = factor * (scaled - unit * jnp.mean(scaled * unit, -1, keepdims=True))
    return (result, incoming * unit)


def angles(places, half):
    freq = THETA ** (-(jnp.arange(half, dtype=jnp.float32) * 2.0 / (2 * half)))
    turn = places.astype(jnp.float32)[:, None] * freq[None, :]
    return (jnp.cos(turn)[:, None, :], jnp.sin(turn)[:, None, :])


def rotate(values, cosine, sine, sign):
    half = values.shape[-1] // 2
    first = values[..., :half]
    second = values[..., half:]
    return jnp.concatenate(
        [first * cosine - sign * second * sine, second * cosine + sign * first * sine], -1
    )


def fetch_weights(shards):
    return (
        lax.all_gather(shards[0], ("dp", "ctx"), axis=0, tiled=True),
        lax.all_gather(shards[1], ("dp", "ctx"), axis=0, tiled=True),
        lax.all_gather(shards[2], ("dp", "ctx"), axis=0, tiled=True),
        lax.all_gather(shards[3], ("dp", "ctx"), axis=0, tiled=True),
        lax.all_gather(shards[4], ("dp", "ctx"), axis=0, tiled=True),
        lax.all_gather(shards[5], ("dp", "ctx"), axis=0, tiled=True),
        lax.all_gather(shards[6], ("dp", "ctx"), axis=0, tiled=True),
        lax.all_gather(shards[7], ("dp", "ctx"), axis=0, tiled=True),
        lax.all_gather(shards[8], ("dp", "ctx"), axis=0, tiled=True),
        lax.all_gather(shards[9], ("dp", "ctx"), axis=0, tiled=True),
    )


def fetch_again(shards):
    return (
        lax.all_gather(shards[0], ("dp", "ctx"), axis=0, tiled=True),
        lax.all_gather(shards[1], ("dp", "ctx"), axis=0, tiled=True),
        lax.all_gather(shards[2], ("dp", "ctx"), axis=0, tiled=True),
        lax.all_gather(shards[3], ("dp", "ctx"), axis=0, tiled=True),
        lax.all_gather(shards[4], ("dp", "ctx"), axis=0, tiled=True),
        lax.all_gather(shards[5], ("dp", "ctx"), axis=0, tiled=True),
        lax.all_gather(shards[6], ("dp", "ctx"), axis=0, tiled=True),
        lax.all_gather(shards[7], ("dp", "ctx"), axis=0, tiled=True),
        lax.all_gather(shards[8], ("dp", "ctx"), axis=0, tiled=True),
        lax.all_gather(shards[9], ("dp", "ctx"), axis=0, tiled=True),
    )


def attention_forward(query_low, key_low, value_low, segments, again):
    rows, heads, head = query_low.shape
    kv_heads = key_low.shape[1] // head
    group = heads // kv_heads
    scale = head ** (-0.5)
    grouped = query_low.reshape(rows, kv_heads, group, head)
    query_index = lax.axis_index("ctx") * rows + jnp.arange(rows, dtype=jnp.int32)

    def visit(carry, piece):
        highest, total, summed = carry
        key_piece, value_piece, segment_piece = piece
        width = key_piece.shape[0]
        key_heads = key_piece.reshape(width, kv_heads, head)
        value_heads = value_piece.reshape(width, kv_heads, head)
        scores = (
            jnp.einsum("qkgd,skd->kgqs", grouped, key_heads, preferred_element_type=jnp.float32)
            * scale
        )
        key_index = jnp.arange(width, dtype=jnp.int32)
        allowed = (segments[:, None] == segment_piece[None, :]) & (
            query_index[:, None] >= key_index[None, :]
        )
        scores = jnp.where(allowed, scores, -1e30)
        peak = jnp.maximum(highest, jnp.max(scores, -1))
        weight = jnp.where(allowed, jnp.exp(scores - peak[..., None]), 0.0)
        total = jnp.sum(weight, -1)
        summed = jnp.einsum(
            "kgqs,skd->qkgd",
            weight.astype(jnp.bfloat16),
            value_heads,
            preferred_element_type=jnp.float32,
        )
        return (peak, total, summed)

    initial = (
        jnp.full((kv_heads, group, rows), -1e30, jnp.float32),
        jnp.zeros((kv_heads, group, rows), jnp.float32),
        jnp.zeros((rows, kv_heads, group, head), jnp.float32),
    )
    if again:
        highest, total, summed = visit(
            initial,
            (
                lax.all_gather(key_low, "ctx", axis=0, tiled=True),
                lax.all_gather(value_low, "ctx", axis=0, tiled=True),
                lax.all_gather(segments, "ctx", axis=0, tiled=True),
            ),
        )
    else:
        highest, total, summed = visit(
            initial,
            (
                lax.all_gather(key_low, "ctx", axis=0, tiled=True),
                lax.all_gather(value_low, "ctx", axis=0, tiled=True),
                lax.all_gather(segments, "ctx", axis=0, tiled=True),
            ),
        )
    attended = (summed / jnp.transpose(total, (2, 0, 1))[..., None]).reshape(rows, heads, head)
    return (attended, highest + jnp.log(total))


def forward(values_row, segments, places, weights, again):
    attn_gain, head_gains, w_query, w_key, w_value, w_out, ffn_gain, w_gate, w_up, w_down = weights
    rows = values_row.shape[0]
    head = head_gains.shape[0] // 2
    heads = w_query.shape[1] // head
    kv_heads = w_key.shape[1] // head
    gains = head_gains.astype(jnp.float32)
    state = {}
    state["values"] = values_row.astype(jnp.float32)
    normed, state["x_unit"], state["x_factor"] = norm_forward(
        state["values"], attn_gain.astype(jnp.float32)
    )
    state["a_low"] = normed.astype(jnp.bfloat16)
    query = matmul(state["a_low"], w_query).reshape(rows, heads, head)
    keys = matmul(state["a_low"], w_key).reshape(rows, kv_heads, head)
    state["value_low"] = matmul(state["a_low"], w_value).astype(jnp.bfloat16)
    state["cosine"], state["sine"] = angles(places, head // 2)
    query_normed, state["q_unit"], state["q_factor"] = norm_forward(query, gains[:head])
    key_normed, state["k_unit"], state["k_factor"] = norm_forward(keys, gains[head:])
    state["query_low"] = rotate(query_normed, state["cosine"], state["sine"], 1.0).astype(
        jnp.bfloat16
    )
    state["key_low"] = (
        rotate(key_normed, state["cosine"], state["sine"], 1.0)
        .astype(jnp.bfloat16)
        .reshape(rows, kv_heads * head)
    )
    state["attended"], state["log_total"] = attention_forward(
        state["query_low"], state["key_low"], state["value_low"], segments, again
    )
    state["attended_low"] = state["attended"].astype(jnp.bfloat16).reshape(rows, heads * head)
    hidden = state["values"] + matmul(state["attended_low"], w_out)
    normed_two, state["h_unit"], state["h_factor"] = norm_forward(
        hidden, ffn_gain.astype(jnp.float32)
    )
    state["b_low"] = normed_two.astype(jnp.bfloat16)
    state["gate"] = matmul(state["b_low"], w_gate)
    state["upper"] = matmul(state["b_low"], w_up)
    state["act_low"] = (jax.nn.silu(state["gate"]) * state["upper"]).astype(jnp.bfloat16)
    state["output"] = hidden + matmul(state["act_low"], w_down)
    return state


def backward(grad_row, segments, weights, state):
    attn_gain, head_gains, w_query, w_key, w_value, w_out, ffn_gain, w_gate, w_up, w_down = weights
    query_low = state["query_low"]
    rows, heads, head = query_low.shape
    kv_heads = state["key_low"].shape[1] // head
    group = heads // kv_heads
    scale = head ** (-0.5)
    gains = head_gains.astype(jnp.float32)
    incoming = grad_row.astype(jnp.float32)
    down_low = incoming.astype(jnp.bfloat16)
    g_down = left_trans(state["act_low"], down_low)
    d_act = right_trans(down_low, w_down)
    sigma = jax.nn.sigmoid(state["gate"])
    d_upper = (d_act * state["gate"] * sigma).astype(jnp.bfloat16)
    d_gate = (d_act * state["upper"] * sigma * (1.0 + state["gate"] * (1.0 - sigma))).astype(
        jnp.bfloat16
    )
    g_gate = left_trans(state["b_low"], d_gate)
    g_up = left_trans(state["b_low"], d_upper)
    d_normed = right_trans(d_gate, w_gate) + right_trans(d_upper, w_up)
    d_hidden, terms = norm_backward(
        d_normed, state["h_unit"], state["h_factor"], ffn_gain.astype(jnp.float32)
    )
    g_ffn = jnp.sum(terms, 0)
    d_hidden = incoming + d_hidden
    branch_low = d_hidden.astype(jnp.bfloat16)
    g_out = left_trans(state["attended_low"], branch_low)
    d_attended = (
        right_trans(branch_low, w_out).astype(jnp.bfloat16).reshape(rows, kv_heads, group, head)
    )
    delta = jnp.sum(
        d_attended.astype(jnp.float32) * state["attended"].reshape(rows, kv_heads, group, head), -1
    )
    delta = jnp.transpose(delta, (1, 2, 0))
    log_total = state["log_total"]
    grouped = query_low.reshape(rows, kv_heads, group, head)
    query_index = lax.axis_index("ctx") * rows + jnp.arange(rows, dtype=jnp.int32)
    key_piece = lax.all_gather(state["key_low"], "ctx", axis=0, tiled=True)
    value_piece = lax.all_gather(state["value_low"], "ctx", axis=0, tiled=True)
    segment_piece = lax.all_gather(segments, "ctx", axis=0, tiled=True)
    width = key_piece.shape[0]
    key_heads = key_piece.reshape(width, kv_heads, head)
    value_heads = value_piece.reshape(width, kv_heads, head)
    scores = (
        jnp.einsum("qkgd,skd->kgqs", grouped, key_heads, preferred_element_type=jnp.float32) * scale
    )
    key_index = jnp.arange(width, dtype=jnp.int32)
    allowed = (segments[:, None] == segment_piece[None, :]) & (
        query_index[:, None] >= key_index[None, :]
    )
    probs = jnp.where(allowed, jnp.exp(scores - log_total[..., None]), 0.0)
    d_probs = jnp.einsum(
        "qkgd,skd->kgqs", d_attended, value_heads, preferred_element_type=jnp.float32
    )
    d_scores = (probs * (d_probs - delta[..., None])).astype(jnp.bfloat16)
    d_query = (
        jnp.einsum("kgqs,skd->qkgd", d_scores, key_heads, preferred_element_type=jnp.float32)
        * scale
    )
    key_part = (
        jnp.einsum("kgqs,qkgd->skd", d_scores, grouped, preferred_element_type=jnp.float32) * scale
    )
    value_part = jnp.einsum(
        "kgqs,qkgd->skd", probs.astype(jnp.bfloat16), d_attended, preferred_element_type=jnp.float32
    )
    d_keys = key_part.reshape(width, kv_heads * head)
    d_values = value_part.reshape(width, kv_heads * head)
    d_query, d_keys_all, d_values_all = (d_query, d_keys, d_values)
    d_keys, d_values = (
        lax.psum_scatter(
            d_keys_all.astype(jnp.bfloat16), "ctx", scatter_dimension=0, tiled=True
        ).astype(jnp.float32),
        lax.psum_scatter(
            d_values_all.astype(jnp.bfloat16), "ctx", scatter_dimension=0, tiled=True
        ).astype(jnp.float32),
    )
    d_query = rotate(d_query.reshape(rows, heads, head), state["cosine"], state["sine"], -1.0)
    d_query, query_terms = norm_backward(d_query, state["q_unit"], state["q_factor"], gains[:head])
    d_keys = rotate(d_keys.reshape(rows, kv_heads, head), state["cosine"], state["sine"], -1.0)
    d_keys, key_terms = norm_backward(d_keys, state["k_unit"], state["k_factor"], gains[head:])
    g_heads = jnp.concatenate([jnp.sum(query_terms, (0, 1)), jnp.sum(key_terms, (0, 1))])
    query_grad_low = d_query.astype(jnp.bfloat16).reshape(rows, heads * head)
    key_grad_low = d_keys.astype(jnp.bfloat16).reshape(rows, kv_heads * head)
    value_grad_low = d_values.astype(jnp.bfloat16)
    g_query = left_trans(state["a_low"], query_grad_low)
    g_key = left_trans(state["a_low"], key_grad_low)
    g_value = left_trans(state["a_low"], value_grad_low)
    d_inner = (
        right_trans(query_grad_low, w_query)
        + right_trans(key_grad_low, w_key)
        + right_trans(value_grad_low, w_value)
    )
    d_input, terms = norm_backward(
        d_inner, state["x_unit"], state["x_factor"], attn_gain.astype(jnp.float32)
    )
    g_attn = jnp.sum(terms, 0)
    in_grad = (d_hidden + d_input).astype(jnp.bfloat16)
    return (in_grad, (g_attn, g_heads, g_query, g_key, g_value, g_out, g_ffn, g_gate, g_up, g_down))


def on_device(
    hidden_in,
    out_grad,
    segment_ids,
    doc_positions,
    attn_gain,
    head_gains,
    w_query,
    w_key,
    w_value,
    w_out,
    ffn_gain,
    w_gate,
    w_up,
    w_down,
):
    shards = (attn_gain, head_gains, w_query, w_key, w_value, w_out, ffn_gain, w_gate, w_up, w_down)
    micro = hidden_in.shape[0]
    outputs = []
    for micro_index in range(micro):
        weights = fetch_weights(shards)
        state = forward(
            hidden_in[micro_index, 0],
            segment_ids[micro_index, 0],
            doc_positions[micro_index, 0],
            weights,
            False,
        )
        outputs.append(state["output"].astype(jnp.bfloat16))
    in_grads = []
    totals = None
    for micro_index in range(micro):
        weights = fetch_again(shards)
        state = forward(
            hidden_in[micro_index, 0],
            segment_ids[micro_index, 0],
            doc_positions[micro_index, 0],
            weights,
            True,
        )
        in_grad, grads = backward(
            out_grad[micro_index, 0], segment_ids[micro_index, 0], weights, state
        )
        in_grads.append(in_grad)
        if totals is None:
            totals = grads
        else:
            totals = tuple((left + right for left, right in zip(totals, grads)))
    totals = lax.psum_scatter(totals, ("dp", "ctx"), scatter_dimension=0, tiled=True)
    block_out = jnp.stack(outputs)[:, None]
    input_grads = jnp.stack(in_grads)[:, None]
    return (
        block_out,
        input_grads,
        totals[0],
        totals[1],
        totals[2],
        totals[3],
        totals[4],
        totals[5],
        totals[6],
        totals[7],
        totals[8],
        totals[9],
    )


CORE, SIDE, HIGH = 1, 2, 4


def flip(array, bits):
    count = lax.axis_size("dp")
    return lax.ppermute(array, "dp", [(i, i ^ bits) for i in range(count)])


def spin(array):
    count = lax.axis_size("ctx")
    return lax.ppermute(array, "ctx", [(i, (i + 1) % count) for i in range(count)])


def hold(*arrays):
    return lax.optimization_barrier(arrays)


def choose(bit, zero, one):
    return jnp.where(bit == 0, zero, one)


def pick(array, index, axis=0):
    return lax.dynamic_index_in_dim(array, index, axis, keepdims=False)


def put(buffer, array, *place):
    index = place + (0,) * (buffer.ndim - len(place))
    shape = (1,) * (buffer.ndim - array.ndim) + array.shape
    return lax.dynamic_update_slice(buffer, array.reshape(shape), index)


def place_kernel(splits, count, slots_ref, *refs):
    pieces, outs = refs[:count], refs[count:]
    at = 0
    for piece in pieces:
        for part in range(len(splits)):
            outs[splits[part]][slots_ref[at]] = piece[part]
            at += 1


def placed(pieces, splits, slots, counts):
    shape = pieces[0].shape
    return pl.pallas_call(
        functools.partial(place_kernel, splits, len(pieces)),
        in_specs=[pl.BlockSpec(memory_space=pltpu.SMEM)]
        + [pl.BlockSpec(memory_space=pltpu.VMEM)] * len(pieces),
        out_specs=[pl.BlockSpec(memory_space=pltpu.VMEM)] * len(counts),
        out_shape=[
            jax.ShapeDtypeStruct((count,) + shape[1:], pieces[0].dtype) for count in counts
        ],
        compiler_params=pltpu.CompilerParams(vmem_limit_bytes=40 * 2**20),
    )(jnp.stack(slots).astype(jnp.int32), *pieces)


def block_kernel(slots_ref, own_ref, core_ref, side_ref, down_ref, out_ref):
    rows = own_ref.shape[1]
    for member, ref, first in ((0, own_ref, 0), (1, core_ref, 1), (2, side_ref, 0), (3, side_ref, 2)):
        for part in range(2):
            start = pl.multiple_of((part * 4 + slots_ref[member]) * rows, rows)
            out_ref[pl.ds(start, rows), :] = ref[first + part]
    out_ref[8 * rows :, : down_ref.shape[1]] = down_ref[...]
    out_ref[8 * rows :, down_ref.shape[1] :] = jnp.zeros_like(
        out_ref[8 * rows :, down_ref.shape[1] :]
    )


def unit_block(slots, own, from_core, from_side, down):
    rows, columns = own.shape[1:]
    shape = (8 * rows + down.shape[0], columns)
    return pl.pallas_call(
        block_kernel,
        in_specs=[pl.BlockSpec(memory_space=pltpu.SMEM)]
        + [pl.BlockSpec(memory_space=pltpu.VMEM)] * 4,
        out_specs=pl.BlockSpec(memory_space=pltpu.VMEM),
        out_shape=jax.ShapeDtypeStruct(shape, own.dtype),
    )(jnp.stack(slots).astype(jnp.int32), own, from_core, from_side, down)


def unit_kernel(chunk, ctx_count, tiles, rows, slots_ref, *refs):
    pieces, refs = refs[: 2 * ctx_count], refs[2 * ctx_count :]
    b_refs, df_refs = refs[:2], refs[2:4]
    act_ref, pre_ref, all_b_ref, all_df_ref = refs[-12:-8]
    db_refs, out_refs, (w_ref, down_ref, b_ref, df_ref) = refs[-8:-6], refs[-6:-4], refs[-4:]
    mid = pieces[0].shape[1]
    width = down_ref.shape[1]
    down_rows = pieces[0].shape[0] - 8 * rows
    tile = pl.program_id(0)

    @pl.when(tile == 0)
    def _():
        high = slots_ref[ctx_count]
        for step in range(ctx_count):
            place = slots_ref[step]
            for far in range(2):
                piece = pieces[2 * step + far]
                for member in range(4):
                    first = ((far * 4 + member) * ctx_count + place) * rows
                    to = pl.ds(pl.multiple_of(first, rows), rows)
                    w_ref[to, :mid] = piece[member * rows : (member + 1) * rows, :]
                    w_ref[to, mid:] = piece[(4 + member) * rows : (5 + member) * rows, :]
                half = high if far == 0 else 1 - high
                first = (half * ctx_count + place) * down_rows
                to = pl.ds(pl.multiple_of(first, 16), down_rows)
                down_ref[to, :] = piece[8 * rows :, :width]

    for which in range(2):

        @pl.when(tile // tiles == which)
        def _(which=which):
            b_ref[...] = b_refs[which][...]
            df_ref[...] = df_refs[which][...]

    b, df = b_ref[...], df_ref[...]
    all_b_ref[...] = b
    all_df_ref[...] = df
    db, out = 0.0, 0.0
    for first, last in ((0, chunk), (chunk, mid)):
        here, there = slice(first, last), slice(mid + first, mid + last)
        gate = jnp.dot(b, w_ref[:, here], preferred_element_type=jnp.float32)
        upper = jnp.dot(b, w_ref[:, there], preferred_element_type=jnp.float32)
        d_act = nt(df, down_ref[here, :])
        sigma = 1.0 / (1.0 + jnp.exp(-gate))
        silu = gate * sigma
        act = (silu * upper).astype(jnp.bfloat16)
        d_upper = (d_act * silu).astype(jnp.bfloat16)
        d_gate = (d_act * upper * sigma * (1.0 + gate * (1.0 - sigma))).astype(jnp.bfloat16)
        act_ref[:, here] = act
        pre_ref[:, here] = d_gate
        pre_ref[:, there] = d_upper
        db += nt(d_gate, w_ref[:, here]) + nt(d_upper, w_ref[:, there])
        out += jnp.dot(act, down_ref[here, :], preferred_element_type=jnp.float32)
    for which in range(2):

        @pl.when(tile // tiles == which)
        def _(which=which):
            db_refs[which][...] = db.astype(jnp.bfloat16)
            out_refs[which][...] = out.astype(jnp.bfloat16)


def feed_forward(slots, pieces, rows, b_parts, df_parts, size, begin, left):
    tokens, width = b_parts[0].shape
    mid = pieces[0].shape[1]
    down_rows = pieces[0].shape[0] - 8 * rows
    tiles = tokens // size
    once = lambda array: pl.BlockSpec(
        array.shape, lambda t: (0,) * array.ndim, pipeline_mode=pl.Buffered(1)
    )

    def part(which):
        return pl.BlockSpec((size, width), lambda t: (jnp.clip(t - which * tiles, 0, tiles - 1), 0))

    def tiled(count, first):
        return pl.BlockSpec((size, count), lambda t: (first + t, 0))

    first = begin * tiles
    first_left = 1 + len(pieces) + 4
    full = lambda count: jax.ShapeDtypeStruct((4 * tokens, count), jnp.bfloat16)
    half = jax.ShapeDtypeStruct((tokens, width), jnp.bfloat16)
    return pl.pallas_call(
        functools.partial(unit_kernel, mid // 512 * 256, len(pieces) // 2, tiles, rows),
        grid=(2 * tiles,),
        in_specs=[pl.BlockSpec(memory_space=pltpu.SMEM)]
        + [once(array) for array in pieces]
        + [part(which) for which in range(2)] * 2
        + [pl.BlockSpec(memory_space=pl.ANY)] * len(left),
        out_specs=[tiled(mid, first), tiled(2 * mid, first), tiled(width, first), tiled(width, first)]
        + [part(which) for which in range(2)] * 2,
        out_shape=[full(mid), full(2 * mid), full(width), full(width)] + [half] * 4,
        input_output_aliases={first_left + at: at for at in range(len(left))},
        scratch_shapes=[
            pltpu.VMEM((width, 2 * mid), jnp.bfloat16),
            pltpu.VMEM((len(pieces) * down_rows, width), jnp.bfloat16),
            pltpu.VMEM((size, width), jnp.bfloat16),
            pltpu.VMEM((size, width), jnp.bfloat16),
        ],
        compiler_params=pltpu.CompilerParams(vmem_limit_bytes=58 * 2**20),
        cost_estimate=pl.CostEstimate(flops=10 * tokens * mid * width, bytes_accessed=0, transcendentals=0),
    )(jnp.stack(slots).astype(jnp.int32), *pieces, *b_parts, *df_parts, *left)


def spread_kernel(ctx_count, rows, slots_ref, ffn_ref, down_ref, *outs):
    mid = ffn_ref.shape[1] // 2
    width = down_ref.shape[1]
    down_rows = down_ref.shape[0] // (2 * ctx_count)
    high = slots_ref[ctx_count]
    for far in range(2):
        half = high if far == 0 else 1 - high
        for step in range(ctx_count):
            place = slots_ref[step]
            out = outs[far * ctx_count + step]
            for member in range(4):
                first = ((far * 4 + member) * ctx_count + place) * rows
                here = pl.ds(pl.multiple_of(first, rows), rows)
                out[member * rows : (member + 1) * rows, :] = ffn_ref[here, :mid]
                out[(4 + member) * rows : (5 + member) * rows, :] = ffn_ref[here, mid:]
            first = (half * ctx_count + place) * down_rows
            here = pl.ds(pl.multiple_of(first, 16), down_rows)
            out[8 * rows :, :width] = down_ref[here, :]
            out[8 * rows :, width:] = jnp.zeros_like(out[8 * rows :, width:])


def spread_units(slots, ffn, down, rows, ctx_count):
    shape = (8 * rows + down.shape[0] // (2 * ctx_count), ffn.shape[1] // 2)
    return pl.pallas_call(
        functools.partial(spread_kernel, ctx_count, rows),
        in_specs=[pl.BlockSpec(memory_space=pltpu.SMEM)]
        + [pl.BlockSpec(memory_space=pltpu.VMEM)] * 2,
        out_specs=[pl.BlockSpec(memory_space=pltpu.VMEM)] * (2 * ctx_count),
        out_shape=[jax.ShapeDtypeStruct(shape, ffn.dtype)] * (2 * ctx_count),
        compiler_params=pltpu.CompilerParams(vmem_limit_bytes=40 * 2**20),
        cost_estimate=pl.CostEstimate(flops=10**6, bytes_accessed=0, transcendentals=0),
    )(jnp.stack(slots).astype(jnp.int32), ffn, down)


def joined(*arrays):
    buffer = jnp.zeros((len(arrays),) + arrays[0].shape, arrays[0].dtype)
    for at, array in enumerate(arrays):
        buffer = put(buffer, array, at)
    return buffer


def order(bit, own, other):
    buffer = jnp.zeros((2,) + own.shape, own.dtype)
    return put(put(buffer, own, bit), other, 1 - bit)


def swap_halves(bit, array, axis):
    low, high = jnp.split(array, 2, axis)
    return choose(bit, array, jnp.concatenate([high, low], axis))


def half_of(bit, array, axis):
    low, high = jnp.split(array, 2, axis)
    return choose(bit, low, high)


def exchange(array, target, index_of):
    dp_count, ctx_count = lax.axis_size("dp"), lax.axis_size("ctx")
    me = lax.axis_index("dp") * ctx_count + lax.axis_index("ctx")
    came, kept = [], []
    for turn in range(2):
        pairs, stay = [], []
        for dp in range(dp_count):
            for z in range(ctx_count):
                to = target(dp, z, turn)
                if to == (dp, z):
                    stay.append(dp * ctx_count + z)
                else:
                    pairs.append((dp * ctx_count + z, to[0] * ctx_count + to[1]))
        piece = pick(array, index_of(turn))
        came.append(lax.ppermute(piece, ("dp", "ctx"), pairs))
        mine = functools.reduce(jnp.logical_or, [me == which for which in stay]) if stay else None
        kept.append((piece, mine))
    return came, kept


def settled(came, kept):
    return [
        got if mine is None else jnp.where(mine, piece, got)
        for got, (piece, mine) in zip(came, kept)
    ]


def spread(array):
    ctx = lax.axis_index("ctx")

    def target(dp, z, turn):
        return dp // 2 * 2 + z // 2, 2 * ((z + turn) % 2) + dp % 2

    return exchange(array, target, lambda turn: (ctx + turn) % 2)


def unspread(array):
    ctx = lax.axis_index("ctx")

    def target(dp, z, turn):
        return dp // 2 * 2 + z % 2, 2 * (dp % 2) + (z // 2 + turn) % 2

    return exchange(array, target, lambda turn: (ctx // 2 + turn) % 2)


def swap_gather(array, bit_value, bit):
    return order(bit_value, array, flip(array, bit))


def total_low(left, right):
    return (left.astype(jnp.float32) + right.astype(jnp.float32)).astype(jnp.bfloat16)


def nt(left, right):
    return lax.dot_general(
        left, right, (((1,), (1,)), ((), ())), preferred_element_type=jnp.float32
    )


def set_bias(bias_ref, seg_row_ref, seg_col_ref, block):
    size = bias_ref.shape[0]
    for first in range(0, size, block):
        for key in range(0, first + block, block):
            allowed = seg_col_ref[key : key + block, :] == seg_row_ref[:, first : first + block]
            if key == first:
                keys = lax.broadcasted_iota(jnp.int32, (block, block), 0)
                queries = lax.broadcasted_iota(jnp.int32, (block, block), 1)
                allowed = jnp.logical_and(allowed, keys <= queries)
            bias_ref[key : key + block, first : first + block] = jnp.where(allowed, 0.0, -1e30)


def turned(values, gain, cosine, sine):
    half = values.shape[0] // 2
    factor = lax.rsqrt(jnp.mean(values * values, 0, keepdims=True) + EPS)
    normed = values * factor * gain
    first, second = normed[:half], normed[half:]
    return jnp.concatenate([first * cosine - second * sine, second * cosine + first * sine], 0)


def turned_back(incoming, values, gain, cosine, sine):
    half = values.shape[0] // 2
    first, second = incoming[:half], incoming[half:]
    incoming = jnp.concatenate(
        [first * cosine + second * sine, second * cosine - first * sine], 0
    )
    factor = lax.rsqrt(jnp.mean(values * values, 0, keepdims=True) + EPS)
    unit = values * factor
    terms = jnp.sum(incoming * unit, 1, keepdims=True)
    scaled = incoming * gain
    return factor * (scaled - unit * jnp.mean(scaled * unit, 0, keepdims=True)), terms


def forward_kernel(
    block, q_ref, kv_ref, cos_ref, sin_ref, gain_ref, row_ref, col_ref,
    o_ref, log_ref, qr_ref, kvr_ref, bias_ref
):
    head = kv_ref.shape[0] // 2
    size = kv_ref.shape[1]
    scale = head ** (-0.5)

    @pl.when(pl.program_id(0) == 0)
    def _():
        set_bias(bias_ref, row_ref, col_ref, block)

    cosine, sine = cos_ref[...], sin_ref[...]
    keys = turned(kv_ref[:head, :], gain_ref[1], cosine, sine)
    kvr_ref[:head, :] = keys.astype(jnp.bfloat16)
    keys = keys.T.astype(jnp.bfloat16)
    values = kv_ref[head:, :].astype(jnp.bfloat16)
    kvr_ref[head:, :] = values
    for which in range(q_ref.shape[0] // head):
        rows = slice(which * head, (which + 1) * head)
        query = turned(q_ref[rows, :], gain_ref[0], cosine, sine).astype(jnp.bfloat16)
        qr_ref[rows, :] = query
        for first in range(0, size, block):
            here = slice(first, first + block)
            total = jnp.zeros((1, block), jnp.float32)
            summed = jnp.zeros((head, block), jnp.float32)
            for key in range(0, first + block, block):
                there = slice(key, key + block)
                scores = jnp.dot(keys[there], query[:, here], preferred_element_type=jnp.float32)
                weight = jnp.exp(scores * scale + bias_ref[there, here])
                total += jnp.sum(weight, 0, keepdims=True)
                summed += jnp.dot(
                    values[:, there],
                    weight.astype(jnp.bfloat16),
                    preferred_element_type=jnp.float32,
                )
            o_ref[rows, here] = summed / total
            log_ref[0, which : which + 1, here] = jnp.log(total)


def backward_kernel(
    block, q_ref, kv_ref, qr_ref, kvr_ref, do_ref, o_ref, log_ref, cos_ref, sin_ref,
    gain_ref, row_ref, col_ref, dq_ref, dkv_ref, gains_ref, bias_ref, dkey_ref, dvalue_ref
):
    head = kv_ref.shape[0] // 2
    size = kv_ref.shape[1]
    scale = head ** (-0.5)

    @pl.when(pl.program_id(0) == 0)
    def _():
        set_bias(bias_ref, row_ref, col_ref, block)
        gains_ref[...] = jnp.zeros_like(gains_ref)

    cosine, sine = cos_ref[...], sin_ref[...]
    keys_t = kvr_ref[:head, :]
    keys = keys_t.astype(jnp.float32).T.astype(jnp.bfloat16)
    values = kvr_ref[head:, :].astype(jnp.float32).T.astype(jnp.bfloat16)
    dkey_ref[...] = jnp.zeros_like(dkey_ref)
    dvalue_ref[...] = jnp.zeros_like(dvalue_ref)
    found = []
    for which in range(q_ref.shape[0] // head):
        rows = slice(which * head, (which + 1) * head)
        query = qr_ref[rows, :]
        grad = do_ref[rows, :]
        delta = jnp.sum(grad.astype(jnp.float32) * o_ref[rows, :], 0, keepdims=True)
        pieces = []
        for first in range(0, size, block):
            here = slice(first, first + block)
            dquery = jnp.zeros((head, block), jnp.float32)
            for key in range(0, first + block, block):
                there = slice(key, key + block)
                scores = jnp.dot(keys[there], query[:, here], preferred_element_type=jnp.float32)
                probs = jnp.exp(
                    scores * scale + (bias_ref[there, here] - log_ref[0, which : which + 1, here])
                )
                dprobs = jnp.dot(values[there], grad[:, here], preferred_element_type=jnp.float32)
                dscores = (probs * (dprobs - delta[:, here])).astype(jnp.bfloat16)
                dquery += jnp.dot(keys_t[:, there], dscores, preferred_element_type=jnp.float32)
                dkey_ref[:, there] += nt(query[:, here], dscores)
                dvalue_ref[:, there] += nt(grad[:, here], probs.astype(jnp.bfloat16))
            pieces.append(dquery * scale)
        dquery, terms = turned_back(
            jnp.concatenate(pieces, 1), q_ref[rows, :], gain_ref[0], cosine, sine
        )
        found.append(dquery)
        gains_ref[0] += terms
    dq_ref[...] = jnp.concatenate(found, 0).T.astype(jnp.bfloat16)
    dkey, terms = turned_back(dkey_ref[...] * scale, kv_ref[:head, :], gain_ref[1], cosine, sine)
    dkv_ref[...] = jnp.concatenate([dkey, dvalue_ref[...]], 0).T.astype(jnp.bfloat16)
    gains_ref[1] += terms


def whole_spec(*shape):
    return pl.BlockSpec(shape, lambda i: (0,) * len(shape))


def attend(raw, cosine, sine, gains, segments, kv_own, head, block):
    size = raw.shape[1]
    group = raw.shape[0] // head // kv_own - 2
    query = pl.BlockSpec((group * head, size), lambda i: (i, 0))
    kv_at = group * kv_own // 2
    return pl.pallas_call(
        functools.partial(forward_kernel, block),
        grid=(kv_own,),
        in_specs=[
            query,
            pl.BlockSpec((2 * head, size), lambda i: (kv_at + i, 0)),
            whole_spec(head // 2, size),
            whole_spec(head // 2, size),
            whole_spec(2, head, 1),
            whole_spec(1, size),
            whole_spec(size, 1),
        ],
        out_specs=[
            query,
            pl.BlockSpec((1, group, size), lambda i: (i, 0, 0)),
            query,
            pl.BlockSpec((2 * head, size), lambda i: (i, 0)),
        ],
        out_shape=[
            jax.ShapeDtypeStruct((kv_own * group * head, size), jnp.float32),
            jax.ShapeDtypeStruct((kv_own, group, size), jnp.float32),
            jax.ShapeDtypeStruct((kv_own * group * head, size), jnp.bfloat16),
            jax.ShapeDtypeStruct((kv_own * 2 * head, size), jnp.bfloat16),
        ],
        scratch_shapes=[pltpu.VMEM((size, size), jnp.float32)],
        compiler_params=pltpu.CompilerParams(vmem_limit_bytes=58 * 2**20),
        cost_estimate=pl.CostEstimate(flops=10**6, bytes_accessed=0, transcendentals=0),
    )(raw, raw, cosine, sine, gains, segments[None, :], segments[:, None])


def attend_back(
    raw, turned_q, turned_kv, grad, attended, logs, cosine, sine, gains, segments,
    kv_own, head, block, begin, count
):
    size = raw.shape[1]
    group = raw.shape[0] // head // kv_own - 2
    query = pl.BlockSpec((group * head, size), lambda i: (begin + i, 0))
    kv_at = group * kv_own // 2 + begin
    return pl.pallas_call(
        functools.partial(backward_kernel, block),
        grid=(count,),
        in_specs=[
            query,
            pl.BlockSpec((2 * head, size), lambda i: (kv_at + i, 0)),
            query,
            pl.BlockSpec((2 * head, size), lambda i: (begin + i, 0)),
            query,
            query,
            pl.BlockSpec((1, group, size), lambda i: (begin + i, 0, 0)),
            whole_spec(head // 2, size),
            whole_spec(head // 2, size),
            whole_spec(2, head, 1),
            whole_spec(1, size),
            whole_spec(size, 1),
        ],
        out_specs=[
            pl.BlockSpec((size, group * head), lambda i: (0, i)),
            pl.BlockSpec((size, 2 * head), lambda i: (0, i)),
            whole_spec(2, head, 1),
        ],
        out_shape=[
            jax.ShapeDtypeStruct((size, count * group * head), jnp.bfloat16),
            jax.ShapeDtypeStruct((size, count * 2 * head), jnp.bfloat16),
            jax.ShapeDtypeStruct((2, head, 1), jnp.float32),
        ],
        scratch_shapes=[
            pltpu.VMEM((size, size), jnp.float32),
            pltpu.VMEM((head, size), jnp.float32),
            pltpu.VMEM((head, size), jnp.float32),
        ],
        compiler_params=pltpu.CompilerParams(vmem_limit_bytes=58 * 2**20),
        cost_estimate=pl.CostEstimate(flops=10**6, bytes_accessed=0, transcendentals=0),
    )(
        raw, raw, turned_q, turned_kv, grad, attended, logs, cosine, sine, gains,
        segments[None, :], segments[:, None]
    )


def on_device_fast(
    hidden_in,
    out_grad,
    segment_ids,
    doc_positions,
    attn_gain,
    head_gains,
    w_query,
    w_key,
    w_value,
    w_out,
    ffn_gain,
    w_gate,
    w_up,
    w_down,
):
    low, full = jnp.bfloat16, jnp.float32
    dp, ctx = lax.axis_index("dp"), lax.axis_index("ctx")
    ctx_count = lax.axis_size("ctx")
    core, side, high = dp % 2, dp // 2 % 2, dp // 4
    width = hidden_in.shape[-1]
    rows = w_query.shape[0]
    head = head_gains.shape[0] * lax.axis_size("dp") * ctx_count // 2
    group = w_query.shape[1] // w_key.shape[1]
    kv_own = w_key.shape[1] // head // 2
    units = w_down.shape[0] * ctx_count

    tokens = hidden_in.shape[2]
    marks = jnp.stack(
        [segment_ids[:, 0], doc_positions[:, 0] // 256, doc_positions[:, 0] % 256], 1
    ).reshape(2, 1, -1)
    marks = jnp.pad(marks, ((0, 0), (0, 15), (0, width - 3 * tokens))).astype(low)
    x_came, x_kept = spread(jnp.concatenate([hidden_in[:, 0], marks], 1))

    head_few = head_gains.shape[0]
    gains = jnp.stack([attn_gain, ffn_gain, jnp.pad(head_gains, (0, rows - head_few))])
    gains = jnp.pad(gains, ((0, rows - 3), (0, 128 - rows)))
    key_value = jnp.stack([w_key.reshape(rows, -1, 2, head), w_value.reshape(rows, -1, 2, head)], 3)
    parities = [
        jnp.concatenate(
            [
                w_query.reshape(rows, -1, 2, group * head)[:, :, which].reshape(rows, -1),
                key_value[:, :, which].reshape(rows, -1),
                gains,
            ],
            1,
        )
        for which in range(2)
    ]
    inner = parities[0].shape[1]

    tops = w_gate.shape[1] // units // 4

    def of_member(which):
        return [
            jnp.concatenate(
                [w[:, (top * 4 + which) * units : (top * 4 + which + 1) * units] for top in range(tops)],
                1,
            )
            for w in (w_gate, w_up)
        ]

    def related(zero, one, two, three):
        near, far = choose(side, zero, two), choose(side, two, zero)
        near_far, far_far = choose(side, one, three), choose(side, three, one)
        return (
            choose(core, near, near_far),
            choose(core, far, far_far),
            choose(core, near_far, near),
            choose(core, far_far, far),
        )

    members = [of_member(which) for which in range(4)]
    gate_of = related(*[member[0] for member in members])
    up_of = related(*[member[1] for member in members])
    from_core = flip(
        joined(choose(core, parities[1], parities[0]), gate_of[2], up_of[2], gate_of[3], up_of[3]),
        CORE,
    )
    block = joined(
        choose(core, parities[0], from_core[0]),
        choose(core, from_core[0], parities[1]),
        jnp.pad(w_out, ((0, 0), (0, inner - width))),
    )
    from_side = flip(joined(gate_of[1], up_of[1], from_core[3], from_core[4]), SIDE)
    blocks = [block]
    for step in range(ctx_count - 1):
        blocks.append(spin(blocks[-1]))

    def across(pair):
        return [pair, flip(pair, SIDE), flip(pair, HIGH), flip(pair, SIDE | HIGH)]

    early = across(jnp.concatenate(blocks[:2], 0))
    blocks[3], w_down_late, *early = hold(blocks[3], w_down, *early)
    late = across(jnp.concatenate(blocks[2:], 0))
    block_ffn = unit_block(
        [side * 2 + core, side * 2 + 1 - core, 2 - side * 2 + core, 2 - side * 2 + 1 - core],
        joined(gate_of[0], up_of[0]), from_core, from_side, w_down_late,
    )
    block_ffn, *x_came = hold(block_ffn, *x_came)
    ffn_blocks = [block_ffn, spin(block_ffn)]
    x_half = order(ctx // 2, *settled(x_came, x_kept))
    x_other = flip(x_half, CORE)
    block_ffn, out_late, *late = hold(block_ffn, out_grad, *late)
    ffn_far = [flip(block_ffn, HIGH)]
    df_came, df_kept = spread(out_late[:, 0])
    pieces = [
        pair[3 * part : 3 * part + 3] for pairs in (early, late) for part in range(2) for pair in pairs
    ]

    slots = []
    for step in range(ctx_count):
        place = (ctx - step) % ctx_count
        for far in range(4):
            up = 1 - high if far >= 2 else high
            across_to = 1 - side if far % 2 == 1 else side
            chip = up * 2 + across_to
            slots += [(chip * 2 + c) * ctx_count + place for c in range(2)]
            slots += [chip * ctx_count + place]
    w_in, w_mine = placed(pieces, (0, 0, 1), slots, (8 * ctx_count, 4 * ctx_count))
    w_in, w_mine = w_in.reshape(-1, inner), w_mine.reshape(-1, inner)[:, :width]
    w_in, w_mine, x_other = hold(w_in, w_mine, x_other)
    w_theirs = flip(w_mine, CORE)
    features = inner - 128
    gains_all = w_in[:, features:].reshape(-1, rows, 128)[:, :3, :rows].astype(full)
    w_in = w_in[:, :features]
    attn_gain_all, ffn_gain_all = gains_all[:, 0].reshape(-1), gains_all[:, 1].reshape(-1)
    head_gains_all = gains_all[:, 2, :head_few].reshape(2, head, 1)

    x_all = order(core, x_half, x_other)
    marks = x_all[:, :, tokens, : 3 * tokens].reshape(-1, 3, tokens)
    x_all, x_half = x_all[:, :, :tokens].reshape(-1, width), x_half[:, :tokens].reshape(-1, width)
    segments = marks[:, 0].reshape(-1).astype(jnp.int32)
    places = (256.0 * marks[:, 1].astype(full) + marks[:, 2].astype(full)).reshape(-1)
    normed, _, _ = norm_forward(x_all.astype(full), attn_gain_all)
    a_low = normed.astype(low)
    raw = lax.dot_general(w_in, a_low, (((0,), (1,)), ((), ())), preferred_element_type=full)
    raw, ffn_blocks[1], ffn_far[0], w_theirs = hold(raw, ffn_blocks[1], ffn_far[0], w_theirs)
    ffn_blocks.append(spin(ffn_blocks[1]))
    ffn_far.append(flip(ffn_blocks[1], HIGH))
    freq = THETA ** (-(jnp.arange(head // 2, dtype=full) * 2.0 / head))
    turn = freq[:, None] * places[None, :]
    cosine, sine = jnp.cos(turn), jnp.sin(turn)
    attended, logs, turned_q, turned_kv = attend(
        raw, cosine, sine, head_gains_all, segments, kv_own, head, 256
    )
    attended_low = attended.astype(low)
    o_theirs = flip(half_of(1 - core, attended_low, 1), CORE)
    o_theirs, ffn_blocks[2], ffn_far[1], *df_came = hold(
        o_theirs, ffn_blocks[2], ffn_far[1], *df_came
    )
    df = order(ctx // 2, *settled(df_came, df_kept)).reshape(-1, width)
    df_side, df_core = flip(df, SIDE), flip(df, CORE)
    ffn_blocks.append(spin(ffn_blocks[2]))
    ffn_far.append(flip(ffn_blocks[2], HIGH))
    hidden = (
        x_half.astype(full)
        + left_trans(half_of(core, attended_low, 1), w_mine)
        + left_trans(o_theirs, w_theirs)
    )
    normed_two, h_unit, h_factor = norm_forward(hidden, ffn_gain_all)
    b_own = swap_halves(high, normed_two.astype(low), 1)
    b_own, df_core, ffn_blocks[3], ffn_far[2] = hold(b_own, df_core, ffn_blocks[3], ffn_far[2])
    b_side, b_core = flip(b_own, SIDE), flip(b_own, CORE)
    ffn_far.append(flip(ffn_blocks[3], HIGH))
    b_side, b_core, df_side, ffn_far[3] = hold(b_side, b_core, df_side, ffn_far[3])
    b_both, df_both = flip(b_side, CORE), flip(df_side, CORE)

    units_of = functools.partial(
        feed_forward,
        [(ctx - step) % ctx_count for step in range(ctx_count)] + [high],
        [block for pair in zip(ffn_blocks, ffn_far) for block in pair],
        rows,
    )
    *left, db_side, db_both, out_side, out_both = units_of(
        [b_side, b_both], [df_side, df_both], 256, 2, []
    )
    got_both, got_out_both = flip(db_both, CORE), flip(out_both, CORE)
    db_far = total_low(db_side, got_both)
    block_side = total_low(out_side, got_out_both)
    to_side, b_own, b_core = hold(joined(db_far, block_side), b_own, b_core)
    from_other = flip(to_side, SIDE)
    act, d_pre, team_b, team_df, db_own, db_core, out_own, out_core = units_of(
        [b_own, b_core], [df, df_core], 256, 0, left
    )
    db_core, d_pre, act = hold(db_core, d_pre, act)
    got_core, got_out_core = flip(db_core, CORE), flip(out_core, CORE)

    def behind(step):
        return (ctx - 1 - step) % ctx_count

    g_down = left_trans(act, team_df).astype(low)
    g_down, team_b, from_other, got_core, got_out_core = hold(
        g_down, team_b, from_other, got_core, got_out_core
    )
    got_side, got_block = from_other[0], from_other[1]
    block_out = hidden + out_own.astype(full) + got_out_core.astype(full) + got_block.astype(full)
    block_came, block_kept = unspread(block_out.astype(low).reshape(2, -1, width))

    db = db_own.astype(full) + got_core.astype(full) + got_side.astype(full)
    db = swap_halves(high, db, 1)
    d_hidden, ffn_terms = norm_backward(db, h_unit, h_factor, ffn_gain_all)
    d_hidden = df.astype(full) + d_hidden
    dz = d_hidden.astype(low)
    dz, team_b = hold(dz, team_b)
    dz_other = flip(dz, CORE)
    g_ffn = left_trans(team_b, d_pre).astype(low)
    terms = spread_units(
        [behind(step) for step in range(ctx_count)] + [high], g_ffn, g_down, rows, ctx_count
    )
    *terms, dz_other = hold(*terms, dz_other)
    near_terms = terms[:ctx_count]
    far_got = [flip(term, HIGH) for term in terms[ctx_count:-1]]
    dz_all = order(core, dz, dz_other).reshape(-1, width)
    d_attended = right_trans(w_mine, dz_all).astype(low)
    g_out = matmul(attended_low, dz_all).astype(low).reshape(2, 2, ctx_count, -1, width)

    def side_square(array):
        near = jnp.where(side == 0, array[:, 0], array[:, 1])
        far = jnp.where(side == 0, array[:, 1], array[:, 0])
        near = joined(pick(near, high), pick(near, 1 - high))
        return near, flip(joined(pick(far, high), pick(far, 1 - high)), SIDE)

    def high_square(near, got):
        sums = near.astype(full) + got.astype(full)
        return sums[0], flip(sums[1].astype(low), HIGH)

    def total(terms):
        return functools.reduce(lambda a, b: a + b, [term.astype(full) for term in terms])

    back = functools.partial(
        attend_back, raw, turned_q, turned_kv, attended=attended, logs=logs, cosine=cosine,
        sine=sine, gains=head_gains_all, segments=segments, kv_own=kv_own, head=head, block=256
    )
    g_out = jnp.stack([pick(g_out, behind(step), 2) for step in range(ctx_count)], 2)
    g_out, d_attended = hold(g_out, d_attended)
    out_near, out_got = side_square(g_out)
    dq_one, dkv_one, g_heads_one = back(grad=d_attended, begin=0, count=kv_own // 2)
    dq_one, out_got, far_got[0], d_attended, *block_came = hold(
        dq_one, out_got, far_got[0], d_attended, *block_came
    )
    unit_total = total_low(near_terms[0], far_got[0])
    out_near, out_got = high_square(out_near, out_got)
    d_attended, unit_total = hold(d_attended, unit_total)
    unit_ring = spin(unit_total)
    dq_two, dkv_two, g_heads_two = back(
        grad=d_attended, begin=kv_own // 2, count=kv_own - kv_own // 2
    )
    g_heads = g_heads_one + g_heads_two
    dq_two, unit_ring, far_got[1], out_got, last_term = hold(
        dq_two, unit_ring, far_got[1], out_got, terms[-1]
    )
    far_got.append(flip(last_term, HIGH))
    unit_total = total_low(unit_ring, total_low(near_terms[1], far_got[1]))
    dq_two, unit_total = hold(dq_two, unit_total)
    unit_ring = spin(unit_total)
    d_raw = jnp.concatenate([dq_one, dq_two, dkv_one, dkv_two], 1)
    d_theirs = right_trans(half_of(1 - core, d_raw, 0), w_in).astype(low)
    d_theirs, d_raw = hold(d_theirs, d_raw)
    d_from = flip(d_theirs, CORE)
    d_inner = right_trans(half_of(core, d_raw, 0), w_in)
    d_inner, d_raw = hold(d_inner, d_raw)
    g_in = left_trans(a_low, d_raw).astype(low).reshape(2, 2, 2, ctx_count, rows, features)
    g_in, d_inner, d_from = hold(g_in, d_inner, d_from)
    d_inner = d_inner + d_from.astype(full)
    _, x_unit, x_factor = norm_forward(x_half.astype(full), attn_gain_all)
    d_input, attn_terms = norm_backward(d_inner, x_unit, x_factor, attn_gain_all)
    in_grad = (d_hidden + d_input).astype(low)

    g_gains = jnp.concatenate(
        [
            jnp.sum(attn_terms, 0).reshape(2, 2, 2, ctx_count, rows),
            jnp.sum(ffn_terms, 0).reshape(2, 2, 2, ctx_count, rows),
            g_heads.reshape(2, 2, 2, ctx_count, head_few),
        ],
        -1,
    ).astype(low)
    blank = ((0, 0), (0, 0), (0, 0), (0, 14), (0, width - g_gains.shape[-1]))
    g_gains = jnp.pad(jnp.moveaxis(g_gains, 2, 3), blank)
    g_in = jnp.moveaxis(g_in, 3, 2).reshape(2, 2, ctx_count, 2 * rows, features)
    g_in = jnp.concatenate([g_in, g_gains], 3)
    g_in = jnp.stack([pick(g_in, behind(step), 2) for step in range(ctx_count)], 2)
    g_in, in_grad = hold(g_in, in_grad)
    early_near, early_got = side_square(g_in[:, :, :2])
    late_near, late_got = side_square(g_in[:, :, 2:])
    in_came, in_kept = unspread(in_grad.reshape(2, -1, width))
    out_total = out_near + out_got.astype(full)
    unit_total = total_low(unit_ring, total_low(near_terms[2], far_got[2]))
    unit_ring = spin(unit_total)
    early_near, early_got = high_square(early_near, early_got)
    early_got, late_got, unit_ring, far_got[3] = hold(early_got, late_got, unit_ring, far_got[3])
    unit_total = total_low(unit_ring, total_low(near_terms[3], far_got[3]))
    ffn_total = jnp.concatenate(
        [unit_total[: 4 * rows], unit_total[4 * rows : 8 * rows]], 1
    ).reshape(2, 2, rows, -1)
    g_down = unit_total[8 * rows :, :width]

    found = [
        pick(pick(ffn_total, side), core),
        flip(pick(pick(ffn_total, side), 1 - core), CORE),
        flip(pick(pick(ffn_total, 1 - side), core), SIDE),
        flip(pick(pick(ffn_total, 1 - side), 1 - core), SIDE | CORE),
    ]
    late_near, late_got = high_square(late_near, late_got)

    def terms_of(near, got, first):
        terms = near + got.astype(full)
        return [jnp.concatenate([terms[at], out_total[first + at]], 0) for at in range(2)]

    in_terms = terms_of(early_near, early_got, 0)
    in_ring = spin(in_terms[0].astype(low))
    in_ring, late_got = hold(in_ring, late_got)
    in_terms += terms_of(late_near, late_got, 2)
    in_ring = spin((in_ring.astype(full) + in_terms[1]).astype(low))
    in_ring, *found = hold(in_ring, *found)
    in_ring = spin((in_ring.astype(full) + in_terms[2]).astype(low))
    in_ring, *in_came = hold(in_ring, *in_came)
    found = related(*found)
    found = (found[0], found[2], found[1], found[3])

    def to_columns(first):
        return jnp.concatenate(
            [
                found[which][:, (first + top) * units : (first + top + 1) * units].astype(full)
                for top in range(tops)
                for which in range(4)
            ],
            1,
        )

    g_gate, g_up = to_columns(0), to_columns(tops)

    in_sum = in_ring.astype(full) + in_terms[3]
    g_in, g_out = in_sum[: 2 * rows].astype(low).reshape(2, rows, width), in_sum[2 * rows + 16 :]
    g_gains = in_sum[2 * rows : 2 * rows + 16]
    g_in, *block_came = hold(g_in, *block_came)
    in_grad = order(ctx % 2, *settled(in_came, in_kept))
    block_out = order(ctx % 2, *settled(block_came, block_kept))
    own = pick(g_in, core).astype(full)
    got = flip(jnp.concatenate([pick(g_in, 1 - core), g_gains.astype(low)], 0), CORE).astype(full)
    g_gains = pick(g_gains[:2] + got[rows : rows + 2], core)
    got = got[:rows]
    even, odd = choose(core, own, got), choose(core, got, own)
    first = group * head * kv_own

    def mixed(start, stop, step, size):
        return jnp.concatenate(
            [part[:, at : at + size] for at in range(start, stop, step) for part in (even, odd)], 1
        )

    return (
        block_out[:, None],
        in_grad[:, None],
        g_gains[:rows],
        g_gains[2 * rows : 2 * rows + head_few],
        mixed(0, first, group * head, group * head),
        mixed(first, features, 2 * head, head),
        mixed(first + head, features, 2 * head, head),
        g_out,
        g_gains[rows : 2 * rows],
        g_gate,
        g_up,
        g_down.astype(full),
    )


def solution(mesh):
    placed = (
        P(None, "dp", "ctx", None),
        P(None, "dp", "ctx", None),
        P(None, "dp", "ctx"),
        P(None, "dp", "ctx"),
        P(("dp", "ctx")),
        P(("dp", "ctx")),
        P(("dp", "ctx"), None),
        P(("dp", "ctx"), None),
        P(("dp", "ctx"), None),
        P(("dp", "ctx"), None),
        P(("dp", "ctx")),
        P(("dp", "ctx"), None),
        P(("dp", "ctx"), None),
        P(("dp", "ctx"), None),
    )
    fits = mesh.shape["dp"] == 8 and mesh.shape["ctx"] == 4
    return jax.shard_map(
        on_device_fast if fits else on_device,
        mesh=mesh,
        in_specs=placed,
        out_specs=(
            P(None, "dp", "ctx", None),
            P(None, "dp", "ctx", None),
            P(("dp", "ctx")),
            P(("dp", "ctx")),
            P(("dp", "ctx"), None),
            P(("dp", "ctx"), None),
            P(("dp", "ctx"), None),
            P(("dp", "ctx"), None),
            P(("dp", "ctx")),
            P(("dp", "ctx"), None),
            P(("dp", "ctx"), None),
            P(("dp", "ctx"), None),
        ),
        check_vma=False,
    )
```

```python
import functools

import jax
import jax.numpy as jnp
from jax import lax
from jax.experimental import pallas as pl
from jax.experimental.pallas import tpu as pltpu
from jax.sharding import PartitionSpec as P

EPS = 1e-05
THETA = 1000000.0


def matmul(left, right):
    return jnp.dot(left, right, preferred_element_type=jnp.float32)


def left_trans(left, right):
    return lax.dot_general(
        left, right, (((0,), (0,)), ((), ())), preferred_element_type=jnp.float32
    )


def right_trans(left, right):
    return lax.dot_general(
        left, right, (((1,), (1,)), ((), ())), preferred_element_type=jnp.float32
    )


def norm_forward(values, gain):
    factor = lax.rsqrt(jnp.mean(values * values, -1, keepdims=True) + EPS)
    unit = values * factor
    return (unit * gain, unit, factor)


def norm_backward(incoming, unit, factor, gain):
    scaled = incoming * gain
    result = factor * (scaled - unit * jnp.mean(scaled * unit, -1, keepdims=True))
    return (result, incoming * unit)


def angles(places, half):
    freq = THETA ** (-(jnp.arange(half, dtype=jnp.float32) * 2.0 / (2 * half)))
    turn = places.astype(jnp.float32)[:, None] * freq[None, :]
    return (jnp.cos(turn)[:, None, :], jnp.sin(turn)[:, None, :])


def rotate(values, cosine, sine, sign):
    half = values.shape[-1] // 2
    first = values[..., :half]
    second = values[..., half:]
    return jnp.concatenate(
        [first * cosine - sign * second * sine, second * cosine + sign * first * sine], -1
    )


def fetch_weights(shards):
    return (
        lax.all_gather(shards[0], ("dp", "ctx"), axis=0, tiled=True),
        lax.all_gather(shards[1], ("dp", "ctx"), axis=0, tiled=True),
        lax.all_gather(shards[2], ("dp", "ctx"), axis=0, tiled=True),
        lax.all_gather(shards[3], ("dp", "ctx"), axis=0, tiled=True),
        lax.all_gather(shards[4], ("dp", "ctx"), axis=0, tiled=True),
        lax.all_gather(shards[5], ("dp", "ctx"), axis=0, tiled=True),
        lax.all_gather(shards[6], ("dp", "ctx"), axis=0, tiled=True),
        lax.all_gather(shards[7], ("dp", "ctx"), axis=0, tiled=True),
        lax.all_gather(shards[8], ("dp", "ctx"), axis=0, tiled=True),
        lax.all_gather(shards[9], ("dp", "ctx"), axis=0, tiled=True),
    )


def fetch_again(shards):
    return (
        lax.all_gather(shards[0], ("dp", "ctx"), axis=0, tiled=True),
        lax.all_gather(shards[1], ("dp", "ctx"), axis=0, tiled=True),
        lax.all_gather(shards[2], ("dp", "ctx"), axis=0, tiled=True),
        lax.all_gather(shards[3], ("dp", "ctx"), axis=0, tiled=True),
        lax.all_gather(shards[4], ("dp", "ctx"), axis=0, tiled=True),
        lax.all_gather(shards[5], ("dp", "ctx"), axis=0, tiled=True),
        lax.all_gather(shards[6], ("dp", "ctx"), axis=0, tiled=True),
        lax.all_gather(shards[7], ("dp", "ctx"), axis=0, tiled=True),
        lax.all_gather(shards[8], ("dp", "ctx"), axis=0, tiled=True),
        lax.all_gather(shards[9], ("dp", "ctx"), axis=0, tiled=True),
    )


def attention_forward(query_low, key_low, value_low, segments, again):
    rows, heads, head = query_low.shape
    kv_heads = key_low.shape[1] // head
    group = heads // kv_heads
    scale = head ** (-0.5)
    grouped = query_low.reshape(rows, kv_heads, group, head)
    query_index = lax.axis_index("ctx") * rows + jnp.arange(rows, dtype=jnp.int32)

    def visit(carry, piece):
        highest, total, summed = carry
        key_piece, value_piece, segment_piece = piece
        width = key_piece.shape[0]
        key_heads = key_piece.reshape(width, kv_heads, head)
        value_heads = value_piece.reshape(width, kv_heads, head)
        scores = (
            jnp.einsum("qkgd,skd->kgqs", grouped, key_heads, preferred_element_type=jnp.float32)
            * scale
        )
        key_index = jnp.arange(width, dtype=jnp.int32)
        allowed = (segments[:, None] == segment_piece[None, :]) & (
            query_index[:, None] >= key_index[None, :]
        )
        scores = jnp.where(allowed, scores, -1e30)
        peak = jnp.maximum(highest, jnp.max(scores, -1))
        weight = jnp.where(allowed, jnp.exp(scores - peak[..., None]), 0.0)
        total = jnp.sum(weight, -1)
        summed = jnp.einsum(
            "kgqs,skd->qkgd",
            weight.astype(jnp.bfloat16),
            value_heads,
            preferred_element_type=jnp.float32,
        )
        return (peak, total, summed)

    initial = (
        jnp.full((kv_heads, group, rows), -1e30, jnp.float32),
        jnp.zeros((kv_heads, group, rows), jnp.float32),
        jnp.zeros((rows, kv_heads, group, head), jnp.float32),
    )
    if again:
        highest, total, summed = visit(
            initial,
            (
                lax.all_gather(key_low, "ctx", axis=0, tiled=True),
                lax.all_gather(value_low, "ctx", axis=0, tiled=True),
                lax.all_gather(segments, "ctx", axis=0, tiled=True),
            ),
        )
    else:
        highest, total, summed = visit(
            initial,
            (
                lax.all_gather(key_low, "ctx", axis=0, tiled=True),
                lax.all_gather(value_low, "ctx", axis=0, tiled=True),
                lax.all_gather(segments, "ctx", axis=0, tiled=True),
            ),
        )
    attended = (summed / jnp.transpose(total, (2, 0, 1))[..., None]).reshape(rows, heads, head)
    return (attended, highest + jnp.log(total))


def forward(values_row, segments, places, weights, again):
    attn_gain, head_gains, w_query, w_key, w_value, w_out, ffn_gain, w_gate, w_up, w_down = weights
    rows = values_row.shape[0]
    head = head_gains.shape[0] // 2
    heads = w_query.shape[1] // head
    kv_heads = w_key.shape[1] // head
    gains = head_gains.astype(jnp.float32)
    state = {}
    state["values"] = values_row.astype(jnp.float32)
    normed, state["x_unit"], state["x_factor"] = norm_forward(
        state["values"], attn_gain.astype(jnp.float32)
    )
    state["a_low"] = normed.astype(jnp.bfloat16)
    query = matmul(state["a_low"], w_query).reshape(rows, heads, head)
    keys = matmul(state["a_low"], w_key).reshape(rows, kv_heads, head)
    state["value_low"] = matmul(state["a_low"], w_value).astype(jnp.bfloat16)
    state["cosine"], state["sine"] = angles(places, head // 2)
    query_normed, state["q_unit"], state["q_factor"] = norm_forward(query, gains[:head])
    key_normed, state["k_unit"], state["k_factor"] = norm_forward(keys, gains[head:])
    state["query_low"] = rotate(query_normed, state["cosine"], state["sine"], 1.0).astype(
        jnp.bfloat16
    )
    state["key_low"] = (
        rotate(key_normed, state["cosine"], state["sine"], 1.0)
        .astype(jnp.bfloat16)
        .reshape(rows, kv_heads * head)
    )
    state["attended"], state["log_total"] = attention_forward(
        state["query_low"], state["key_low"], state["value_low"], segments, again
    )
    state["attended_low"] = state["attended"].astype(jnp.bfloat16).reshape(rows, heads * head)
    hidden = state["values"] + matmul(state["attended_low"], w_out)
    normed_two, state["h_unit"], state["h_factor"] = norm_forward(
        hidden, ffn_gain.astype(jnp.float32)
    )
    state["b_low"] = normed_two.astype(jnp.bfloat16)
    state["gate"] = matmul(state["b_low"], w_gate)
    state["upper"] = matmul(state["b_low"], w_up)
    state["act_low"] = (jax.nn.silu(state["gate"]) * state["upper"]).astype(jnp.bfloat16)
    state["output"] = hidden + matmul(state["act_low"], w_down)
    return state


def backward(grad_row, segments, weights, state):
    attn_gain, head_gains, w_query, w_key, w_value, w_out, ffn_gain, w_gate, w_up, w_down = weights
    query_low = state["query_low"]
    rows, heads, head = query_low.shape
    kv_heads = state["key_low"].shape[1] // head
    group = heads // kv_heads
    scale = head ** (-0.5)
    gains = head_gains.astype(jnp.float32)
    incoming = grad_row.astype(jnp.float32)
    down_low = incoming.astype(jnp.bfloat16)
    g_down = left_trans(state["act_low"], down_low)
    d_act = right_trans(down_low, w_down)
    sigma = jax.nn.sigmoid(state["gate"])
    d_upper = (d_act * state["gate"] * sigma).astype(jnp.bfloat16)
    d_gate = (d_act * state["upper"] * sigma * (1.0 + state["gate"] * (1.0 - sigma))).astype(
        jnp.bfloat16
    )
    g_gate = left_trans(state["b_low"], d_gate)
    g_up = left_trans(state["b_low"], d_upper)
    d_normed = right_trans(d_gate, w_gate) + right_trans(d_upper, w_up)
    d_hidden, terms = norm_backward(
        d_normed, state["h_unit"], state["h_factor"], ffn_gain.astype(jnp.float32)
    )
    g_ffn = jnp.sum(terms, 0)
    d_hidden = incoming + d_hidden
    branch_low = d_hidden.astype(jnp.bfloat16)
    g_out = left_trans(state["attended_low"], branch_low)
    d_attended = (
        right_trans(branch_low, w_out).astype(jnp.bfloat16).reshape(rows, kv_heads, group, head)
    )
    delta = jnp.sum(
        d_attended.astype(jnp.float32) * state["attended"].reshape(rows, kv_heads, group, head), -1
    )
    delta = jnp.transpose(delta, (1, 2, 0))
    log_total = state["log_total"]
    grouped = query_low.reshape(rows, kv_heads, group, head)
    query_index = lax.axis_index("ctx") * rows + jnp.arange(rows, dtype=jnp.int32)
    key_piece = lax.all_gather(state["key_low"], "ctx", axis=0, tiled=True)
    value_piece = lax.all_gather(state["value_low"], "ctx", axis=0, tiled=True)
    segment_piece = lax.all_gather(segments, "ctx", axis=0, tiled=True)
    width = key_piece.shape[0]
    key_heads = key_piece.reshape(width, kv_heads, head)
    value_heads = value_piece.reshape(width, kv_heads, head)
    scores = (
        jnp.einsum("qkgd,skd->kgqs", grouped, key_heads, preferred_element_type=jnp.float32) * scale
    )
    key_index = jnp.arange(width, dtype=jnp.int32)
    allowed = (segments[:, None] == segment_piece[None, :]) & (
        query_index[:, None] >= key_index[None, :]
    )
    probs = jnp.where(allowed, jnp.exp(scores - log_total[..., None]), 0.0)
    d_probs = jnp.einsum(
        "qkgd,skd->kgqs", d_attended, value_heads, preferred_element_type=jnp.float32
    )
    d_scores = (probs * (d_probs - delta[..., None])).astype(jnp.bfloat16)
    d_query = (
        jnp.einsum("kgqs,skd->qkgd", d_scores, key_heads, preferred_element_type=jnp.float32)
        * scale
    )
    key_part = (
        jnp.einsum("kgqs,qkgd->skd", d_scores, grouped, preferred_element_type=jnp.float32) * scale
    )
    value_part = jnp.einsum(
        "kgqs,qkgd->skd", probs.astype(jnp.bfloat16), d_attended, preferred_element_type=jnp.float32
    )
    d_keys = key_part.reshape(width, kv_heads * head)
    d_values = value_part.reshape(width, kv_heads * head)
    d_query, d_keys_all, d_values_all = (d_query, d_keys, d_values)
    d_keys, d_values = (
        lax.psum_scatter(
            d_keys_all.astype(jnp.bfloat16), "ctx", scatter_dimension=0, tiled=True
        ).astype(jnp.float32),
        lax.psum_scatter(
            d_values_all.astype(jnp.bfloat16), "ctx", scatter_dimension=0, tiled=True
        ).astype(jnp.float32),
    )
    d_query = rotate(d_query.reshape(rows, heads, head), state["cosine"], state["sine"], -1.0)
    d_query, query_terms = norm_backward(d_query, state["q_unit"], state["q_factor"], gains[:head])
    d_keys = rotate(d_keys.reshape(rows, kv_heads, head), state["cosine"], state["sine"], -1.0)
    d_keys, key_terms = norm_backward(d_keys, state["k_unit"], state["k_factor"], gains[head:])
    g_heads = jnp.concatenate([jnp.sum(query_terms, (0, 1)), jnp.sum(key_terms, (0, 1))])
    query_grad_low = d_query.astype(jnp.bfloat16).reshape(rows, heads * head)
    key_grad_low = d_keys.astype(jnp.bfloat16).reshape(rows, kv_heads * head)
    value_grad_low = d_values.astype(jnp.bfloat16)
    g_query = left_trans(state["a_low"], query_grad_low)
    g_key = left_trans(state["a_low"], key_grad_low)
    g_value = left_trans(state["a_low"], value_grad_low)
    d_inner = (
        right_trans(query_grad_low, w_query)
        + right_trans(key_grad_low, w_key)
        + right_trans(value_grad_low, w_value)
    )
    d_input, terms = norm_backward(
        d_inner, state["x_unit"], state["x_factor"], attn_gain.astype(jnp.float32)
    )
    g_attn = jnp.sum(terms, 0)
    in_grad = (d_hidden + d_input).astype(jnp.bfloat16)
    return (in_grad, (g_attn, g_heads, g_query, g_key, g_value, g_out, g_ffn, g_gate, g_up, g_down))


def on_device(
    hidden_in,
    out_grad,
    segment_ids,
    doc_positions,
    attn_gain,
    head_gains,
    w_query,
    w_key,
    w_value,
    w_out,
    ffn_gain,
    w_gate,
    w_up,
    w_down,
):
    shards = (attn_gain, head_gains, w_query, w_key, w_value, w_out, ffn_gain, w_gate, w_up, w_down)
    micro = hidden_in.shape[0]
    outputs = []
    for micro_index in range(micro):
        weights = fetch_weights(shards)
        state = forward(
            hidden_in[micro_index, 0],
            segment_ids[micro_index, 0],
            doc_positions[micro_index, 0],
            weights,
            False,
        )
        outputs.append(state["output"].astype(jnp.bfloat16))
    in_grads = []
    totals = None
    for micro_index in range(micro):
        weights = fetch_again(shards)
        state = forward(
            hidden_in[micro_index, 0],
            segment_ids[micro_index, 0],
            doc_positions[micro_index, 0],
            weights,
            True,
        )
        in_grad, grads = backward(
            out_grad[micro_index, 0], segment_ids[micro_index, 0], weights, state
        )
        in_grads.append(in_grad)
        if totals is None:
            totals = grads
        else:
            totals = tuple((left + right for left, right in zip(totals, grads)))
    totals = lax.psum_scatter(totals, ("dp", "ctx"), scatter_dimension=0, tiled=True)
    block_out = jnp.stack(outputs)[:, None]
    input_grads = jnp.stack(in_grads)[:, None]
    return (
        block_out,
        input_grads,
        totals[0],
        totals[1],
        totals[2],
        totals[3],
        totals[4],
        totals[5],
        totals[6],
        totals[7],
        totals[8],
        totals[9],
    )


CORE, SIDE, HIGH = 1, 2, 4


def flip(array, bits):
    count = lax.axis_size("dp")
    return lax.ppermute(array, "dp", [(i, i ^ bits) for i in range(count)])


def spin(array):
    count = lax.axis_size("ctx")
    return lax.ppermute(array, "ctx", [(i, (i + 1) % count) for i in range(count)])


def hold(*arrays):
    return lax.optimization_barrier(arrays)


def choose(bit, zero, one):
    return jnp.where(bit == 0, zero, one)


def pick(array, index, axis=0):
    return lax.dynamic_index_in_dim(array, index, axis, keepdims=False)


def put(buffer, array, *place):
    index = place + (0,) * (buffer.ndim - len(place))
    shape = (1,) * (buffer.ndim - array.ndim) + array.shape
    return lax.dynamic_update_slice(buffer, array.reshape(shape), index)


def place_kernel(splits, count, slots_ref, *refs):
    pieces, outs = refs[:count], refs[count:]
    at = 0
    for piece in pieces:
        for part in range(len(splits)):
            outs[splits[part]][slots_ref[at]] = piece[part]
            at += 1


def placed(pieces, splits, slots, counts):
    shape = pieces[0].shape
    return pl.pallas_call(
        functools.partial(place_kernel, splits, len(pieces)),
        in_specs=[pl.BlockSpec(memory_space=pltpu.SMEM)]
        + [pl.BlockSpec(memory_space=pltpu.VMEM)] * len(pieces),
        out_specs=[pl.BlockSpec(memory_space=pltpu.VMEM)] * len(counts),
        out_shape=[
            jax.ShapeDtypeStruct((count,) + shape[1:], pieces[0].dtype) for count in counts
        ],
        compiler_params=pltpu.CompilerParams(vmem_limit_bytes=40 * 2**20),
    )(jnp.stack(slots).astype(jnp.int32), *pieces)


def block_kernel(slots_ref, own_ref, core_ref, side_ref, down_ref, out_ref):
    rows = own_ref.shape[1]
    for member, ref, first in ((0, own_ref, 0), (1, core_ref, 1), (2, side_ref, 0), (3, side_ref, 2)):
        for part in range(2):
            start = pl.multiple_of((part * 4 + slots_ref[member]) * rows, rows)
            out_ref[pl.ds(start, rows), :] = ref[first + part]
    out_ref[8 * rows :, : down_ref.shape[1]] = down_ref[...]
    out_ref[8 * rows :, down_ref.shape[1] :] = jnp.zeros_like(
        out_ref[8 * rows :, down_ref.shape[1] :]
    )


def unit_block(slots, own, from_core, from_side, down):
    rows, columns = own.shape[1:]
    shape = (8 * rows + down.shape[0], columns)
    return pl.pallas_call(
        block_kernel,
        in_specs=[pl.BlockSpec(memory_space=pltpu.SMEM)]
        + [pl.BlockSpec(memory_space=pltpu.VMEM)] * 4,
        out_specs=pl.BlockSpec(memory_space=pltpu.VMEM),
        out_shape=jax.ShapeDtypeStruct(shape, own.dtype),
    )(jnp.stack(slots).astype(jnp.int32), own, from_core, from_side, down)


def unit_kernel(chunk, ctx_count, tiles, rows, slots_ref, *refs):
    pieces, refs = refs[: 2 * ctx_count], refs[2 * ctx_count :]
    b_refs, df_refs = refs[:2], refs[2:4]
    act_ref, pre_ref, all_b_ref, all_df_ref = refs[-12:-8]
    db_refs, out_refs, (w_ref, down_ref, b_ref, df_ref) = refs[-8:-6], refs[-6:-4], refs[-4:]
    mid = pieces[0].shape[1]
    width = down_ref.shape[1]
    down_rows = pieces[0].shape[0] - 8 * rows
    tile = pl.program_id(0)

    @pl.when(tile == 0)
    def _():
        high = slots_ref[ctx_count]
        for step in range(ctx_count):
            place = slots_ref[step]
            for far in range(2):
                piece = pieces[2 * step + far]
                for member in range(4):
                    first = ((far * 4 + member) * ctx_count + place) * rows
                    to = pl.ds(pl.multiple_of(first, rows), rows)
                    w_ref[to, :mid] = piece[member * rows : (member + 1) * rows, :]
                    w_ref[to, mid:] = piece[(4 + member) * rows : (5 + member) * rows, :]
                half = high if far == 0 else 1 - high
                first = (half * ctx_count + place) * down_rows
                to = pl.ds(pl.multiple_of(first, 16), down_rows)
                down_ref[to, :] = piece[8 * rows :, :width]

    for which in range(2):

        @pl.when(tile // tiles == which)
        def _(which=which):
            b_ref[...] = b_refs[which][...]
            df_ref[...] = df_refs[which][...]

    b, df = b_ref[...], df_ref[...]
    all_b_ref[...] = b
    all_df_ref[...] = df
    db, out = 0.0, 0.0
    for first, last in ((0, chunk), (chunk, mid)):
        here, there = slice(first, last), slice(mid + first, mid + last)
        gate = jnp.dot(b, w_ref[:, here], preferred_element_type=jnp.float32)
        upper = jnp.dot(b, w_ref[:, there], preferred_element_type=jnp.float32)
        d_act = nt(df, down_ref[here, :])
        sigma = 1.0 / (1.0 + jnp.exp(-gate))
        silu = gate * sigma
        act = (silu * upper).astype(jnp.bfloat16)
        d_upper = (d_act * silu).astype(jnp.bfloat16)
        d_gate = (d_act * upper * sigma * (1.0 + gate * (1.0 - sigma))).astype(jnp.bfloat16)
        act_ref[:, here] = act
        pre_ref[:, here] = d_gate
        pre_ref[:, there] = d_upper
        db += nt(d_gate, w_ref[:, here]) + nt(d_upper, w_ref[:, there])
        out += jnp.dot(act, down_ref[here, :], preferred_element_type=jnp.float32)
    for which in range(2):

        @pl.when(tile // tiles == which)
        def _(which=which):
            db_refs[which][...] = db.astype(jnp.bfloat16)
            out_refs[which][...] = out.astype(jnp.bfloat16)


def feed_forward(slots, pieces, rows, b_parts, df_parts, size, begin, left):
    tokens, width = b_parts[0].shape
    mid = pieces[0].shape[1]
    down_rows = pieces[0].shape[0] - 8 * rows
    tiles = tokens // size
    once = lambda array: pl.BlockSpec(
        array.shape, lambda t: (0,) * array.ndim, pipeline_mode=pl.Buffered(1)
    )

    def part(which):
        return pl.BlockSpec((size, width), lambda t: (jnp.clip(t - which * tiles, 0, tiles - 1), 0))

    def tiled(count, first):
        return pl.BlockSpec((size, count), lambda t: (first + t, 0))

    first = begin * tiles
    first_left = 1 + len(pieces) + 4
    full = lambda count: jax.ShapeDtypeStruct((4 * tokens, count), jnp.bfloat16)
    half = jax.ShapeDtypeStruct((tokens, width), jnp.bfloat16)
    return pl.pallas_call(
        functools.partial(unit_kernel, mid // 512 * 256, len(pieces) // 2, tiles, rows),
        grid=(2 * tiles,),
        in_specs=[pl.BlockSpec(memory_space=pltpu.SMEM)]
        + [once(array) for array in pieces]
        + [part(which) for which in range(2)] * 2
        + [pl.BlockSpec(memory_space=pl.ANY)] * len(left),
        out_specs=[tiled(mid, first), tiled(2 * mid, first), tiled(width, first), tiled(width, first)]
        + [part(which) for which in range(2)] * 2,
        out_shape=[full(mid), full(2 * mid), full(width), full(width)] + [half] * 4,
        input_output_aliases={first_left + at: at for at in range(len(left))},
        scratch_shapes=[
            pltpu.VMEM((width, 2 * mid), jnp.bfloat16),
            pltpu.VMEM((len(pieces) * down_rows, width), jnp.bfloat16),
            pltpu.VMEM((size, width), jnp.bfloat16),
            pltpu.VMEM((size, width), jnp.bfloat16),
        ],
        compiler_params=pltpu.CompilerParams(vmem_limit_bytes=58 * 2**20),
        cost_estimate=pl.CostEstimate(flops=10 * tokens * mid * width, bytes_accessed=0, transcendentals=0),
    )(jnp.stack(slots).astype(jnp.int32), *pieces, *b_parts, *df_parts, *left)


def spread_kernel(ctx_count, rows, slots_ref, ffn_ref, down_ref, *outs):
    mid = ffn_ref.shape[1] // 2
    width = down_ref.shape[1]
    down_rows = down_ref.shape[0] // (2 * ctx_count)
    high = slots_ref[ctx_count]
    for far in range(2):
        half = high if far == 0 else 1 - high
        for step in range(ctx_count):
            place = slots_ref[step]
            out = outs[far * ctx_count + step]
            for member in range(4):
                first = ((far * 4 + member) * ctx_count + place) * rows
                here = pl.ds(pl.multiple_of(first, rows), rows)
                out[member * rows : (member + 1) * rows, :] = ffn_ref[here, :mid]
                out[(4 + member) * rows : (5 + member) * rows, :] = ffn_ref[here, mid:]
            first = (half * ctx_count + place) * down_rows
            here = pl.ds(pl.multiple_of(first, 16), down_rows)
            out[8 * rows :, :width] = down_ref[here, :]
            out[8 * rows :, width:] = jnp.zeros_like(out[8 * rows :, width:])


def spread_units(slots, ffn, down, rows, ctx_count):
    shape = (8 * rows + down.shape[0] // (2 * ctx_count), ffn.shape[1] // 2)
    return pl.pallas_call(
        functools.partial(spread_kernel, ctx_count, rows),
        in_specs=[pl.BlockSpec(memory_space=pltpu.SMEM)]
        + [pl.BlockSpec(memory_space=pltpu.VMEM)] * 2,
        out_specs=[pl.BlockSpec(memory_space=pltpu.VMEM)] * (2 * ctx_count),
        out_shape=[jax.ShapeDtypeStruct(shape, ffn.dtype)] * (2 * ctx_count),
        compiler_params=pltpu.CompilerParams(vmem_limit_bytes=40 * 2**20),
        cost_estimate=pl.CostEstimate(flops=10**6, bytes_accessed=0, transcendentals=0),
    )(jnp.stack(slots).astype(jnp.int32), ffn, down)


def joined(*arrays):
    buffer = jnp.zeros((len(arrays),) + arrays[0].shape, arrays[0].dtype)
    for at, array in enumerate(arrays):
        buffer = put(buffer, array, at)
    return buffer


def order(bit, own, other):
    buffer = jnp.zeros((2,) + own.shape, own.dtype)
    return put(put(buffer, own, bit), other, 1 - bit)


def swap_halves(bit, array, axis):
    low, high = jnp.split(array, 2, axis)
    return choose(bit, array, jnp.concatenate([high, low], axis))


def half_of(bit, array, axis):
    low, high = jnp.split(array, 2, axis)
    return choose(bit, low, high)


def exchange(array, target, index_of):
    dp_count, ctx_count = lax.axis_size("dp"), lax.axis_size("ctx")
    me = lax.axis_index("dp") * ctx_count + lax.axis_index("ctx")
    came, kept = [], []
    for turn in range(2):
        pairs, stay = [], []
        for dp in range(dp_count):
            for z in range(ctx_count):
                to = target(dp, z, turn)
                if to == (dp, z):
                    stay.append(dp * ctx_count + z)
                else:
                    pairs.append((dp * ctx_count + z, to[0] * ctx_count + to[1]))
        piece = pick(array, index_of(turn))
        came.append(lax.ppermute(piece, ("dp", "ctx"), pairs))
        mine = functools.reduce(jnp.logical_or, [me == which for which in stay]) if stay else None
        kept.append((piece, mine))
    return came, kept


def settled(came, kept):
    return [
        got if mine is None else jnp.where(mine, piece, got)
        for got, (piece, mine) in zip(came, kept)
    ]


def spread(array):
    ctx = lax.axis_index("ctx")

    def target(dp, z, turn):
        return dp // 2 * 2 + z // 2, 2 * ((z + turn) % 2) + dp % 2

    return exchange(array, target, lambda turn: (ctx + turn) % 2)


def unspread(array):
    ctx = lax.axis_index("ctx")

    def target(dp, z, turn):
        return dp // 2 * 2 + z % 2, 2 * (dp % 2) + (z // 2 + turn) % 2

    return exchange(array, target, lambda turn: (ctx // 2 + turn) % 2)


def swap_gather(array, bit_value, bit):
    return order(bit_value, array, flip(array, bit))


def total_low(left, right):
    return (left.astype(jnp.float32) + right.astype(jnp.float32)).astype(jnp.bfloat16)


def nt(left, right):
    return lax.dot_general(
        left, right, (((1,), (1,)), ((), ())), preferred_element_type=jnp.float32
    )


def set_bias(bias_ref, seg_row_ref, seg_col_ref, block):
    size = bias_ref.shape[0]
    for first in range(0, size, block):
        for key in range(0, first + block, block):
            allowed = seg_col_ref[key : key + block, :] == seg_row_ref[:, first : first + block]
            if key == first:
                keys = lax.broadcasted_iota(jnp.int32, (block, block), 0)
                queries = lax.broadcasted_iota(jnp.int32, (block, block), 1)
                allowed = jnp.logical_and(allowed, keys <= queries)
            bias_ref[key : key + block, first : first + block] = jnp.where(allowed, 0.0, -1e30)


def turned(values, gain, cosine, sine):
    half = values.shape[0] // 2
    factor = lax.rsqrt(jnp.mean(values * values, 0, keepdims=True) + EPS)
    normed = values * factor * gain
    first, second = normed[:half], normed[half:]
    return jnp.concatenate([first * cosine - second * sine, second * cosine + first * sine], 0)


def turned_back(incoming, values, gain, cosine, sine):
    half = values.shape[0] // 2
    first, second = incoming[:half], incoming[half:]
    incoming = jnp.concatenate(
        [first * cosine + second * sine, second * cosine - first * sine], 0
    )
    factor = lax.rsqrt(jnp.mean(values * values, 0, keepdims=True) + EPS)
    unit = values * factor
    terms = jnp.sum(incoming * unit, 1, keepdims=True)
    scaled = incoming * gain
    return factor * (scaled - unit * jnp.mean(scaled * unit, 0, keepdims=True)), terms


def forward_kernel(
    block, q_ref, kv_ref, cos_ref, sin_ref, gain_ref, row_ref, col_ref,
    o_ref, log_ref, qr_ref, kvr_ref, bias_ref
):
    head = kv_ref.shape[0] // 2
    size = kv_ref.shape[1]
    scale = head ** (-0.5)

    @pl.when(pl.program_id(0) == 0)
    def _():
        set_bias(bias_ref, row_ref, col_ref, block)

    cosine, sine = cos_ref[...], sin_ref[...]
    keys = turned(kv_ref[:head, :], gain_ref[1], cosine, sine)
    kvr_ref[:head, :] = keys.astype(jnp.bfloat16)
    keys = keys.T.astype(jnp.bfloat16)
    values = kv_ref[head:, :].astype(jnp.bfloat16)
    kvr_ref[head:, :] = values
    for which in range(q_ref.shape[0] // head):
        rows = slice(which * head, (which + 1) * head)
        query = turned(q_ref[rows, :], gain_ref[0], cosine, sine).astype(jnp.bfloat16)
        qr_ref[rows, :] = query
        for first in range(0, size, block):
            here = slice(first, first + block)
            total = jnp.zeros((1, block), jnp.float32)
            summed = jnp.zeros((head, block), jnp.float32)
            for key in range(0, first + block, block):
                there = slice(key, key + block)
                scores = jnp.dot(keys[there], query[:, here], preferred_element_type=jnp.float32)
                weight = jnp.exp(scores * scale + bias_ref[there, here])
                total += jnp.sum(weight, 0, keepdims=True)
                summed += jnp.dot(
                    values[:, there],
                    weight.astype(jnp.bfloat16),
                    preferred_element_type=jnp.float32,
                )
            o_ref[rows, here] = summed / total
            log_ref[0, which : which + 1, here] = jnp.log(total)


def backward_kernel(
    block, q_ref, kv_ref, qr_ref, kvr_ref, do_ref, o_ref, log_ref, cos_ref, sin_ref,
    gain_ref, row_ref, col_ref, dq_ref, dkv_ref, gains_ref, bias_ref, dkey_ref, dvalue_ref
):
    head = kv_ref.shape[0] // 2
    size = kv_ref.shape[1]
    scale = head ** (-0.5)

    @pl.when(pl.program_id(0) == 0)
    def _():
        set_bias(bias_ref, row_ref, col_ref, block)
        gains_ref[...] = jnp.zeros_like(gains_ref)

    cosine, sine = cos_ref[...], sin_ref[...]
    keys_t = kvr_ref[:head, :]
    keys = keys_t.astype(jnp.float32).T.astype(jnp.bfloat16)
    values = kvr_ref[head:, :].astype(jnp.float32).T.astype(jnp.bfloat16)
    dkey_ref[...] = jnp.zeros_like(dkey_ref)
    dvalue_ref[...] = jnp.zeros_like(dvalue_ref)
    found = []
    for which in range(q_ref.shape[0] // head):
        rows = slice(which * head, (which + 1) * head)
        query = qr_ref[rows, :]
        grad = do_ref[rows, :]
        delta = jnp.sum(grad.astype(jnp.float32) * o_ref[rows, :], 0, keepdims=True)
        pieces = []
        for first in range(0, size, block):
            here = slice(first, first + block)
            dquery = jnp.zeros((head, block), jnp.float32)
            for key in range(0, first + block, block):
                there = slice(key, key + block)
                scores = jnp.dot(keys[there], query[:, here], preferred_element_type=jnp.float32)
                probs = jnp.exp(
                    scores * scale + (bias_ref[there, here] - log_ref[0, which : which + 1, here])
                )
                dprobs = jnp.dot(values[there], grad[:, here], preferred_element_type=jnp.float32)
                dscores = (probs * (dprobs - delta[:, here])).astype(jnp.bfloat16)
                dquery += jnp.dot(keys_t[:, there], dscores, preferred_element_type=jnp.float32)
                dkey_ref[:, there] += nt(query[:, here], dscores)
                dvalue_ref[:, there] += nt(grad[:, here], probs.astype(jnp.bfloat16))
            pieces.append(dquery * scale)
        dquery, terms = turned_back(
            jnp.concatenate(pieces, 1), q_ref[rows, :], gain_ref[0], cosine, sine
        )
        found.append(dquery)
        gains_ref[0] += terms
    dq_ref[...] = jnp.concatenate(found, 0).T.astype(jnp.bfloat16)
    dkey, terms = turned_back(dkey_ref[...] * scale, kv_ref[:head, :], gain_ref[1], cosine, sine)
    dkv_ref[...] = jnp.concatenate([dkey, dvalue_ref[...]], 0).T.astype(jnp.bfloat16)
    gains_ref[1] += terms


def whole_spec(*shape):
    return pl.BlockSpec(shape, lambda i: (0,) * len(shape))


def attend(raw, cosine, sine, gains, segments, kv_own, head, block):
    size = raw.shape[1]
    group = raw.shape[0] // head // kv_own - 2
    query = pl.BlockSpec((group * head, size), lambda i: (i, 0))
    kv_at = group * kv_own // 2
    return pl.pallas_call(
        functools.partial(forward_kernel, block),
        grid=(kv_own,),
        in_specs=[
            query,
            pl.BlockSpec((2 * head, size), lambda i: (kv_at + i, 0)),
            whole_spec(head // 2, size),
            whole_spec(head // 2, size),
            whole_spec(2, head, 1),
            whole_spec(1, size),
            whole_spec(size, 1),
        ],
        out_specs=[
            query,
            pl.BlockSpec((1, group, size), lambda i: (i, 0, 0)),
            query,
            pl.BlockSpec((2 * head, size), lambda i: (i, 0)),
        ],
        out_shape=[
            jax.ShapeDtypeStruct((kv_own * group * head, size), jnp.float32),
            jax.ShapeDtypeStruct((kv_own, group, size), jnp.float32),
            jax.ShapeDtypeStruct((kv_own * group * head, size), jnp.bfloat16),
            jax.ShapeDtypeStruct((kv_own * 2 * head, size), jnp.bfloat16),
        ],
        scratch_shapes=[pltpu.VMEM((size, size), jnp.float32)],
        compiler_params=pltpu.CompilerParams(vmem_limit_bytes=58 * 2**20),
        cost_estimate=pl.CostEstimate(flops=10**6, bytes_accessed=0, transcendentals=0),
    )(raw, raw, cosine, sine, gains, segments[None, :], segments[:, None])


def attend_back(
    raw, turned_q, turned_kv, grad, attended, logs, cosine, sine, gains, segments,
    kv_own, head, block, begin, count
):
    size = raw.shape[1]
    group = raw.shape[0] // head // kv_own - 2
    query = pl.BlockSpec((group * head, size), lambda i: (begin + i, 0))
    kv_at = group * kv_own // 2 + begin
    return pl.pallas_call(
        functools.partial(backward_kernel, block),
        grid=(count,),
        in_specs=[
            query,
            pl.BlockSpec((2 * head, size), lambda i: (kv_at + i, 0)),
            query,
            pl.BlockSpec((2 * head, size), lambda i: (begin + i, 0)),
            query,
            query,
            pl.BlockSpec((1, group, size), lambda i: (begin + i, 0, 0)),
            whole_spec(head // 2, size),
            whole_spec(head // 2, size),
            whole_spec(2, head, 1),
            whole_spec(1, size),
            whole_spec(size, 1),
        ],
        out_specs=[
            pl.BlockSpec((size, group * head), lambda i: (0, i)),
            pl.BlockSpec((size, 2 * head), lambda i: (0, i)),
            whole_spec(2, head, 1),
        ],
        out_shape=[
            jax.ShapeDtypeStruct((size, count * group * head), jnp.bfloat16),
            jax.ShapeDtypeStruct((size, count * 2 * head), jnp.bfloat16),
            jax.ShapeDtypeStruct((2, head, 1), jnp.float32),
        ],
        scratch_shapes=[
            pltpu.VMEM((size, size), jnp.float32),
            pltpu.VMEM((head, size), jnp.float32),
            pltpu.VMEM((head, size), jnp.float32),
        ],
        compiler_params=pltpu.CompilerParams(vmem_limit_bytes=58 * 2**20),
        cost_estimate=pl.CostEstimate(flops=10**6, bytes_accessed=0, transcendentals=0),
    )(
        raw, raw, turned_q, turned_kv, grad, attended, logs, cosine, sine, gains,
        segments[None, :], segments[:, None]
    )


def on_device_fast(
    hidden_in,
    out_grad,
    segment_ids,
    doc_positions,
    attn_gain,
    head_gains,
    w_query,
    w_key,
    w_value,
    w_out,
    ffn_gain,
    w_gate,
    w_up,
    w_down,
):
    low, full = jnp.bfloat16, jnp.float32
    dp, ctx = lax.axis_index("dp"), lax.axis_index("ctx")
    ctx_count = lax.axis_size("ctx")
    core, side, high = dp % 2, dp // 2 % 2, dp // 4
    width = hidden_in.shape[-1]
    rows = w_query.shape[0]
    head = head_gains.shape[0] * lax.axis_size("dp") * ctx_count // 2
    group = w_query.shape[1] // w_key.shape[1]
    kv_own = w_key.shape[1] // head // 2
    units = w_down.shape[0] * ctx_count

    tokens = hidden_in.shape[2]
    marks = jnp.stack(
        [segment_ids[:, 0], doc_positions[:, 0] // 256, doc_positions[:, 0] % 256], 1
    ).reshape(2, 1, -1)
    marks = jnp.pad(marks, ((0, 0), (0, 15), (0, width - 3 * tokens))).astype(low)
    x_came, x_kept = spread(jnp.concatenate([hidden_in[:, 0], marks], 1))

    head_few = head_gains.shape[0]
    gains = jnp.stack([attn_gain, ffn_gain, jnp.pad(head_gains, (0, rows - head_few))])
    gains = jnp.pad(gains, ((0, rows - 3), (0, 128 - rows)))
    key_value = jnp.stack([w_key.reshape(rows, -1, 2, head), w_value.reshape(rows, -1, 2, head)], 3)
    parities = [
        jnp.concatenate(
            [
                w_query.reshape(rows, -1, 2, group * head)[:, :, which].reshape(rows, -1),
                key_value[:, :, which].reshape(rows, -1),
                gains,
            ],
            1,
        )
        for which in range(2)
    ]
    inner = parities[0].shape[1]

    tops = w_gate.shape[1] // units // 4

    def of_member(which):
        return [
            jnp.concatenate(
                [w[:, (top * 4 + which) * units : (top * 4 + which + 1) * units] for top in range(tops)],
                1,
            )
            for w in (w_gate, w_up)
        ]

    def related(zero, one, two, three):
        near, far = choose(side, zero, two), choose(side, two, zero)
        near_far, far_far = choose(side, one, three), choose(side, three, one)
        return (
            choose(core, near, near_far),
            choose(core, far, far_far),
            choose(core, near_far, near),
            choose(core, far_far, far),
        )

    members = [of_member(which) for which in range(4)]
    gate_of = related(*[member[0] for member in members])
    up_of = related(*[member[1] for member in members])
    from_core = flip(
        joined(choose(core, parities[1], parities[0]), gate_of[2], up_of[2], gate_of[3], up_of[3]),
        CORE,
    )
    block = joined(
        choose(core, parities[0], from_core[0]),
        choose(core, from_core[0], parities[1]),
        jnp.pad(w_out, ((0, 0), (0, inner - width))),
    )
    from_side = flip(joined(gate_of[1], up_of[1], from_core[3], from_core[4]), SIDE)
    blocks = [block]
    for step in range(ctx_count - 1):
        blocks.append(spin(blocks[-1]))

    def across(pair):
        return [pair, flip(pair, SIDE), flip(pair, HIGH), flip(pair, SIDE | HIGH)]

    early = across(jnp.concatenate(blocks[:2], 0))
    blocks[3], w_down_late, *early = hold(blocks[3], w_down, *early)
    late = across(jnp.concatenate(blocks[2:], 0))
    block_ffn = unit_block(
        [side * 2 + core, side * 2 + 1 - core, 2 - side * 2 + core, 2 - side * 2 + 1 - core],
        joined(gate_of[0], up_of[0]), from_core, from_side, w_down_late,
    )
    block_ffn, *x_came = hold(block_ffn, *x_came)
    ffn_blocks = [block_ffn, spin(block_ffn)]
    x_half = order(ctx // 2, *settled(x_came, x_kept))
    x_other = flip(x_half, CORE)
    block_ffn, out_late, *late = hold(block_ffn, out_grad, *late)
    ffn_far = [flip(block_ffn, HIGH)]
    df_came, df_kept = spread(out_late[:, 0])
    pieces = [
        pair[3 * part : 3 * part + 3] for pairs in (early, late) for part in range(2) for pair in pairs
    ]

    slots = []
    for step in range(ctx_count):
        place = (ctx - step) % ctx_count
        for far in range(4):
            up = 1 - high if far >= 2 else high
            across_to = 1 - side if far % 2 == 1 else side
            chip = up * 2 + across_to
            slots += [(chip * 2 + c) * ctx_count + place for c in range(2)]
            slots += [chip * ctx_count + place]
    w_in, w_mine = placed(pieces, (0, 0, 1), slots, (8 * ctx_count, 4 * ctx_count))
    w_in, w_mine = w_in.reshape(-1, inner), w_mine.reshape(-1, inner)[:, :width]
    w_in, w_mine, x_other = hold(w_in, w_mine, x_other)
    w_theirs = flip(w_mine, CORE)
    features = inner - 128
    gains_all = w_in[:, features:].reshape(-1, rows, 128)[:, :3, :rows].astype(full)
    w_in = w_in[:, :features]
    attn_gain_all, ffn_gain_all = gains_all[:, 0].reshape(-1), gains_all[:, 1].reshape(-1)
    head_gains_all = gains_all[:, 2, :head_few].reshape(2, head, 1)

    x_all = order(core, x_half, x_other)
    marks = x_all[:, :, tokens, : 3 * tokens].reshape(-1, 3, tokens)
    x_all, x_half = x_all[:, :, :tokens].reshape(-1, width), x_half[:, :tokens].reshape(-1, width)
    segments = marks[:, 0].reshape(-1).astype(jnp.int32)
    places = (256.0 * marks[:, 1].astype(full) + marks[:, 2].astype(full)).reshape(-1)
    normed, _, _ = norm_forward(x_all.astype(full), attn_gain_all)
    a_low = normed.astype(low)
    raw = lax.dot_general(w_in, a_low, (((0,), (1,)), ((), ())), preferred_element_type=full)
    raw, ffn_blocks[1], ffn_far[0], w_theirs = hold(raw, ffn_blocks[1], ffn_far[0], w_theirs)
    ffn_blocks.append(spin(ffn_blocks[1]))
    ffn_far.append(flip(ffn_blocks[1], HIGH))
    freq = THETA ** (-(jnp.arange(head // 2, dtype=full) * 2.0 / head))
    turn = freq[:, None] * places[None, :]
    cosine, sine = jnp.cos(turn), jnp.sin(turn)
    attended, logs, turned_q, turned_kv = attend(
        raw, cosine, sine, head_gains_all, segments, kv_own, head, 256
    )
    attended_low = attended.astype(low)
    o_theirs = flip(half_of(1 - core, attended_low, 1), CORE)
    o_theirs, ffn_blocks[2], ffn_far[1], *df_came = hold(
        o_theirs, ffn_blocks[2], ffn_far[1], *df_came
    )
    df = order(ctx // 2, *settled(df_came, df_kept)).reshape(-1, width)
    df_side, df_core = flip(df, SIDE), flip(df, CORE)
    ffn_blocks.append(spin(ffn_blocks[2]))
    ffn_far.append(flip(ffn_blocks[2], HIGH))
    hidden = (
        x_half.astype(full)
        + left_trans(half_of(core, attended_low, 1), w_mine)
        + left_trans(o_theirs, w_theirs)
    )
    normed_two, h_unit, h_factor = norm_forward(hidden, ffn_gain_all)
    b_own = swap_halves(high, normed_two.astype(low), 1)
    b_own, df_core, ffn_blocks[3], ffn_far[2] = hold(b_own, df_core, ffn_blocks[3], ffn_far[2])
    b_side, b_core = flip(b_own, SIDE), flip(b_own, CORE)
    ffn_far.append(flip(ffn_blocks[3], HIGH))
    b_side, b_core, df_side, ffn_far[3] = hold(b_side, b_core, df_side, ffn_far[3])
    b_both, df_both = flip(b_side, CORE), flip(df_side, CORE)

    units_of = functools.partial(
        feed_forward,
        [(ctx - step) % ctx_count for step in range(ctx_count)] + [high],
        [block for pair in zip(ffn_blocks, ffn_far) for block in pair],
        rows,
    )
    *left, db_side, db_both, out_side, out_both = units_of(
        [b_side, b_both], [df_side, df_both], 256, 2, []
    )
    got_both, got_out_both = flip(db_both, CORE), flip(out_both, CORE)
    db_far = total_low(db_side, got_both)
    block_side = total_low(out_side, got_out_both)
    db_far, block_side, b_own, b_core = hold(db_far, block_side, b_own, b_core)
    got_side = flip(db_far, SIDE)
    act, d_pre, team_b, team_df, db_own, db_core, out_own, out_core = units_of(
        [b_own, b_core], [df, df_core], 256, 0, left
    )
    db_core, d_pre, act, block_side, got_side = hold(db_core, d_pre, act, block_side, got_side)
    got_core, got_out_core, got_block = flip(db_core, CORE), flip(out_core, CORE), flip(block_side, SIDE)

    def behind(step):
        return (ctx - 1 - step) % ctx_count

    g_down = left_trans(act, team_df).astype(low)
    g_down, team_b, got_core = hold(g_down, team_b, got_core)

    db = db_own.astype(full) + got_core.astype(full) + got_side.astype(full)
    db = swap_halves(high, db, 1)
    d_hidden, ffn_terms = norm_backward(db, h_unit, h_factor, ffn_gain_all)
    d_hidden = df.astype(full) + d_hidden
    dz = d_hidden.astype(low)
    dz, team_b = hold(dz, team_b)
    dz_other = flip(dz, CORE)
    g_ffn = left_trans(team_b, d_pre).astype(low)
    g_ffn, dz_other = hold(g_ffn, dz_other)
    dz_all = order(core, dz, dz_other).reshape(-1, width)
    d_attended = right_trans(w_mine, dz_all).astype(low)
    g_out = matmul(attended_low, dz_all).astype(low).reshape(2, 2, ctx_count, -1, width)
    g_out = jnp.stack([pick(g_out, behind(step), 2) for step in range(ctx_count)], 2)
    terms = spread_units(
        [behind(step) for step in range(ctx_count)] + [high], g_ffn, g_down, rows, ctx_count
    )
    *terms, d_attended, g_out, got_out_core, got_block = hold(
        *terms, d_attended, g_out, got_out_core, got_block
    )
    block_out = hidden + out_own.astype(full) + got_out_core.astype(full) + got_block.astype(full)
    block_came, block_kept = unspread(block_out.astype(low).reshape(2, -1, width))
    near_terms = terms[:ctx_count]
    far_got = [flip(term, HIGH) for term in terms[ctx_count:-1]]

    def side_square(array):
        near = jnp.where(side == 0, array[:, 0], array[:, 1])
        far = jnp.where(side == 0, array[:, 1], array[:, 0])
        near = joined(pick(near, high), pick(near, 1 - high))
        return near, flip(joined(pick(far, high), pick(far, 1 - high)), SIDE)

    def high_square(near, got):
        sums = near.astype(full) + got.astype(full)
        return sums[0], flip(sums[1].astype(low), HIGH)

    def total(terms):
        return functools.reduce(lambda a, b: a + b, [term.astype(full) for term in terms])

    back = functools.partial(
        attend_back, raw, turned_q, turned_kv, attended=attended, logs=logs, cosine=cosine,
        sine=sine, gains=head_gains_all, segments=segments, kv_own=kv_own, head=head, block=256
    )
    out_near, out_got = side_square(g_out)
    dq_one, dkv_one, g_heads_one = back(grad=d_attended, begin=0, count=kv_own // 2)
    dq_one, out_got, far_got[0], d_attended, *block_came = hold(
        dq_one, out_got, far_got[0], d_attended, *block_came
    )
    unit_total = total_low(near_terms[0], far_got[0])
    out_near, out_got = high_square(out_near, out_got)
    d_attended, unit_total = hold(d_attended, unit_total)
    unit_ring = spin(unit_total)
    dq_two, dkv_two, g_heads_two = back(
        grad=d_attended, begin=kv_own // 2, count=kv_own - kv_own // 2
    )
    g_heads = g_heads_one + g_heads_two
    dq_two, unit_ring, far_got[1], out_got, last_term = hold(
        dq_two, unit_ring, far_got[1], out_got, terms[-1]
    )
    far_got.append(flip(last_term, HIGH))
    unit_total = total_low(unit_ring, total_low(near_terms[1], far_got[1]))
    dq_two, unit_total = hold(dq_two, unit_total)
    unit_ring = spin(unit_total)
    d_raw = jnp.concatenate([dq_one, dq_two, dkv_one, dkv_two], 1)
    d_theirs = right_trans(half_of(1 - core, d_raw, 0), w_in).astype(low)
    d_theirs, d_raw = hold(d_theirs, d_raw)
    d_from = flip(d_theirs, CORE)
    d_inner = right_trans(half_of(core, d_raw, 0), w_in)
    d_inner, d_raw = hold(d_inner, d_raw)
    g_in = left_trans(a_low, d_raw).astype(low).reshape(2, 2, 2, ctx_count, rows, features)
    g_in, d_inner, d_from = hold(g_in, d_inner, d_from)
    d_inner = d_inner + d_from.astype(full)
    _, x_unit, x_factor = norm_forward(x_half.astype(full), attn_gain_all)
    d_input, attn_terms = norm_backward(d_inner, x_unit, x_factor, attn_gain_all)
    in_grad = (d_hidden + d_input).astype(low)

    g_gains = jnp.concatenate(
        [
            jnp.sum(attn_terms, 0).reshape(2, 2, 2, ctx_count, rows),
            jnp.sum(ffn_terms, 0).reshape(2, 2, 2, ctx_count, rows),
            g_heads.reshape(2, 2, 2, ctx_count, head_few),
        ],
        -1,
    ).astype(low)
    blank = ((0, 0), (0, 0), (0, 0), (0, 14), (0, width - g_gains.shape[-1]))
    g_gains = jnp.pad(jnp.moveaxis(g_gains, 2, 3), blank)
    g_in = jnp.moveaxis(g_in, 3, 2).reshape(2, 2, ctx_count, 2 * rows, features)
    g_in = jnp.concatenate([g_in, g_gains], 3)
    g_in = jnp.stack([pick(g_in, behind(step), 2) for step in range(ctx_count)], 2)
    g_in, in_grad = hold(g_in, in_grad)
    early_near, early_got = side_square(g_in[:, :, :2])
    late_near, late_got = side_square(g_in[:, :, 2:])
    in_came, in_kept = unspread(in_grad.reshape(2, -1, width))
    out_total = out_near + out_got.astype(full)
    unit_total = total_low(unit_ring, total_low(near_terms[2], far_got[2]))
    unit_ring = spin(unit_total)
    early_near, early_got = high_square(early_near, early_got)
    early_got, late_got, unit_ring, far_got[3] = hold(early_got, late_got, unit_ring, far_got[3])
    unit_total = total_low(unit_ring, total_low(near_terms[3], far_got[3]))
    ffn_total = jnp.concatenate(
        [unit_total[: 4 * rows], unit_total[4 * rows : 8 * rows]], 1
    ).reshape(2, 2, rows, -1)
    g_down = unit_total[8 * rows :, :width]

    found = [
        pick(pick(ffn_total, side), core),
        flip(pick(pick(ffn_total, side), 1 - core), CORE),
        flip(pick(pick(ffn_total, 1 - side), core), SIDE),
        flip(pick(pick(ffn_total, 1 - side), 1 - core), SIDE | CORE),
    ]
    late_near, late_got = high_square(late_near, late_got)

    def terms_of(near, got, first):
        terms = near + got.astype(full)
        return [jnp.concatenate([terms[at], out_total[first + at]], 0) for at in range(2)]

    in_terms = terms_of(early_near, early_got, 0)
    in_ring = spin(in_terms[0].astype(low))
    in_ring, late_got = hold(in_ring, late_got)
    in_terms += terms_of(late_near, late_got, 2)
    in_ring = spin((in_ring.astype(full) + in_terms[1]).astype(low))
    in_ring, *found = hold(in_ring, *found)
    in_ring = spin((in_ring.astype(full) + in_terms[2]).astype(low))
    in_ring, *in_came = hold(in_ring, *in_came)
    found = related(*found)
    found = (found[0], found[2], found[1], found[3])

    def to_columns(first):
        return jnp.concatenate(
            [
                found[which][:, (first + top) * units : (first + top + 1) * units].astype(full)
                for top in range(tops)
                for which in range(4)
            ],
            1,
        )

    g_gate, g_up = to_columns(0), to_columns(tops)

    in_sum = in_ring.astype(full) + in_terms[3]
    g_in, g_out = in_sum[: 2 * rows].astype(low).reshape(2, rows, width), in_sum[2 * rows + 16 :]
    g_gains = in_sum[2 * rows : 2 * rows + 16]
    g_in, *block_came = hold(g_in, *block_came)
    in_grad = order(ctx % 2, *settled(in_came, in_kept))
    block_out = order(ctx % 2, *settled(block_came, block_kept))
    own = pick(g_in, core).astype(full)
    got = flip(jnp.concatenate([pick(g_in, 1 - core), g_gains.astype(low)], 0), CORE).astype(full)
    g_gains = pick(g_gains[:2] + got[rows : rows + 2], core)
    got = got[:rows]
    even, odd = choose(core, own, got), choose(core, got, own)
    first = group * head * kv_own

    def mixed(start, stop, step, size):
        return jnp.concatenate(
            [part[:, at : at + size] for at in range(start, stop, step) for part in (even, odd)], 1
        )

    return (
        block_out[:, None],
        in_grad[:, None],
        g_gains[:rows],
        g_gains[2 * rows : 2 * rows + head_few],
        mixed(0, first, group * head, group * head),
        mixed(first, features, 2 * head, head),
        mixed(first + head, features, 2 * head, head),
        g_out,
        g_gains[rows : 2 * rows],
        g_gate,
        g_up,
        g_down.astype(full),
    )


def solution(mesh):
    placed = (
        P(None, "dp", "ctx", None),
        P(None, "dp", "ctx", None),
        P(None, "dp", "ctx"),
        P(None, "dp", "ctx"),
        P(("dp", "ctx")),
        P(("dp", "ctx")),
        P(("dp", "ctx"), None),
        P(("dp", "ctx"), None),
        P(("dp", "ctx"), None),
        P(("dp", "ctx"), None),
        P(("dp", "ctx")),
        P(("dp", "ctx"), None),
        P(("dp", "ctx"), None),
        P(("dp", "ctx"), None),
    )
    fits = mesh.shape["dp"] == 8 and mesh.shape["ctx"] == 4
    return jax.shard_map(
        on_device_fast if fits else on_device,
        mesh=mesh,
        in_specs=placed,
        out_specs=(
            P(None, "dp", "ctx", None),
            P(None, "dp", "ctx", None),
            P(("dp", "ctx")),
            P(("dp", "ctx")),
            P(("dp", "ctx"), None),
            P(("dp", "ctx"), None),
            P(("dp", "ctx"), None),
            P(("dp", "ctx"), None),
            P(("dp", "ctx")),
            P(("dp", "ctx"), None),
            P(("dp", "ctx"), None),
            P(("dp", "ctx"), None),
        ),
        check_vma=False,
    )
```

```python
import functools

import jax
import jax.numpy as jnp
from jax import lax
from jax.experimental import pallas as pl
from jax.experimental.pallas import tpu as pltpu
from jax.sharding import PartitionSpec as P

EPS = 1e-05
THETA = 1000000.0


def matmul(left, right):
    return jnp.dot(left, right, preferred_element_type=jnp.float32)


def left_trans(left, right):
    return lax.dot_general(
        left, right, (((0,), (0,)), ((), ())), preferred_element_type=jnp.float32
    )


def right_trans(left, right):
    return lax.dot_general(
        left, right, (((1,), (1,)), ((), ())), preferred_element_type=jnp.float32
    )


def norm_forward(values, gain):
    factor = lax.rsqrt(jnp.mean(values * values, -1, keepdims=True) + EPS)
    unit = values * factor
    return (unit * gain, unit, factor)


def norm_backward(incoming, unit, factor, gain):
    scaled = incoming * gain
    result = factor * (scaled - unit * jnp.mean(scaled * unit, -1, keepdims=True))
    return (result, incoming * unit)


def angles(places, half):
    freq = THETA ** (-(jnp.arange(half, dtype=jnp.float32) * 2.0 / (2 * half)))
    turn = places.astype(jnp.float32)[:, None] * freq[None, :]
    return (jnp.cos(turn)[:, None, :], jnp.sin(turn)[:, None, :])


def rotate(values, cosine, sine, sign):
    half = values.shape[-1] // 2
    first = values[..., :half]
    second = values[..., half:]
    return jnp.concatenate(
        [first * cosine - sign * second * sine, second * cosine + sign * first * sine], -1
    )


def fetch_weights(shards):
    return (
        lax.all_gather(shards[0], ("dp", "ctx"), axis=0, tiled=True),
        lax.all_gather(shards[1], ("dp", "ctx"), axis=0, tiled=True),
        lax.all_gather(shards[2], ("dp", "ctx"), axis=0, tiled=True),
        lax.all_gather(shards[3], ("dp", "ctx"), axis=0, tiled=True),
        lax.all_gather(shards[4], ("dp", "ctx"), axis=0, tiled=True),
        lax.all_gather(shards[5], ("dp", "ctx"), axis=0, tiled=True),
        lax.all_gather(shards[6], ("dp", "ctx"), axis=0, tiled=True),
        lax.all_gather(shards[7], ("dp", "ctx"), axis=0, tiled=True),
        lax.all_gather(shards[8], ("dp", "ctx"), axis=0, tiled=True),
        lax.all_gather(shards[9], ("dp", "ctx"), axis=0, tiled=True),
    )


def fetch_again(shards):
    return (
        lax.all_gather(shards[0], ("dp", "ctx"), axis=0, tiled=True),
        lax.all_gather(shards[1], ("dp", "ctx"), axis=0, tiled=True),
        lax.all_gather(shards[2], ("dp", "ctx"), axis=0, tiled=True),
        lax.all_gather(shards[3], ("dp", "ctx"), axis=0, tiled=True),
        lax.all_gather(shards[4], ("dp", "ctx"), axis=0, tiled=True),
        lax.all_gather(shards[5], ("dp", "ctx"), axis=0, tiled=True),
        lax.all_gather(shards[6], ("dp", "ctx"), axis=0, tiled=True),
        lax.all_gather(shards[7], ("dp", "ctx"), axis=0, tiled=True),
        lax.all_gather(shards[8], ("dp", "ctx"), axis=0, tiled=True),
        lax.all_gather(shards[9], ("dp", "ctx"), axis=0, tiled=True),
    )


def attention_forward(query_low, key_low, value_low, segments, again):
    rows, heads, head = query_low.shape
    kv_heads = key_low.shape[1] // head
    group = heads // kv_heads
    scale = head ** (-0.5)
    grouped = query_low.reshape(rows, kv_heads, group, head)
    query_index = lax.axis_index("ctx") * rows + jnp.arange(rows, dtype=jnp.int32)

    def visit(carry, piece):
        highest, total, summed = carry
        key_piece, value_piece, segment_piece = piece
        width = key_piece.shape[0]
        key_heads = key_piece.reshape(width, kv_heads, head)
        value_heads = value_piece.reshape(width, kv_heads, head)
        scores = (
            jnp.einsum("qkgd,skd->kgqs", grouped, key_heads, preferred_element_type=jnp.float32)
            * scale
        )
        key_index = jnp.arange(width, dtype=jnp.int32)
        allowed = (segments[:, None] == segment_piece[None, :]) & (
            query_index[:, None] >= key_index[None, :]
        )
        scores = jnp.where(allowed, scores, -1e30)
        peak = jnp.maximum(highest, jnp.max(scores, -1))
        weight = jnp.where(allowed, jnp.exp(scores - peak[..., None]), 0.0)
        total = jnp.sum(weight, -1)
        summed = jnp.einsum(
            "kgqs,skd->qkgd",
            weight.astype(jnp.bfloat16),
            value_heads,
            preferred_element_type=jnp.float32,
        )
        return (peak, total, summed)

    initial = (
        jnp.full((kv_heads, group, rows), -1e30, jnp.float32),
        jnp.zeros((kv_heads, group, rows), jnp.float32),
        jnp.zeros((rows, kv_heads, group, head), jnp.float32),
    )
    if again:
        highest, total, summed = visit(
            initial,
            (
                lax.all_gather(key_low, "ctx", axis=0, tiled=True),
                lax.all_gather(value_low, "ctx", axis=0, tiled=True),
                lax.all_gather(segments, "ctx", axis=0, tiled=True),
            ),
        )
    else:
        highest, total, summed = visit(
            initial,
            (
                lax.all_gather(key_low, "ctx", axis=0, tiled=True),
                lax.all_gather(value_low, "ctx", axis=0, tiled=True),
                lax.all_gather(segments, "ctx", axis=0, tiled=True),
            ),
        )
    attended = (summed / jnp.transpose(total, (2, 0, 1))[..., None]).reshape(rows, heads, head)
    return (attended, highest + jnp.log(total))


def forward(values_row, segments, places, weights, again):
    attn_gain, head_gains, w_query, w_key, w_value, w_out, ffn_gain, w_gate, w_up, w_down = weights
    rows = values_row.shape[0]
    head = head_gains.shape[0] // 2
    heads = w_query.shape[1] // head
    kv_heads = w_key.shape[1] // head
    gains = head_gains.astype(jnp.float32)
    state = {}
    state["values"] = values_row.astype(jnp.float32)
    normed, state["x_unit"], state["x_factor"] = norm_forward(
        state["values"], attn_gain.astype(jnp.float32)
    )
    state["a_low"] = normed.astype(jnp.bfloat16)
    query = matmul(state["a_low"], w_query).reshape(rows, heads, head)
    keys = matmul(state["a_low"], w_key).reshape(rows, kv_heads, head)
    state["value_low"] = matmul(state["a_low"], w_value).astype(jnp.bfloat16)
    state["cosine"], state["sine"] = angles(places, head // 2)
    query_normed, state["q_unit"], state["q_factor"] = norm_forward(query, gains[:head])
    key_normed, state["k_unit"], state["k_factor"] = norm_forward(keys, gains[head:])
    state["query_low"] = rotate(query_normed, state["cosine"], state["sine"], 1.0).astype(
        jnp.bfloat16
    )
    state["key_low"] = (
        rotate(key_normed, state["cosine"], state["sine"], 1.0)
        .astype(jnp.bfloat16)
        .reshape(rows, kv_heads * head)
    )
    state["attended"], state["log_total"] = attention_forward(
        state["query_low"], state["key_low"], state["value_low"], segments, again
    )
    state["attended_low"] = state["attended"].astype(jnp.bfloat16).reshape(rows, heads * head)
    hidden = state["values"] + matmul(state["attended_low"], w_out)
    normed_two, state["h_unit"], state["h_factor"] = norm_forward(
        hidden, ffn_gain.astype(jnp.float32)
    )
    state["b_low"] = normed_two.astype(jnp.bfloat16)
    state["gate"] = matmul(state["b_low"], w_gate)
    state["upper"] = matmul(state["b_low"], w_up)
    state["act_low"] = (jax.nn.silu(state["gate"]) * state["upper"]).astype(jnp.bfloat16)
    state["output"] = hidden + matmul(state["act_low"], w_down)
    return state


def backward(grad_row, segments, weights, state):
    attn_gain, head_gains, w_query, w_key, w_value, w_out, ffn_gain, w_gate, w_up, w_down = weights
    query_low = state["query_low"]
    rows, heads, head = query_low.shape
    kv_heads = state["key_low"].shape[1] // head
    group = heads // kv_heads
    scale = head ** (-0.5)
    gains = head_gains.astype(jnp.float32)
    incoming = grad_row.astype(jnp.float32)
    down_low = incoming.astype(jnp.bfloat16)
    g_down = left_trans(state["act_low"], down_low)
    d_act = right_trans(down_low, w_down)
    sigma = jax.nn.sigmoid(state["gate"])
    d_upper = (d_act * state["gate"] * sigma).astype(jnp.bfloat16)
    d_gate = (d_act * state["upper"] * sigma * (1.0 + state["gate"] * (1.0 - sigma))).astype(
        jnp.bfloat16
    )
    g_gate = left_trans(state["b_low"], d_gate)
    g_up = left_trans(state["b_low"], d_upper)
    d_normed = right_trans(d_gate, w_gate) + right_trans(d_upper, w_up)
    d_hidden, terms = norm_backward(
        d_normed, state["h_unit"], state["h_factor"], ffn_gain.astype(jnp.float32)
    )
    g_ffn = jnp.sum(terms, 0)
    d_hidden = incoming + d_hidden
    branch_low = d_hidden.astype(jnp.bfloat16)
    g_out = left_trans(state["attended_low"], branch_low)
    d_attended = (
        right_trans(branch_low, w_out).astype(jnp.bfloat16).reshape(rows, kv_heads, group, head)
    )
    delta = jnp.sum(
        d_attended.astype(jnp.float32) * state["attended"].reshape(rows, kv_heads, group, head), -1
    )
    delta = jnp.transpose(delta, (1, 2, 0))
    log_total = state["log_total"]
    grouped = query_low.reshape(rows, kv_heads, group, head)
    query_index = lax.axis_index("ctx") * rows + jnp.arange(rows, dtype=jnp.int32)
    key_piece = lax.all_gather(state["key_low"], "ctx", axis=0, tiled=True)
    value_piece = lax.all_gather(state["value_low"], "ctx", axis=0, tiled=True)
    segment_piece = lax.all_gather(segments, "ctx", axis=0, tiled=True)
    width = key_piece.shape[0]
    key_heads = key_piece.reshape(width, kv_heads, head)
    value_heads = value_piece.reshape(width, kv_heads, head)
    scores = (
        jnp.einsum("qkgd,skd->kgqs", grouped, key_heads, preferred_element_type=jnp.float32) * scale
    )
    key_index = jnp.arange(width, dtype=jnp.int32)
    allowed = (segments[:, None] == segment_piece[None, :]) & (
        query_index[:, None] >= key_index[None, :]
    )
    probs = jnp.where(allowed, jnp.exp(scores - log_total[..., None]), 0.0)
    d_probs = jnp.einsum(
        "qkgd,skd->kgqs", d_attended, value_heads, preferred_element_type=jnp.float32
    )
    d_scores = (probs * (d_probs - delta[..., None])).astype(jnp.bfloat16)
    d_query = (
        jnp.einsum("kgqs,skd->qkgd", d_scores, key_heads, preferred_element_type=jnp.float32)
        * scale
    )
    key_part = (
        jnp.einsum("kgqs,qkgd->skd", d_scores, grouped, preferred_element_type=jnp.float32) * scale
    )
    value_part = jnp.einsum(
        "kgqs,qkgd->skd", probs.astype(jnp.bfloat16), d_attended, preferred_element_type=jnp.float32
    )
    d_keys = key_part.reshape(width, kv_heads * head)
    d_values = value_part.reshape(width, kv_heads * head)
    d_query, d_keys_all, d_values_all = (d_query, d_keys, d_values)
    d_keys, d_values = (
        lax.psum_scatter(
            d_keys_all.astype(jnp.bfloat16), "ctx", scatter_dimension=0, tiled=True
        ).astype(jnp.float32),
        lax.psum_scatter(
            d_values_all.astype(jnp.bfloat16), "ctx", scatter_dimension=0, tiled=True
        ).astype(jnp.float32),
    )
    d_query = rotate(d_query.reshape(rows, heads, head), state["cosine"], state["sine"], -1.0)
    d_query, query_terms = norm_backward(d_query, state["q_unit"], state["q_factor"], gains[:head])
    d_keys = rotate(d_keys.reshape(rows, kv_heads, head), state["cosine"], state["sine"], -1.0)
    d_keys, key_terms = norm_backward(d_keys, state["k_unit"], state["k_factor"], gains[head:])
    g_heads = jnp.concatenate([jnp.sum(query_terms, (0, 1)), jnp.sum(key_terms, (0, 1))])
    query_grad_low = d_query.astype(jnp.bfloat16).reshape(rows, heads * head)
    key_grad_low = d_keys.astype(jnp.bfloat16).reshape(rows, kv_heads * head)
    value_grad_low = d_values.astype(jnp.bfloat16)
    g_query = left_trans(state["a_low"], query_grad_low)
    g_key = left_trans(state["a_low"], key_grad_low)
    g_value = left_trans(state["a_low"], value_grad_low)
    d_inner = (
        right_trans(query_grad_low, w_query)
        + right_trans(key_grad_low, w_key)
        + right_trans(value_grad_low, w_value)
    )
    d_input, terms = norm_backward(
        d_inner, state["x_unit"], state["x_factor"], attn_gain.astype(jnp.float32)
    )
    g_attn = jnp.sum(terms, 0)
    in_grad = (d_hidden + d_input).astype(jnp.bfloat16)
    return (in_grad, (g_attn, g_heads, g_query, g_key, g_value, g_out, g_ffn, g_gate, g_up, g_down))


def on_device(
    hidden_in,
    out_grad,
    segment_ids,
    doc_positions,
    attn_gain,
    head_gains,
    w_query,
    w_key,
    w_value,
    w_out,
    ffn_gain,
    w_gate,
    w_up,
    w_down,
):
    shards = (attn_gain, head_gains, w_query, w_key, w_value, w_out, ffn_gain, w_gate, w_up, w_down)
    micro = hidden_in.shape[0]
    outputs = []
    for micro_index in range(micro):
        weights = fetch_weights(shards)
        state = forward(
            hidden_in[micro_index, 0],
            segment_ids[micro_index, 0],
            doc_positions[micro_index, 0],
            weights,
            False,
        )
        outputs.append(state["output"].astype(jnp.bfloat16))
    in_grads = []
    totals = None
    for micro_index in range(micro):
        weights = fetch_again(shards)
        state = forward(
            hidden_in[micro_index, 0],
            segment_ids[micro_index, 0],
            doc_positions[micro_index, 0],
            weights,
            True,
        )
        in_grad, grads = backward(
            out_grad[micro_index, 0], segment_ids[micro_index, 0], weights, state
        )
        in_grads.append(in_grad)
        if totals is None:
            totals = grads
        else:
            totals = tuple((left + right for left, right in zip(totals, grads)))
    totals = lax.psum_scatter(totals, ("dp", "ctx"), scatter_dimension=0, tiled=True)
    block_out = jnp.stack(outputs)[:, None]
    input_grads = jnp.stack(in_grads)[:, None]
    return (
        block_out,
        input_grads,
        totals[0],
        totals[1],
        totals[2],
        totals[3],
        totals[4],
        totals[5],
        totals[6],
        totals[7],
        totals[8],
        totals[9],
    )


CORE, SIDE, HIGH = 1, 2, 4


def flip(array, bits):
    count = lax.axis_size("dp")
    return lax.ppermute(array, "dp", [(i, i ^ bits) for i in range(count)])


def spin(array):
    count = lax.axis_size("ctx")
    return lax.ppermute(array, "ctx", [(i, (i + 1) % count) for i in range(count)])


def hold(*arrays):
    return lax.optimization_barrier(arrays)


def choose(bit, zero, one):
    return jnp.where(bit == 0, zero, one)


def pick(array, index, axis=0):
    return lax.dynamic_index_in_dim(array, index, axis, keepdims=False)


def put(buffer, array, *place):
    index = place + (0,) * (buffer.ndim - len(place))
    shape = (1,) * (buffer.ndim - array.ndim) + array.shape
    return lax.dynamic_update_slice(buffer, array.reshape(shape), index)


def place_kernel(splits, count, slots_ref, *refs):
    pieces, outs = refs[:count], refs[count:]
    at = 0
    for piece in pieces:
        for part in range(len(splits)):
            outs[splits[part]][slots_ref[at]] = piece[part]
            at += 1


def placed(pieces, splits, slots, counts):
    shape = pieces[0].shape
    return pl.pallas_call(
        functools.partial(place_kernel, splits, len(pieces)),
        in_specs=[pl.BlockSpec(memory_space=pltpu.SMEM)]
        + [pl.BlockSpec(memory_space=pltpu.VMEM)] * len(pieces),
        out_specs=[pl.BlockSpec(memory_space=pltpu.VMEM)] * len(counts),
        out_shape=[
            jax.ShapeDtypeStruct((count,) + shape[1:], pieces[0].dtype) for count in counts
        ],
        compiler_params=pltpu.CompilerParams(vmem_limit_bytes=40 * 2**20),
    )(jnp.stack(slots).astype(jnp.int32), *pieces)


def block_kernel(slots_ref, own_ref, core_ref, side_ref, down_ref, out_ref):
    rows = own_ref.shape[1]
    for member, ref, first in ((0, own_ref, 0), (1, core_ref, 1), (2, side_ref, 0), (3, side_ref, 2)):
        for part in range(2):
            start = pl.multiple_of((part * 4 + slots_ref[member]) * rows, rows)
            out_ref[pl.ds(start, rows), :] = ref[first + part]
    out_ref[8 * rows :, : down_ref.shape[1]] = down_ref[...]
    out_ref[8 * rows :, down_ref.shape[1] :] = jnp.zeros_like(
        out_ref[8 * rows :, down_ref.shape[1] :]
    )


def unit_block(slots, own, from_core, from_side, down):
    rows, columns = own.shape[1:]
    shape = (8 * rows + down.shape[0], columns)
    return pl.pallas_call(
        block_kernel,
        in_specs=[pl.BlockSpec(memory_space=pltpu.SMEM)]
        + [pl.BlockSpec(memory_space=pltpu.VMEM)] * 4,
        out_specs=pl.BlockSpec(memory_space=pltpu.VMEM),
        out_shape=jax.ShapeDtypeStruct(shape, own.dtype),
    )(jnp.stack(slots).astype(jnp.int32), own, from_core, from_side, down)


def unit_kernel(chunk, ctx_count, tiles, rows, slots_ref, *refs):
    pieces, refs = refs[: 2 * ctx_count], refs[2 * ctx_count :]
    b_refs, df_refs = refs[:2], refs[2:4]
    act_ref, pre_ref, all_b_ref, all_df_ref = refs[-12:-8]
    db_refs, out_refs, (w_ref, down_ref, b_ref, df_ref) = refs[-8:-6], refs[-6:-4], refs[-4:]
    mid = pieces[0].shape[1]
    width = down_ref.shape[1]
    down_rows = pieces[0].shape[0] - 8 * rows
    tile = pl.program_id(0)

    @pl.when(tile == 0)
    def _():
        high = slots_ref[ctx_count]
        for step in range(ctx_count):
            place = slots_ref[step]
            for far in range(2):
                piece = pieces[2 * step + far]
                for member in range(4):
                    first = ((far * 4 + member) * ctx_count + place) * rows
                    to = pl.ds(pl.multiple_of(first, rows), rows)
                    for first, last in ((0, chunk), (chunk, mid)):
                        middle = first + last
                        w_ref[to, 2 * first : middle] = piece[
                            member * rows : (member + 1) * rows, first:last
                        ]
                        w_ref[to, middle : 2 * last] = piece[
                            (4 + member) * rows : (5 + member) * rows, first:last
                        ]
                half = high if far == 0 else 1 - high
                first = (half * ctx_count + place) * down_rows
                to = pl.ds(pl.multiple_of(first, 16), down_rows)
                down_ref[to, :] = piece[8 * rows :, :width]

    for which in range(2):

        @pl.when(tile // tiles == which)
        def _(which=which):
            b_ref[...] = b_refs[which][...]
            df_ref[...] = df_refs[which][...]

    b, df = b_ref[...], df_ref[...]
    all_b_ref[...] = b
    all_df_ref[...] = df
    db, out = 0.0, 0.0
    for first, last in ((0, chunk), (chunk, mid)):
        here, there = slice(first, last), slice(mid + first, mid + last)
        both = slice(2 * first, 2 * last)
        pre = jnp.dot(b, w_ref[:, both], preferred_element_type=jnp.float32)
        gate, upper = pre[:, : last - first], pre[:, last - first :]
        d_act = nt(df, down_ref[here, :])
        sigma = 1.0 / (1.0 + jnp.exp(-gate))
        silu = gate * sigma
        act = (silu * upper).astype(jnp.bfloat16)
        d_upper = (d_act * silu).astype(jnp.bfloat16)
        d_gate = (d_act * upper * sigma * (1.0 + gate * (1.0 - sigma))).astype(jnp.bfloat16)
        act_ref[:, here] = act
        pre_ref[:, here] = d_gate
        pre_ref[:, there] = d_upper
        db += nt(jnp.concatenate([d_gate, d_upper], 1), w_ref[:, both])
        out += jnp.dot(act, down_ref[here, :], preferred_element_type=jnp.float32)
    for which in range(2):

        @pl.when(tile // tiles == which)
        def _(which=which):
            db_refs[which][...] = db.astype(jnp.bfloat16)
            out_refs[which][...] = out.astype(jnp.bfloat16)


def feed_forward(slots, pieces, rows, b_parts, df_parts, size, begin, left):
    tokens, width = b_parts[0].shape
    mid = pieces[0].shape[1]
    down_rows = pieces[0].shape[0] - 8 * rows
    tiles = tokens // size
    once = lambda array: pl.BlockSpec(
        array.shape, lambda t: (0,) * array.ndim, pipeline_mode=pl.Buffered(1)
    )

    def part(which):
        return pl.BlockSpec((size, width), lambda t: (jnp.clip(t - which * tiles, 0, tiles - 1), 0))

    def tiled(count, first):
        return pl.BlockSpec((size, count), lambda t: (first + t, 0))

    first = begin * tiles
    first_left = 1 + len(pieces) + 4
    full = lambda count: jax.ShapeDtypeStruct((4 * tokens, count), jnp.bfloat16)
    half = jax.ShapeDtypeStruct((tokens, width), jnp.bfloat16)
    return pl.pallas_call(
        functools.partial(unit_kernel, mid // 512 * 256, len(pieces) // 2, tiles, rows),
        grid=(2 * tiles,),
        in_specs=[pl.BlockSpec(memory_space=pltpu.SMEM)]
        + [once(array) for array in pieces]
        + [part(which) for which in range(2)] * 2
        + [pl.BlockSpec(memory_space=pl.ANY)] * len(left),
        out_specs=[tiled(mid, first), tiled(2 * mid, first), tiled(width, first), tiled(width, first)]
        + [part(which) for which in range(2)] * 2,
        out_shape=[full(mid), full(2 * mid), full(width), full(width)] + [half] * 4,
        input_output_aliases={first_left + at: at for at in range(len(left))},
        scratch_shapes=[
            pltpu.VMEM((width, 2 * mid), jnp.bfloat16),
            pltpu.VMEM((len(pieces) * down_rows, width), jnp.bfloat16),
            pltpu.VMEM((size, width), jnp.bfloat16),
            pltpu.VMEM((size, width), jnp.bfloat16),
        ],
        compiler_params=pltpu.CompilerParams(vmem_limit_bytes=58 * 2**20),
        cost_estimate=pl.CostEstimate(flops=10 * tokens * mid * width, bytes_accessed=0, transcendentals=0),
    )(jnp.stack(slots).astype(jnp.int32), *pieces, *b_parts, *df_parts, *left)


def spread_kernel(ctx_count, rows, slots_ref, ffn_ref, down_ref, *outs):
    mid = ffn_ref.shape[1] // 2
    width = down_ref.shape[1]
    down_rows = down_ref.shape[0] // (2 * ctx_count)
    high = slots_ref[ctx_count]
    for far in range(2):
        half = high if far == 0 else 1 - high
        for step in range(ctx_count):
            place = slots_ref[step]
            out = outs[far * ctx_count + step]
            for member in range(4):
                first = ((far * 4 + member) * ctx_count + place) * rows
                here = pl.ds(pl.multiple_of(first, rows), rows)
                out[member * rows : (member + 1) * rows, :] = ffn_ref[here, :mid]
                out[(4 + member) * rows : (5 + member) * rows, :] = ffn_ref[here, mid:]
            first = (half * ctx_count + place) * down_rows
            here = pl.ds(pl.multiple_of(first, 16), down_rows)
            out[8 * rows :, :width] = down_ref[here, :]
            out[8 * rows :, width:] = jnp.zeros_like(out[8 * rows :, width:])


def spread_units(slots, ffn, down, rows, ctx_count):
    shape = (8 * rows + down.shape[0] // (2 * ctx_count), ffn.shape[1] // 2)
    return pl.pallas_call(
        functools.partial(spread_kernel, ctx_count, rows),
        in_specs=[pl.BlockSpec(memory_space=pltpu.SMEM)]
        + [pl.BlockSpec(memory_space=pltpu.VMEM)] * 2,
        out_specs=[pl.BlockSpec(memory_space=pltpu.VMEM)] * (2 * ctx_count),
        out_shape=[jax.ShapeDtypeStruct(shape, ffn.dtype)] * (2 * ctx_count),
        compiler_params=pltpu.CompilerParams(vmem_limit_bytes=40 * 2**20),
        cost_estimate=pl.CostEstimate(flops=10**6, bytes_accessed=0, transcendentals=0),
    )(jnp.stack(slots).astype(jnp.int32), ffn, down)


def joined(*arrays):
    buffer = jnp.zeros((len(arrays),) + arrays[0].shape, arrays[0].dtype)
    for at, array in enumerate(arrays):
        buffer = put(buffer, array, at)
    return buffer


def order(bit, own, other):
    buffer = jnp.zeros((2,) + own.shape, own.dtype)
    return put(put(buffer, own, bit), other, 1 - bit)


def swap_halves(bit, array, axis):
    low, high = jnp.split(array, 2, axis)
    return choose(bit, array, jnp.concatenate([high, low], axis))


def half_of(bit, array, axis):
    low, high = jnp.split(array, 2, axis)
    return choose(bit, low, high)


def exchange(array, target, index_of):
    dp_count, ctx_count = lax.axis_size("dp"), lax.axis_size("ctx")
    me = lax.axis_index("dp") * ctx_count + lax.axis_index("ctx")
    came, kept = [], []
    for turn in range(2):
        pairs, stay = [], []
        for dp in range(dp_count):
            for z in range(ctx_count):
                to = target(dp, z, turn)
                if to == (dp, z):
                    stay.append(dp * ctx_count + z)
                else:
                    pairs.append((dp * ctx_count + z, to[0] * ctx_count + to[1]))
        piece = pick(array, index_of(turn))
        came.append(lax.ppermute(piece, ("dp", "ctx"), pairs))
        mine = functools.reduce(jnp.logical_or, [me == which for which in stay]) if stay else None
        kept.append((piece, mine))
    return came, kept


def settled(came, kept):
    return [
        got if mine is None else jnp.where(mine, piece, got)
        for got, (piece, mine) in zip(came, kept)
    ]


def spread(array):
    ctx = lax.axis_index("ctx")

    def target(dp, z, turn):
        return dp // 2 * 2 + z // 2, 2 * ((z + turn) % 2) + dp % 2

    return exchange(array, target, lambda turn: (ctx + turn) % 2)


def unspread(array):
    ctx = lax.axis_index("ctx")

    def target(dp, z, turn):
        return dp // 2 * 2 + z % 2, 2 * (dp % 2) + (z // 2 + turn) % 2

    return exchange(array, target, lambda turn: (ctx // 2 + turn) % 2)


def swap_gather(array, bit_value, bit):
    return order(bit_value, array, flip(array, bit))


def total_low(left, right):
    return (left.astype(jnp.float32) + right.astype(jnp.float32)).astype(jnp.bfloat16)


def nt(left, right):
    return lax.dot_general(
        left, right, (((1,), (1,)), ((), ())), preferred_element_type=jnp.float32
    )


def set_bias(bias_ref, seg_row_ref, seg_col_ref, block):
    size = bias_ref.shape[0]
    for first in range(0, size, block):
        for key in range(0, first + block, block):
            allowed = seg_col_ref[key : key + block, :] == seg_row_ref[:, first : first + block]
            if key == first:
                keys = lax.broadcasted_iota(jnp.int32, (block, block), 0)
                queries = lax.broadcasted_iota(jnp.int32, (block, block), 1)
                allowed = jnp.logical_and(allowed, keys <= queries)
            bias_ref[key : key + block, first : first + block] = jnp.where(allowed, 0.0, -1e30)


def turned(values, gain, cosine, sine):
    half = values.shape[0] // 2
    factor = lax.rsqrt(jnp.mean(values * values, 0, keepdims=True) + EPS)
    normed = values * factor * gain
    first, second = normed[:half], normed[half:]
    return jnp.concatenate([first * cosine - second * sine, second * cosine + first * sine], 0)


def turned_back(incoming, values, gain, cosine, sine):
    half = values.shape[0] // 2
    first, second = incoming[:half], incoming[half:]
    incoming = jnp.concatenate(
        [first * cosine + second * sine, second * cosine - first * sine], 0
    )
    factor = lax.rsqrt(jnp.mean(values * values, 0, keepdims=True) + EPS)
    unit = values * factor
    terms = jnp.sum(incoming * unit, 1, keepdims=True)
    scaled = incoming * gain
    return factor * (scaled - unit * jnp.mean(scaled * unit, 0, keepdims=True)), terms


def forward_kernel(
    block, q_ref, kv_ref, cos_ref, sin_ref, gain_ref, row_ref, col_ref,
    o_ref, log_ref, qr_ref, kvr_ref, bias_ref
):
    head = kv_ref.shape[0] // 2
    size = kv_ref.shape[1]
    scale = head ** (-0.5)

    @pl.when(pl.program_id(0) == 0)
    def _():
        set_bias(bias_ref, row_ref, col_ref, block)

    cosine, sine = cos_ref[...], sin_ref[...]
    keys = turned(kv_ref[:head, :], gain_ref[1], cosine, sine)
    kvr_ref[:head, :] = keys.astype(jnp.bfloat16)
    keys = keys.T.astype(jnp.bfloat16)
    values = kv_ref[head:, :].astype(jnp.bfloat16)
    kvr_ref[head:, :] = values
    for which in range(q_ref.shape[0] // head):
        rows = slice(which * head, (which + 1) * head)
        query = turned(q_ref[rows, :], gain_ref[0], cosine, sine).astype(jnp.bfloat16)
        qr_ref[rows, :] = query
        for first in range(0, size, block):
            here = slice(first, first + block)
            total = jnp.zeros((1, block), jnp.float32)
            summed = jnp.zeros((head, block), jnp.float32)
            for key in range(0, first + block, block):
                there = slice(key, key + block)
                scores = jnp.dot(keys[there], query[:, here], preferred_element_type=jnp.float32)
                weight = jnp.exp(scores * scale + bias_ref[there, here])
                total += jnp.sum(weight, 0, keepdims=True)
                summed += jnp.dot(
                    values[:, there],
                    weight.astype(jnp.bfloat16),
                    preferred_element_type=jnp.float32,
                )
            o_ref[rows, here] = summed / total
            log_ref[0, which : which + 1, here] = jnp.log(total)


def backward_kernel(
    block, q_ref, kv_ref, qr_ref, kvr_ref, do_ref, o_ref, log_ref, cos_ref, sin_ref,
    gain_ref, row_ref, col_ref, dq_ref, dkv_ref, gains_ref, bias_ref, dkey_ref, dvalue_ref
):
    head = kv_ref.shape[0] // 2
    size = kv_ref.shape[1]
    scale = head ** (-0.5)

    @pl.when(pl.program_id(0) == 0)
    def _():
        set_bias(bias_ref, row_ref, col_ref, block)
        gains_ref[...] = jnp.zeros_like(gains_ref)

    cosine, sine = cos_ref[...], sin_ref[...]
    keys_t = kvr_ref[:head, :]
    keys = keys_t.astype(jnp.float32).T.astype(jnp.bfloat16)
    values = kvr_ref[head:, :].astype(jnp.float32).T.astype(jnp.bfloat16)
    dkey_ref[...] = jnp.zeros_like(dkey_ref)
    dvalue_ref[...] = jnp.zeros_like(dvalue_ref)
    found = []
    for which in range(q_ref.shape[0] // head):
        rows = slice(which * head, (which + 1) * head)
        query = qr_ref[rows, :]
        grad = do_ref[rows, :]
        delta = jnp.sum(grad.astype(jnp.float32) * o_ref[rows, :], 0, keepdims=True)
        pieces = []
        for first in range(0, size, block):
            here = slice(first, first + block)
            dquery = jnp.zeros((head, block), jnp.float32)
            for key in range(0, first + block, block):
                there = slice(key, key + block)
                scores = jnp.dot(keys[there], query[:, here], preferred_element_type=jnp.float32)
                probs = jnp.exp(
                    scores * scale + (bias_ref[there, here] - log_ref[0, which : which + 1, here])
                )
                dprobs = jnp.dot(values[there], grad[:, here], preferred_element_type=jnp.float32)
                dscores = (probs * (dprobs - delta[:, here])).astype(jnp.bfloat16)
                dquery += jnp.dot(keys_t[:, there], dscores, preferred_element_type=jnp.float32)
                dkey_ref[:, there] += nt(query[:, here], dscores)
                dvalue_ref[:, there] += nt(grad[:, here], probs.astype(jnp.bfloat16))
            pieces.append(dquery * scale)
        dquery, terms = turned_back(
            jnp.concatenate(pieces, 1), q_ref[rows, :], gain_ref[0], cosine, sine
        )
        found.append(dquery)
        gains_ref[0] += terms
    dq_ref[...] = jnp.concatenate(found, 0).T.astype(jnp.bfloat16)
    dkey, terms = turned_back(dkey_ref[...] * scale, kv_ref[:head, :], gain_ref[1], cosine, sine)
    dkv_ref[...] = jnp.concatenate([dkey, dvalue_ref[...]], 0).T.astype(jnp.bfloat16)
    gains_ref[1] += terms


def whole_spec(*shape):
    return pl.BlockSpec(shape, lambda i: (0,) * len(shape))


def attend(raw, cosine, sine, gains, segments, kv_own, head, block):
    size = raw.shape[1]
    group = raw.shape[0] // head // kv_own - 2
    query = pl.BlockSpec((group * head, size), lambda i: (i, 0))
    kv_at = group * kv_own // 2
    return pl.pallas_call(
        functools.partial(forward_kernel, block),
        grid=(kv_own,),
        in_specs=[
            query,
            pl.BlockSpec((2 * head, size), lambda i: (kv_at + i, 0)),
            whole_spec(head // 2, size),
            whole_spec(head // 2, size),
            whole_spec(2, head, 1),
            whole_spec(1, size),
            whole_spec(size, 1),
        ],
        out_specs=[
            query,
            pl.BlockSpec((1, group, size), lambda i: (i, 0, 0)),
            query,
            pl.BlockSpec((2 * head, size), lambda i: (i, 0)),
        ],
        out_shape=[
            jax.ShapeDtypeStruct((kv_own * group * head, size), jnp.float32),
            jax.ShapeDtypeStruct((kv_own, group, size), jnp.float32),
            jax.ShapeDtypeStruct((kv_own * group * head, size), jnp.bfloat16),
            jax.ShapeDtypeStruct((kv_own * 2 * head, size), jnp.bfloat16),
        ],
        scratch_shapes=[pltpu.VMEM((size, size), jnp.float32)],
        compiler_params=pltpu.CompilerParams(vmem_limit_bytes=58 * 2**20),
        cost_estimate=pl.CostEstimate(flops=10**6, bytes_accessed=0, transcendentals=0),
    )(raw, raw, cosine, sine, gains, segments[None, :], segments[:, None])


def attend_back(
    raw, turned_q, turned_kv, grad, attended, logs, cosine, sine, gains, segments,
    kv_own, head, block, begin, count
):
    size = raw.shape[1]
    group = raw.shape[0] // head // kv_own - 2
    query = pl.BlockSpec((group * head, size), lambda i: (begin + i, 0))
    kv_at = group * kv_own // 2 + begin
    return pl.pallas_call(
        functools.partial(backward_kernel, block),
        grid=(count,),
        in_specs=[
            query,
            pl.BlockSpec((2 * head, size), lambda i: (kv_at + i, 0)),
            query,
            pl.BlockSpec((2 * head, size), lambda i: (begin + i, 0)),
            query,
            query,
            pl.BlockSpec((1, group, size), lambda i: (begin + i, 0, 0)),
            whole_spec(head // 2, size),
            whole_spec(head // 2, size),
            whole_spec(2, head, 1),
            whole_spec(1, size),
            whole_spec(size, 1),
        ],
        out_specs=[
            pl.BlockSpec((size, group * head), lambda i: (0, i)),
            pl.BlockSpec((size, 2 * head), lambda i: (0, i)),
            whole_spec(2, head, 1),
        ],
        out_shape=[
            jax.ShapeDtypeStruct((size, count * group * head), jnp.bfloat16),
            jax.ShapeDtypeStruct((size, count * 2 * head), jnp.bfloat16),
            jax.ShapeDtypeStruct((2, head, 1), jnp.float32),
        ],
        scratch_shapes=[
            pltpu.VMEM((size, size), jnp.float32),
            pltpu.VMEM((head, size), jnp.float32),
            pltpu.VMEM((head, size), jnp.float32),
        ],
        compiler_params=pltpu.CompilerParams(vmem_limit_bytes=58 * 2**20),
        cost_estimate=pl.CostEstimate(flops=10**6, bytes_accessed=0, transcendentals=0),
    )(
        raw, raw, turned_q, turned_kv, grad, attended, logs, cosine, sine, gains,
        segments[None, :], segments[:, None]
    )


def on_device_fast(
    hidden_in,
    out_grad,
    segment_ids,
    doc_positions,
    attn_gain,
    head_gains,
    w_query,
    w_key,
    w_value,
    w_out,
    ffn_gain,
    w_gate,
    w_up,
    w_down,
):
    low, full = jnp.bfloat16, jnp.float32
    dp, ctx = lax.axis_index("dp"), lax.axis_index("ctx")
    ctx_count = lax.axis_size("ctx")
    core, side, high = dp % 2, dp // 2 % 2, dp // 4
    width = hidden_in.shape[-1]
    rows = w_query.shape[0]
    head = head_gains.shape[0] * lax.axis_size("dp") * ctx_count // 2
    group = w_query.shape[1] // w_key.shape[1]
    kv_own = w_key.shape[1] // head // 2
    units = w_down.shape[0] * ctx_count

    tokens = hidden_in.shape[2]
    marks = jnp.stack(
        [segment_ids[:, 0], doc_positions[:, 0] // 256, doc_positions[:, 0] % 256], 1
    ).reshape(2, 1, -1)
    marks = jnp.pad(marks, ((0, 0), (0, 15), (0, width - 3 * tokens))).astype(low)
    x_came, x_kept = spread(jnp.concatenate([hidden_in[:, 0], marks], 1))

    head_few = head_gains.shape[0]
    gains = jnp.stack([attn_gain, ffn_gain, jnp.pad(head_gains, (0, rows - head_few))])
    gains = jnp.pad(gains, ((0, rows - 3), (0, 128 - rows)))
    key_value = jnp.stack([w_key.reshape(rows, -1, 2, head), w_value.reshape(rows, -1, 2, head)], 3)
    parities = [
        jnp.concatenate(
            [
                w_query.reshape(rows, -1, 2, group * head)[:, :, which].reshape(rows, -1),
                key_value[:, :, which].reshape(rows, -1),
                gains,
            ],
            1,
        )
        for which in range(2)
    ]
    inner = parities[0].shape[1]

    tops = w_gate.shape[1] // units // 4

    def of_member(which):
        return [
            jnp.concatenate(
                [w[:, (top * 4 + which) * units : (top * 4 + which + 1) * units] for top in range(tops)],
                1,
            )
            for w in (w_gate, w_up)
        ]

    def related(zero, one, two, three):
        near, far = choose(side, zero, two), choose(side, two, zero)
        near_far, far_far = choose(side, one, three), choose(side, three, one)
        return (
            choose(core, near, near_far),
            choose(core, far, far_far),
            choose(core, near_far, near),
            choose(core, far_far, far),
        )

    members = [of_member(which) for which in range(4)]
    gate_of = related(*[member[0] for member in members])
    up_of = related(*[member[1] for member in members])
    from_core = flip(
        joined(choose(core, parities[1], parities[0]), gate_of[2], up_of[2], gate_of[3], up_of[3]),
        CORE,
    )
    block = joined(
        choose(core, parities[0], from_core[0]),
        choose(core, from_core[0], parities[1]),
        jnp.pad(w_out, ((0, 0), (0, inner - width))),
    )
    from_side = flip(joined(gate_of[1], up_of[1], from_core[3], from_core[4]), SIDE)
    blocks = [block]
    for step in range(ctx_count - 1):
        blocks.append(spin(blocks[-1]))

    def across(pair):
        return [pair, flip(pair, SIDE), flip(pair, HIGH), flip(pair, SIDE | HIGH)]

    early = across(jnp.concatenate(blocks[:2], 0))
    blocks[3], w_down_late, *early = hold(blocks[3], w_down, *early)
    late = across(jnp.concatenate(blocks[2:], 0))
    block_ffn = unit_block(
        [side * 2 + core, side * 2 + 1 - core, 2 - side * 2 + core, 2 - side * 2 + 1 - core],
        joined(gate_of[0], up_of[0]), from_core, from_side, w_down_late,
    )
    block_ffn, *x_came = hold(block_ffn, *x_came)
    ffn_blocks = [block_ffn, spin(block_ffn)]
    x_half = order(ctx // 2, *settled(x_came, x_kept))
    x_other = flip(x_half, CORE)
    block_ffn, out_late, *late = hold(block_ffn, out_grad, *late)
    ffn_far = [flip(block_ffn, HIGH)]
    df_came, df_kept = spread(out_late[:, 0])
    pieces = [
        pair[3 * part : 3 * part + 3] for pairs in (early, late) for part in range(2) for pair in pairs
    ]

    slots = []
    for step in range(ctx_count):
        place = (ctx - step) % ctx_count
        for far in range(4):
            up = 1 - high if far >= 2 else high
            across_to = 1 - side if far % 2 == 1 else side
            chip = up * 2 + across_to
            slots += [(chip * 2 + c) * ctx_count + place for c in range(2)]
            slots += [chip * ctx_count + place]
    w_in, w_mine = placed(pieces, (0, 0, 1), slots, (8 * ctx_count, 4 * ctx_count))
    w_in, w_mine = w_in.reshape(-1, inner), w_mine.reshape(-1, inner)[:, :width]
    w_in, w_mine, x_other = hold(w_in, w_mine, x_other)
    w_theirs = flip(w_mine, CORE)
    features = inner - 128
    gains_all = w_in[:, features:].reshape(-1, rows, 128)[:, :3, :rows].astype(full)
    w_in = w_in[:, :features]
    attn_gain_all, ffn_gain_all = gains_all[:, 0].reshape(-1), gains_all[:, 1].reshape(-1)
    head_gains_all = gains_all[:, 2, :head_few].reshape(2, head, 1)

    x_all = order(core, x_half, x_other)
    marks = x_all[:, :, tokens, : 3 * tokens].reshape(-1, 3, tokens)
    x_all, x_half = x_all[:, :, :tokens].reshape(-1, width), x_half[:, :tokens].reshape(-1, width)
    segments = marks[:, 0].reshape(-1).astype(jnp.int32)
    places = (256.0 * marks[:, 1].astype(full) + marks[:, 2].astype(full)).reshape(-1)
    normed, _, _ = norm_forward(x_all.astype(full), attn_gain_all)
    a_low = normed.astype(low)
    raw = lax.dot_general(w_in, a_low, (((0,), (1,)), ((), ())), preferred_element_type=full)
    raw, ffn_blocks[1], ffn_far[0], w_theirs = hold(raw, ffn_blocks[1], ffn_far[0], w_theirs)
    ffn_blocks.append(spin(ffn_blocks[1]))
    ffn_far.append(flip(ffn_blocks[1], HIGH))
    freq = THETA ** (-(jnp.arange(head // 2, dtype=full) * 2.0 / head))
    turn = freq[:, None] * places[None, :]
    cosine, sine = jnp.cos(turn), jnp.sin(turn)
    attended, logs, turned_q, turned_kv = attend(
        raw, cosine, sine, head_gains_all, segments, kv_own, head, 256
    )
    attended_low = attended.astype(low)
    o_theirs = flip(half_of(1 - core, attended_low, 1), CORE)
    o_theirs, ffn_blocks[2], ffn_far[1], *df_came = hold(
        o_theirs, ffn_blocks[2], ffn_far[1], *df_came
    )
    df = order(ctx // 2, *settled(df_came, df_kept)).reshape(-1, width)
    df_side, df_core = flip(df, SIDE), flip(df, CORE)
    ffn_blocks.append(spin(ffn_blocks[2]))
    ffn_far.append(flip(ffn_blocks[2], HIGH))
    hidden = (
        x_half.astype(full)
        + left_trans(half_of(core, attended_low, 1), w_mine)
        + left_trans(o_theirs, w_theirs)
    )
    normed_two, h_unit, h_factor = norm_forward(hidden, ffn_gain_all)
    b_own = swap_halves(high, normed_two.astype(low), 1)
    b_own, df_core, ffn_blocks[3], ffn_far[2] = hold(b_own, df_core, ffn_blocks[3], ffn_far[2])
    b_side, b_core = flip(b_own, SIDE), flip(b_own, CORE)
    ffn_far.append(flip(ffn_blocks[3], HIGH))
    b_side, b_core, df_side, ffn_far[3] = hold(b_side, b_core, df_side, ffn_far[3])
    b_both, df_both = flip(b_side, CORE), flip(df_side, CORE)

    units_of = functools.partial(
        feed_forward,
        [(ctx - step) % ctx_count for step in range(ctx_count)] + [high],
        [block for pair in zip(ffn_blocks, ffn_far) for block in pair],
        rows,
    )
    *left, db_side, db_both, out_side, out_both = units_of(
        [b_side, b_both], [df_side, df_both], 256, 2, []
    )
    got_both, got_out_both = flip(db_both, CORE), flip(out_both, CORE)
    db_far = total_low(db_side, got_both)
    block_side = total_low(out_side, got_out_both)
    db_far, block_side, b_own, b_core = hold(db_far, block_side, b_own, b_core)
    got_side = flip(db_far, SIDE)
    act, d_pre, team_b, team_df, db_own, db_core, out_own, out_core = units_of(
        [b_own, b_core], [df, df_core], 256, 0, left
    )
    db_core, d_pre, act, block_side, got_side = hold(db_core, d_pre, act, block_side, got_side)
    got_core, got_out_core, got_block = flip(db_core, CORE), flip(out_core, CORE), flip(block_side, SIDE)

    def behind(step):
        return (ctx - 1 - step) % ctx_count

    g_down = left_trans(act, team_df).astype(low)
    g_down, team_b, got_core = hold(g_down, team_b, got_core)

    db = db_own.astype(full) + got_core.astype(full) + got_side.astype(full)
    db = swap_halves(high, db, 1)
    d_hidden, ffn_terms = norm_backward(db, h_unit, h_factor, ffn_gain_all)
    d_hidden = df.astype(full) + d_hidden
    dz = d_hidden.astype(low)
    dz, team_b = hold(dz, team_b)
    dz_other = flip(dz, CORE)
    g_ffn = left_trans(team_b, d_pre).astype(low)
    g_ffn, dz_other = hold(g_ffn, dz_other)
    dz_all = order(core, dz, dz_other).reshape(-1, width)
    d_attended = right_trans(w_mine, dz_all).astype(low)
    g_out = matmul(attended_low, dz_all).astype(low).reshape(2, 2, ctx_count, -1, width)
    g_out = jnp.stack([pick(g_out, behind(step), 2) for step in range(ctx_count)], 2)
    terms = spread_units(
        [behind(step) for step in range(ctx_count)] + [high], g_ffn, g_down, rows, ctx_count
    )
    *terms, d_attended, g_out, got_out_core, got_block = hold(
        *terms, d_attended, g_out, got_out_core, got_block
    )
    block_out = hidden + out_own.astype(full) + got_out_core.astype(full) + got_block.astype(full)
    block_came, block_kept = unspread(block_out.astype(low).reshape(2, -1, width))
    near_terms = terms[:ctx_count]
    far_got = [flip(term, HIGH) for term in terms[ctx_count:-1]]

    def side_square(array):
        near = jnp.where(side == 0, array[:, 0], array[:, 1])
        far = jnp.where(side == 0, array[:, 1], array[:, 0])
        near = joined(pick(near, high), pick(near, 1 - high))
        return near, flip(joined(pick(far, high), pick(far, 1 - high)), SIDE)

    def high_square(near, got):
        sums = near.astype(full) + got.astype(full)
        return sums[0], flip(sums[1].astype(low), HIGH)

    def total(terms):
        return functools.reduce(lambda a, b: a + b, [term.astype(full) for term in terms])

    back = functools.partial(
        attend_back, raw, turned_q, turned_kv, attended=attended, logs=logs, cosine=cosine,
        sine=sine, gains=head_gains_all, segments=segments, kv_own=kv_own, head=head, block=256
    )
    out_near, out_got = side_square(g_out)
    dq_one, dkv_one, g_heads_one = back(grad=d_attended, begin=0, count=kv_own // 2)
    dq_one, out_got, far_got[0], d_attended, *block_came = hold(
        dq_one, out_got, far_got[0], d_attended, *block_came
    )
    unit_total = total_low(near_terms[0], far_got[0])
    out_near, out_got = high_square(out_near, out_got)
    d_attended, unit_total = hold(d_attended, unit_total)
    unit_ring = spin(unit_total)
    dq_two, dkv_two, g_heads_two = back(
        grad=d_attended, begin=kv_own // 2, count=kv_own - kv_own // 2
    )
    g_heads = g_heads_one + g_heads_two
    dq_two, unit_ring, far_got[1], out_got, last_term = hold(
        dq_two, unit_ring, far_got[1], out_got, terms[-1]
    )
    far_got.append(flip(last_term, HIGH))
    unit_total = total_low(unit_ring, total_low(near_terms[1], far_got[1]))
    dq_two, unit_total = hold(dq_two, unit_total)
    unit_ring = spin(unit_total)
    d_raw = jnp.concatenate([dq_one, dq_two, dkv_one, dkv_two], 1)
    d_theirs = right_trans(half_of(1 - core, d_raw, 0), w_in).astype(low)
    d_theirs, d_raw = hold(d_theirs, d_raw)
    d_from = flip(d_theirs, CORE)
    d_inner = right_trans(half_of(core, d_raw, 0), w_in)
    d_inner, d_raw = hold(d_inner, d_raw)
    g_in = left_trans(a_low, d_raw).astype(low).reshape(2, 2, 2, ctx_count, rows, features)
    g_in, d_inner, d_from = hold(g_in, d_inner, d_from)
    d_inner = d_inner + d_from.astype(full)
    _, x_unit, x_factor = norm_forward(x_half.astype(full), attn_gain_all)
    d_input, attn_terms = norm_backward(d_inner, x_unit, x_factor, attn_gain_all)
    in_grad = (d_hidden + d_input).astype(low)

    g_gains = jnp.concatenate(
        [
            jnp.sum(attn_terms, 0).reshape(2, 2, 2, ctx_count, rows),
            jnp.sum(ffn_terms, 0).reshape(2, 2, 2, ctx_count, rows),
            g_heads.reshape(2, 2, 2, ctx_count, head_few),
        ],
        -1,
    ).astype(low)
    blank = ((0, 0), (0, 0), (0, 0), (0, 14), (0, width - g_gains.shape[-1]))
    g_gains = jnp.pad(jnp.moveaxis(g_gains, 2, 3), blank)
    g_in = jnp.moveaxis(g_in, 3, 2).reshape(2, 2, ctx_count, 2 * rows, features)
    g_in = jnp.concatenate([g_in, g_gains], 3)
    g_in = jnp.stack([pick(g_in, behind(step), 2) for step in range(ctx_count)], 2)
    g_in, in_grad = hold(g_in, in_grad)
    early_near, early_got = side_square(g_in[:, :, :2])
    late_near, late_got = side_square(g_in[:, :, 2:])
    in_came, in_kept = unspread(in_grad.reshape(2, -1, width))
    out_total = out_near + out_got.astype(full)
    unit_total = total_low(unit_ring, total_low(near_terms[2], far_got[2]))
    unit_ring = spin(unit_total)
    early_near, early_got = high_square(early_near, early_got)
    early_got, late_got, unit_ring, far_got[3] = hold(early_got, late_got, unit_ring, far_got[3])
    unit_total = total_low(unit_ring, total_low(near_terms[3], far_got[3]))
    ffn_total = jnp.concatenate(
        [unit_total[: 4 * rows], unit_total[4 * rows : 8 * rows]], 1
    ).reshape(2, 2, rows, -1)
    g_down = unit_total[8 * rows :, :width]

    found = [
        pick(pick(ffn_total, side), core),
        flip(pick(pick(ffn_total, side), 1 - core), CORE),
        flip(pick(pick(ffn_total, 1 - side), core), SIDE),
        flip(pick(pick(ffn_total, 1 - side), 1 - core), SIDE | CORE),
    ]
    late_near, late_got = high_square(late_near, late_got)

    def terms_of(near, got, first):
        terms = near + got.astype(full)
        return [jnp.concatenate([terms[at], out_total[first + at]], 0) for at in range(2)]

    in_terms = terms_of(early_near, early_got, 0)
    in_ring = spin(in_terms[0].astype(low))
    in_ring, late_got = hold(in_ring, late_got)
    in_terms += terms_of(late_near, late_got, 2)
    in_ring = spin((in_ring.astype(full) + in_terms[1]).astype(low))
    in_ring, *found = hold(in_ring, *found)
    in_ring = spin((in_ring.astype(full) + in_terms[2]).astype(low))
    in_ring, *in_came = hold(in_ring, *in_came)
    found = related(*found)
    found = (found[0], found[2], found[1], found[3])

    def to_columns(first):
        return jnp.concatenate(
            [
                found[which][:, (first + top) * units : (first + top + 1) * units].astype(full)
                for top in range(tops)
                for which in range(4)
            ],
            1,
        )

    g_gate, g_up = to_columns(0), to_columns(tops)

    in_sum = in_ring.astype(full) + in_terms[3]
    g_in, g_out = in_sum[: 2 * rows].astype(low).reshape(2, rows, width), in_sum[2 * rows + 16 :]
    g_gains = in_sum[2 * rows : 2 * rows + 16]
    g_in, *block_came = hold(g_in, *block_came)
    in_grad = order(ctx % 2, *settled(in_came, in_kept))
    block_out = order(ctx % 2, *settled(block_came, block_kept))
    own = pick(g_in, core).astype(full)
    got = flip(jnp.concatenate([pick(g_in, 1 - core), g_gains.astype(low)], 0), CORE).astype(full)
    g_gains = pick(g_gains[:2] + got[rows : rows + 2], core)
    got = got[:rows]
    even, odd = choose(core, own, got), choose(core, got, own)
    first = group * head * kv_own

    def mixed(start, stop, step, size):
        return jnp.concatenate(
            [part[:, at : at + size] for at in range(start, stop, step) for part in (even, odd)], 1
        )

    return (
        block_out[:, None],
        in_grad[:, None],
        g_gains[:rows],
        g_gains[2 * rows : 2 * rows + head_few],
        mixed(0, first, group * head, group * head),
        mixed(first, features, 2 * head, head),
        mixed(first + head, features, 2 * head, head),
        g_out,
        g_gains[rows : 2 * rows],
        g_gate,
        g_up,
        g_down.astype(full),
    )


def solution(mesh):
    placed = (
        P(None, "dp", "ctx", None),
        P(None, "dp", "ctx", None),
        P(None, "dp", "ctx"),
        P(None, "dp", "ctx"),
        P(("dp", "ctx")),
        P(("dp", "ctx")),
        P(("dp", "ctx"), None),
        P(("dp", "ctx"), None),
        P(("dp", "ctx"), None),
        P(("dp", "ctx"), None),
        P(("dp", "ctx")),
        P(("dp", "ctx"), None),
        P(("dp", "ctx"), None),
        P(("dp", "ctx"), None),
    )
    fits = mesh.shape["dp"] == 8 and mesh.shape["ctx"] == 4
    return jax.shard_map(
        on_device_fast if fits else on_device,
        mesh=mesh,
        in_specs=placed,
        out_specs=(
            P(None, "dp", "ctx", None),
            P(None, "dp", "ctx", None),
            P(("dp", "ctx")),
            P(("dp", "ctx")),
            P(("dp", "ctx"), None),
            P(("dp", "ctx"), None),
            P(("dp", "ctx"), None),
            P(("dp", "ctx"), None),
            P(("dp", "ctx")),
            P(("dp", "ctx"), None),
            P(("dp", "ctx"), None),
            P(("dp", "ctx"), None),
        ),
        check_vma=False,
    )
```

```python
import functools

import jax
import jax.numpy as jnp
from jax import lax
from jax.experimental import pallas as pl
from jax.experimental.pallas import tpu as pltpu
from jax.sharding import PartitionSpec as P

EPS = 1e-05
THETA = 1000000.0


def matmul(left, right):
    return jnp.dot(left, right, preferred_element_type=jnp.float32)


def left_trans(left, right):
    return lax.dot_general(
        left, right, (((0,), (0,)), ((), ())), preferred_element_type=jnp.float32
    )


def right_trans(left, right):
    return lax.dot_general(
        left, right, (((1,), (1,)), ((), ())), preferred_element_type=jnp.float32
    )


def norm_forward(values, gain):
    factor = lax.rsqrt(jnp.mean(values * values, -1, keepdims=True) + EPS)
    unit = values * factor
    return (unit * gain, unit, factor)


def norm_backward(incoming, unit, factor, gain):
    scaled = incoming * gain
    result = factor * (scaled - unit * jnp.mean(scaled * unit, -1, keepdims=True))
    return (result, incoming * unit)


def angles(places, half):
    freq = THETA ** (-(jnp.arange(half, dtype=jnp.float32) * 2.0 / (2 * half)))
    turn = places.astype(jnp.float32)[:, None] * freq[None, :]
    return (jnp.cos(turn)[:, None, :], jnp.sin(turn)[:, None, :])


def rotate(values, cosine, sine, sign):
    half = values.shape[-1] // 2
    first = values[..., :half]
    second = values[..., half:]
    return jnp.concatenate(
        [first * cosine - sign * second * sine, second * cosine + sign * first * sine], -1
    )


def fetch_weights(shards):
    return (
        lax.all_gather(shards[0], ("dp", "ctx"), axis=0, tiled=True),
        lax.all_gather(shards[1], ("dp", "ctx"), axis=0, tiled=True),
        lax.all_gather(shards[2], ("dp", "ctx"), axis=0, tiled=True),
        lax.all_gather(shards[3], ("dp", "ctx"), axis=0, tiled=True),
        lax.all_gather(shards[4], ("dp", "ctx"), axis=0, tiled=True),
        lax.all_gather(shards[5], ("dp", "ctx"), axis=0, tiled=True),
        lax.all_gather(shards[6], ("dp", "ctx"), axis=0, tiled=True),
        lax.all_gather(shards[7], ("dp", "ctx"), axis=0, tiled=True),
        lax.all_gather(shards[8], ("dp", "ctx"), axis=0, tiled=True),
        lax.all_gather(shards[9], ("dp", "ctx"), axis=0, tiled=True),
    )


def fetch_again(shards):
    return (
        lax.all_gather(shards[0], ("dp", "ctx"), axis=0, tiled=True),
        lax.all_gather(shards[1], ("dp", "ctx"), axis=0, tiled=True),
        lax.all_gather(shards[2], ("dp", "ctx"), axis=0, tiled=True),
        lax.all_gather(shards[3], ("dp", "ctx"), axis=0, tiled=True),
        lax.all_gather(shards[4], ("dp", "ctx"), axis=0, tiled=True),
        lax.all_gather(shards[5], ("dp", "ctx"), axis=0, tiled=True),
        lax.all_gather(shards[6], ("dp", "ctx"), axis=0, tiled=True),
        lax.all_gather(shards[7], ("dp", "ctx"), axis=0, tiled=True),
        lax.all_gather(shards[8], ("dp", "ctx"), axis=0, tiled=True),
        lax.all_gather(shards[9], ("dp", "ctx"), axis=0, tiled=True),
    )


def attention_forward(query_low, key_low, value_low, segments, again):
    rows, heads, head = query_low.shape
    kv_heads = key_low.shape[1] // head
    group = heads // kv_heads
    scale = head ** (-0.5)
    grouped = query_low.reshape(rows, kv_heads, group, head)
    query_index = lax.axis_index("ctx") * rows + jnp.arange(rows, dtype=jnp.int32)

    def visit(carry, piece):
        highest, total, summed = carry
        key_piece, value_piece, segment_piece = piece
        width = key_piece.shape[0]
        key_heads = key_piece.reshape(width, kv_heads, head)
        value_heads = value_piece.reshape(width, kv_heads, head)
        scores = (
            jnp.einsum("qkgd,skd->kgqs", grouped, key_heads, preferred_element_type=jnp.float32)
            * scale
        )
        key_index = jnp.arange(width, dtype=jnp.int32)
        allowed = (segments[:, None] == segment_piece[None, :]) & (
            query_index[:, None] >= key_index[None, :]
        )
        scores = jnp.where(allowed, scores, -1e30)
        peak = jnp.maximum(highest, jnp.max(scores, -1))
        weight = jnp.where(allowed, jnp.exp(scores - peak[..., None]), 0.0)
        total = jnp.sum(weight, -1)
        summed = jnp.einsum(
            "kgqs,skd->qkgd",
            weight.astype(jnp.bfloat16),
            value_heads,
            preferred_element_type=jnp.float32,
        )
        return (peak, total, summed)

    initial = (
        jnp.full((kv_heads, group, rows), -1e30, jnp.float32),
        jnp.zeros((kv_heads, group, rows), jnp.float32),
        jnp.zeros((rows, kv_heads, group, head), jnp.float32),
    )
    if again:
        highest, total, summed = visit(
            initial,
            (
                lax.all_gather(key_low, "ctx", axis=0, tiled=True),
                lax.all_gather(value_low, "ctx", axis=0, tiled=True),
                lax.all_gather(segments, "ctx", axis=0, tiled=True),
            ),
        )
    else:
        highest, total, summed = visit(
            initial,
            (
                lax.all_gather(key_low, "ctx", axis=0, tiled=True),
                lax.all_gather(value_low, "ctx", axis=0, tiled=True),
                lax.all_gather(segments, "ctx", axis=0, tiled=True),
            ),
        )
    attended = (summed / jnp.transpose(total, (2, 0, 1))[..., None]).reshape(rows, heads, head)
    return (attended, highest + jnp.log(total))


def forward(values_row, segments, places, weights, again):
    attn_gain, head_gains, w_query, w_key, w_value, w_out, ffn_gain, w_gate, w_up, w_down = weights
    rows = values_row.shape[0]
    head = head_gains.shape[0] // 2
    heads = w_query.shape[1] // head
    kv_heads = w_key.shape[1] // head
    gains = head_gains.astype(jnp.float32)
    state = {}
    state["values"] = values_row.astype(jnp.float32)
    normed, state["x_unit"], state["x_factor"] = norm_forward(
        state["values"], attn_gain.astype(jnp.float32)
    )
    state["a_low"] = normed.astype(jnp.bfloat16)
    query = matmul(state["a_low"], w_query).reshape(rows, heads, head)
    keys = matmul(state["a_low"], w_key).reshape(rows, kv_heads, head)
    state["value_low"] = matmul(state["a_low"], w_value).astype(jnp.bfloat16)
    state["cosine"], state["sine"] = angles(places, head // 2)
    query_normed, state["q_unit"], state["q_factor"] = norm_forward(query, gains[:head])
    key_normed, state["k_unit"], state["k_factor"] = norm_forward(keys, gains[head:])
    state["query_low"] = rotate(query_normed, state["cosine"], state["sine"], 1.0).astype(
        jnp.bfloat16
    )
    state["key_low"] = (
        rotate(key_normed, state["cosine"], state["sine"], 1.0)
        .astype(jnp.bfloat16)
        .reshape(rows, kv_heads * head)
    )
    state["attended"], state["log_total"] = attention_forward(
        state["query_low"], state["key_low"], state["value_low"], segments, again
    )
    state["attended_low"] = state["attended"].astype(jnp.bfloat16).reshape(rows, heads * head)
    hidden = state["values"] + matmul(state["attended_low"], w_out)
    normed_two, state["h_unit"], state["h_factor"] = norm_forward(
        hidden, ffn_gain.astype(jnp.float32)
    )
    state["b_low"] = normed_two.astype(jnp.bfloat16)
    state["gate"] = matmul(state["b_low"], w_gate)
    state["upper"] = matmul(state["b_low"], w_up)
    state["act_low"] = (jax.nn.silu(state["gate"]) * state["upper"]).astype(jnp.bfloat16)
    state["output"] = hidden + matmul(state["act_low"], w_down)
    return state


def backward(grad_row, segments, weights, state):
    attn_gain, head_gains, w_query, w_key, w_value, w_out, ffn_gain, w_gate, w_up, w_down = weights
    query_low = state["query_low"]
    rows, heads, head = query_low.shape
    kv_heads = state["key_low"].shape[1] // head
    group = heads // kv_heads
    scale = head ** (-0.5)
    gains = head_gains.astype(jnp.float32)
    incoming = grad_row.astype(jnp.float32)
    down_low = incoming.astype(jnp.bfloat16)
    g_down = left_trans(state["act_low"], down_low)
    d_act = right_trans(down_low, w_down)
    sigma = jax.nn.sigmoid(state["gate"])
    d_upper = (d_act * state["gate"] * sigma).astype(jnp.bfloat16)
    d_gate = (d_act * state["upper"] * sigma * (1.0 + state["gate"] * (1.0 - sigma))).astype(
        jnp.bfloat16
    )
    g_gate = left_trans(state["b_low"], d_gate)
    g_up = left_trans(state["b_low"], d_upper)
    d_normed = right_trans(d_gate, w_gate) + right_trans(d_upper, w_up)
    d_hidden, terms = norm_backward(
        d_normed, state["h_unit"], state["h_factor"], ffn_gain.astype(jnp.float32)
    )
    g_ffn = jnp.sum(terms, 0)
    d_hidden = incoming + d_hidden
    branch_low = d_hidden.astype(jnp.bfloat16)
    g_out = left_trans(state["attended_low"], branch_low)
    d_attended = (
        right_trans(branch_low, w_out).astype(jnp.bfloat16).reshape(rows, kv_heads, group, head)
    )
    delta = jnp.sum(
        d_attended.astype(jnp.float32) * state["attended"].reshape(rows, kv_heads, group, head), -1
    )
    delta = jnp.transpose(delta, (1, 2, 0))
    log_total = state["log_total"]
    grouped = query_low.reshape(rows, kv_heads, group, head)
    query_index = lax.axis_index("ctx") * rows + jnp.arange(rows, dtype=jnp.int32)
    key_piece = lax.all_gather(state["key_low"], "ctx", axis=0, tiled=True)
    value_piece = lax.all_gather(state["value_low"], "ctx", axis=0, tiled=True)
    segment_piece = lax.all_gather(segments, "ctx", axis=0, tiled=True)
    width = key_piece.shape[0]
    key_heads = key_piece.reshape(width, kv_heads, head)
    value_heads = value_piece.reshape(width, kv_heads, head)
    scores = (
        jnp.einsum("qkgd,skd->kgqs", grouped, key_heads, preferred_element_type=jnp.float32) * scale
    )
    key_index = jnp.arange(width, dtype=jnp.int32)
    allowed = (segments[:, None] == segment_piece[None, :]) & (
        query_index[:, None] >= key_index[None, :]
    )
    probs = jnp.where(allowed, jnp.exp(scores - log_total[..., None]), 0.0)
    d_probs = jnp.einsum(
        "qkgd,skd->kgqs", d_attended, value_heads, preferred_element_type=jnp.float32
    )
    d_scores = (probs * (d_probs - delta[..., None])).astype(jnp.bfloat16)
    d_query = (
        jnp.einsum("kgqs,skd->qkgd", d_scores, key_heads, preferred_element_type=jnp.float32)
        * scale
    )
    key_part = (
        jnp.einsum("kgqs,qkgd->skd", d_scores, grouped, preferred_element_type=jnp.float32) * scale
    )
    value_part = jnp.einsum(
        "kgqs,qkgd->skd", probs.astype(jnp.bfloat16), d_attended, preferred_element_type=jnp.float32
    )
    d_keys = key_part.reshape(width, kv_heads * head)
    d_values = value_part.reshape(width, kv_heads * head)
    d_query, d_keys_all, d_values_all = (d_query, d_keys, d_values)
    d_keys, d_values = (
        lax.psum_scatter(
            d_keys_all.astype(jnp.bfloat16), "ctx", scatter_dimension=0, tiled=True
        ).astype(jnp.float32),
        lax.psum_scatter(
            d_values_all.astype(jnp.bfloat16), "ctx", scatter_dimension=0, tiled=True
        ).astype(jnp.float32),
    )
    d_query = rotate(d_query.reshape(rows, heads, head), state["cosine"], state["sine"], -1.0)
    d_query, query_terms = norm_backward(d_query, state["q_unit"], state["q_factor"], gains[:head])
    d_keys = rotate(d_keys.reshape(rows, kv_heads, head), state["cosine"], state["sine"], -1.0)
    d_keys, key_terms = norm_backward(d_keys, state["k_unit"], state["k_factor"], gains[head:])
    g_heads = jnp.concatenate([jnp.sum(query_terms, (0, 1)), jnp.sum(key_terms, (0, 1))])
    query_grad_low = d_query.astype(jnp.bfloat16).reshape(rows, heads * head)
    key_grad_low = d_keys.astype(jnp.bfloat16).reshape(rows, kv_heads * head)
    value_grad_low = d_values.astype(jnp.bfloat16)
    g_query = left_trans(state["a_low"], query_grad_low)
    g_key = left_trans(state["a_low"], key_grad_low)
    g_value = left_trans(state["a_low"], value_grad_low)
    d_inner = (
        right_trans(query_grad_low, w_query)
        + right_trans(key_grad_low, w_key)
        + right_trans(value_grad_low, w_value)
    )
    d_input, terms = norm_backward(
        d_inner, state["x_unit"], state["x_factor"], attn_gain.astype(jnp.float32)
    )
    g_attn = jnp.sum(terms, 0)
    in_grad = (d_hidden + d_input).astype(jnp.bfloat16)
    return (in_grad, (g_attn, g_heads, g_query, g_key, g_value, g_out, g_ffn, g_gate, g_up, g_down))


def on_device(
    hidden_in,
    out_grad,
    segment_ids,
    doc_positions,
    attn_gain,
    head_gains,
    w_query,
    w_key,
    w_value,
    w_out,
    ffn_gain,
    w_gate,
    w_up,
    w_down,
):
    shards = (attn_gain, head_gains, w_query, w_key, w_value, w_out, ffn_gain, w_gate, w_up, w_down)
    micro = hidden_in.shape[0]
    outputs = []
    for micro_index in range(micro):
        weights = fetch_weights(shards)
        state = forward(
            hidden_in[micro_index, 0],
            segment_ids[micro_index, 0],
            doc_positions[micro_index, 0],
            weights,
            False,
        )
        outputs.append(state["output"].astype(jnp.bfloat16))
    in_grads = []
    totals = None
    for micro_index in range(micro):
        weights = fetch_again(shards)
        state = forward(
            hidden_in[micro_index, 0],
            segment_ids[micro_index, 0],
            doc_positions[micro_index, 0],
            weights,
            True,
        )
        in_grad, grads = backward(
            out_grad[micro_index, 0], segment_ids[micro_index, 0], weights, state
        )
        in_grads.append(in_grad)
        if totals is None:
            totals = grads
        else:
            totals = tuple((left + right for left, right in zip(totals, grads)))
    totals = lax.psum_scatter(totals, ("dp", "ctx"), scatter_dimension=0, tiled=True)
    block_out = jnp.stack(outputs)[:, None]
    input_grads = jnp.stack(in_grads)[:, None]
    return (
        block_out,
        input_grads,
        totals[0],
        totals[1],
        totals[2],
        totals[3],
        totals[4],
        totals[5],
        totals[6],
        totals[7],
        totals[8],
        totals[9],
    )


CORE, SIDE, HIGH = 1, 2, 4


def flip(array, bits):
    count = lax.axis_size("dp")
    return lax.ppermute(array, "dp", [(i, i ^ bits) for i in range(count)])


def spin(array):
    count = lax.axis_size("ctx")
    return lax.ppermute(array, "ctx", [(i, (i + 1) % count) for i in range(count)])


def hold(*arrays):
    return lax.optimization_barrier(arrays)


def choose(bit, zero, one):
    return jnp.where(bit == 0, zero, one)


def pick(array, index, axis=0):
    return lax.dynamic_index_in_dim(array, index, axis, keepdims=False)


def put(buffer, array, *place):
    index = place + (0,) * (buffer.ndim - len(place))
    shape = (1,) * (buffer.ndim - array.ndim) + array.shape
    return lax.dynamic_update_slice(buffer, array.reshape(shape), index)


def place_kernel(splits, count, slots_ref, *refs):
    pieces, outs = refs[:count], refs[count:]
    at = 0
    for piece in pieces:
        for part in range(len(splits)):
            outs[splits[part]][slots_ref[at]] = piece[part]
            at += 1


def placed(pieces, splits, slots, counts):
    shape = pieces[0].shape
    return pl.pallas_call(
        functools.partial(place_kernel, splits, len(pieces)),
        in_specs=[pl.BlockSpec(memory_space=pltpu.SMEM)]
        + [pl.BlockSpec(memory_space=pltpu.VMEM)] * len(pieces),
        out_specs=[pl.BlockSpec(memory_space=pltpu.VMEM)] * len(counts),
        out_shape=[
            jax.ShapeDtypeStruct((count,) + shape[1:], pieces[0].dtype) for count in counts
        ],
        compiler_params=pltpu.CompilerParams(vmem_limit_bytes=40 * 2**20),
    )(jnp.stack(slots).astype(jnp.int32), *pieces)


def block_kernel(slots_ref, own_ref, core_ref, side_ref, down_ref, out_ref):
    rows = own_ref.shape[1]
    for member, ref, first in ((0, own_ref, 0), (1, core_ref, 1), (2, side_ref, 0), (3, side_ref, 2)):
        for part in range(2):
            start = pl.multiple_of((part * 4 + slots_ref[member]) * rows, rows)
            out_ref[pl.ds(start, rows), :] = ref[first + part]
    out_ref[8 * rows :, : down_ref.shape[1]] = down_ref[...]
    out_ref[8 * rows :, down_ref.shape[1] :] = jnp.zeros_like(
        out_ref[8 * rows :, down_ref.shape[1] :]
    )


def unit_block(slots, own, from_core, from_side, down):
    rows, columns = own.shape[1:]
    shape = (8 * rows + down.shape[0], columns)
    return pl.pallas_call(
        block_kernel,
        in_specs=[pl.BlockSpec(memory_space=pltpu.SMEM)]
        + [pl.BlockSpec(memory_space=pltpu.VMEM)] * 4,
        out_specs=pl.BlockSpec(memory_space=pltpu.VMEM),
        out_shape=jax.ShapeDtypeStruct(shape, own.dtype),
    )(jnp.stack(slots).astype(jnp.int32), own, from_core, from_side, down)


def unit_kernel(chunk, ctx_count, tiles, rows, slots_ref, *refs):
    pieces, refs = refs[: 2 * ctx_count], refs[2 * ctx_count :]
    b_refs, df_refs = refs[:2], refs[2:4]
    act_ref, pre_ref, all_b_ref, all_df_ref = refs[-12:-8]
    db_refs, out_refs, (w_ref, down_ref, b_ref, df_ref) = refs[-8:-6], refs[-6:-4], refs[-4:]
    mid = pieces[0].shape[1]
    width = down_ref.shape[1]
    down_rows = pieces[0].shape[0] - 8 * rows
    tile = pl.program_id(0)

    @pl.when(tile == 0)
    def _():
        high = slots_ref[ctx_count]
        for step in range(ctx_count):
            place = slots_ref[step]
            for far in range(2):
                piece = pieces[2 * step + far]
                for member in range(4):
                    first = ((far * 4 + member) * ctx_count + place) * rows
                    to = pl.ds(pl.multiple_of(first, rows), rows)
                    for first, last in ((0, chunk),):
                        middle = first + last
                        w_ref[to, 2 * first : middle] = piece[
                            member * rows : (member + 1) * rows, first:last
                        ]
                        w_ref[to, middle : 2 * last] = piece[
                            (4 + member) * rows : (5 + member) * rows, first:last
                        ]
                half = high if far == 0 else 1 - high
                first = (half * ctx_count + place) * down_rows
                to = pl.ds(pl.multiple_of(first, 16), down_rows)
                down_ref[to, :] = piece[8 * rows :, :width]

    for which in range(2):

        @pl.when(tile // tiles == which)
        def _(which=which):
            b_ref[...] = b_refs[which][...]
            df_ref[...] = df_refs[which][...]

    b, df = b_ref[...], df_ref[...]
    all_b_ref[...] = b
    all_df_ref[...] = df
    db, out = 0.0, 0.0
    for first, last in ((0, chunk),):
        here, there = slice(first, last), slice(mid + first, mid + last)
        both = slice(2 * first, 2 * last)
        pre = jnp.dot(b, w_ref[:, both], preferred_element_type=jnp.float32)
        gate, upper = pre[:, : last - first], pre[:, last - first :]
        d_act = nt(df, down_ref[here, :])
        sigma = 1.0 / (1.0 + jnp.exp(-gate))
        silu = gate * sigma
        act = (silu * upper).astype(jnp.bfloat16)
        d_upper = (d_act * silu).astype(jnp.bfloat16)
        d_gate = (d_act * upper * sigma * (1.0 + gate * (1.0 - sigma))).astype(jnp.bfloat16)
        act_ref[:, here] = act
        pre_ref[:, here] = d_gate
        pre_ref[:, there] = d_upper
        db += nt(jnp.concatenate([d_gate, d_upper], 1), w_ref[:, both])
        out += jnp.dot(act, down_ref[here, :], preferred_element_type=jnp.float32)
    for which in range(2):

        @pl.when(tile // tiles == which)
        def _(which=which):
            db_refs[which][...] = db.astype(jnp.bfloat16)
            out_refs[which][...] = out.astype(jnp.bfloat16)


def feed_forward(slots, pieces, rows, b_parts, df_parts, size, begin, left):
    tokens, width = b_parts[0].shape
    mid = pieces[0].shape[1]
    down_rows = pieces[0].shape[0] - 8 * rows
    tiles = tokens // size
    once = lambda array: pl.BlockSpec(
        array.shape, lambda t: (0,) * array.ndim, pipeline_mode=pl.Buffered(1)
    )

    def part(which):
        return pl.BlockSpec((size, width), lambda t: (jnp.clip(t - which * tiles, 0, tiles - 1), 0))

    def tiled(count, first):
        return pl.BlockSpec((size, count), lambda t: (first + t, 0))

    first = begin * tiles
    first_left = 1 + len(pieces) + 4
    full = lambda count: jax.ShapeDtypeStruct((4 * tokens, count), jnp.bfloat16)
    half = jax.ShapeDtypeStruct((tokens, width), jnp.bfloat16)
    return pl.pallas_call(
        functools.partial(unit_kernel, mid, len(pieces) // 2, tiles, rows),
        grid=(2 * tiles,),
        in_specs=[pl.BlockSpec(memory_space=pltpu.SMEM)]
        + [once(array) for array in pieces]
        + [part(which) for which in range(2)] * 2
        + [pl.BlockSpec(memory_space=pl.ANY)] * len(left),
        out_specs=[tiled(mid, first), tiled(2 * mid, first), tiled(width, first), tiled(width, first)]
        + [part(which) for which in range(2)] * 2,
        out_shape=[full(mid), full(2 * mid), full(width), full(width)] + [half] * 4,
        input_output_aliases={first_left + at: at for at in range(len(left))},
        scratch_shapes=[
            pltpu.VMEM((width, 2 * mid), jnp.bfloat16),
            pltpu.VMEM((len(pieces) * down_rows, width), jnp.bfloat16),
            pltpu.VMEM((size, width), jnp.bfloat16),
            pltpu.VMEM((size, width), jnp.bfloat16),
        ],
        compiler_params=pltpu.CompilerParams(vmem_limit_bytes=58 * 2**20),
        cost_estimate=pl.CostEstimate(flops=10 * tokens * mid * width, bytes_accessed=0, transcendentals=0),
    )(jnp.stack(slots).astype(jnp.int32), *pieces, *b_parts, *df_parts, *left)


def spread_kernel(ctx_count, rows, slots_ref, ffn_ref, down_ref, *outs):
    mid = ffn_ref.shape[1] // 2
    width = down_ref.shape[1]
    down_rows = down_ref.shape[0] // (2 * ctx_count)
    high = slots_ref[ctx_count]
    for far in range(2):
        half = high if far == 0 else 1 - high
        for step in range(ctx_count):
            place = slots_ref[step]
            out = outs[far * ctx_count + step]
            for member in range(4):
                first = ((far * 4 + member) * ctx_count + place) * rows
                here = pl.ds(pl.multiple_of(first, rows), rows)
                out[member * rows : (member + 1) * rows, :] = ffn_ref[here, :mid]
                out[(4 + member) * rows : (5 + member) * rows, :] = ffn_ref[here, mid:]
            first = (half * ctx_count + place) * down_rows
            here = pl.ds(pl.multiple_of(first, 16), down_rows)
            out[8 * rows :, :width] = down_ref[here, :]
            out[8 * rows :, width:] = jnp.zeros_like(out[8 * rows :, width:])


def spread_units(slots, ffn, down, rows, ctx_count):
    shape = (8 * rows + down.shape[0] // (2 * ctx_count), ffn.shape[1] // 2)
    return pl.pallas_call(
        functools.partial(spread_kernel, ctx_count, rows),
        in_specs=[pl.BlockSpec(memory_space=pltpu.SMEM)]
        + [pl.BlockSpec(memory_space=pltpu.VMEM)] * 2,
        out_specs=[pl.BlockSpec(memory_space=pltpu.VMEM)] * (2 * ctx_count),
        out_shape=[jax.ShapeDtypeStruct(shape, ffn.dtype)] * (2 * ctx_count),
        compiler_params=pltpu.CompilerParams(vmem_limit_bytes=40 * 2**20),
        cost_estimate=pl.CostEstimate(flops=10**6, bytes_accessed=0, transcendentals=0),
    )(jnp.stack(slots).astype(jnp.int32), ffn, down)


def joined(*arrays):
    buffer = jnp.zeros((len(arrays),) + arrays[0].shape, arrays[0].dtype)
    for at, array in enumerate(arrays):
        buffer = put(buffer, array, at)
    return buffer


def order(bit, own, other):
    buffer = jnp.zeros((2,) + own.shape, own.dtype)
    return put(put(buffer, own, bit), other, 1 - bit)


def swap_halves(bit, array, axis):
    low, high = jnp.split(array, 2, axis)
    return choose(bit, array, jnp.concatenate([high, low], axis))


def half_of(bit, array, axis):
    low, high = jnp.split(array, 2, axis)
    return choose(bit, low, high)


def exchange(array, target, index_of):
    dp_count, ctx_count = lax.axis_size("dp"), lax.axis_size("ctx")
    me = lax.axis_index("dp") * ctx_count + lax.axis_index("ctx")
    came, kept = [], []
    for turn in range(2):
        pairs, stay = [], []
        for dp in range(dp_count):
            for z in range(ctx_count):
                to = target(dp, z, turn)
                if to == (dp, z):
                    stay.append(dp * ctx_count + z)
                else:
                    pairs.append((dp * ctx_count + z, to[0] * ctx_count + to[1]))
        piece = pick(array, index_of(turn))
        came.append(lax.ppermute(piece, ("dp", "ctx"), pairs))
        mine = functools.reduce(jnp.logical_or, [me == which for which in stay]) if stay else None
        kept.append((piece, mine))
    return came, kept


def settled(came, kept):
    return [
        got if mine is None else jnp.where(mine, piece, got)
        for got, (piece, mine) in zip(came, kept)
    ]


def spread(array):
    ctx = lax.axis_index("ctx")

    def target(dp, z, turn):
        return dp // 2 * 2 + z // 2, 2 * ((z + turn) % 2) + dp % 2

    return exchange(array, target, lambda turn: (ctx + turn) % 2)


def unspread(array):
    ctx = lax.axis_index("ctx")

    def target(dp, z, turn):
        return dp // 2 * 2 + z % 2, 2 * (dp % 2) + (z // 2 + turn) % 2

    return exchange(array, target, lambda turn: (ctx // 2 + turn) % 2)


def swap_gather(array, bit_value, bit):
    return order(bit_value, array, flip(array, bit))


def total_low(left, right):
    return (left.astype(jnp.float32) + right.astype(jnp.float32)).astype(jnp.bfloat16)


def nt(left, right):
    return lax.dot_general(
        left, right, (((1,), (1,)), ((), ())), preferred_element_type=jnp.float32
    )


def set_bias(bias_ref, seg_row_ref, seg_col_ref, block):
    size = bias_ref.shape[0]
    for first in range(0, size, block):
        for key in range(0, first + block, block):
            allowed = seg_col_ref[key : key + block, :] == seg_row_ref[:, first : first + block]
            if key == first:
                keys = lax.broadcasted_iota(jnp.int32, (block, block), 0)
                queries = lax.broadcasted_iota(jnp.int32, (block, block), 1)
                allowed = jnp.logical_and(allowed, keys <= queries)
            bias_ref[key : key + block, first : first + block] = jnp.where(allowed, 0.0, -1e30)


def turned(values, gain, cosine, sine):
    half = values.shape[0] // 2
    factor = lax.rsqrt(jnp.mean(values * values, 0, keepdims=True) + EPS)
    normed = values * factor * gain
    first, second = normed[:half], normed[half:]
    return jnp.concatenate([first * cosine - second * sine, second * cosine + first * sine], 0)


def turned_back(incoming, values, gain, cosine, sine):
    half = values.shape[0] // 2
    first, second = incoming[:half], incoming[half:]
    incoming = jnp.concatenate(
        [first * cosine + second * sine, second * cosine - first * sine], 0
    )
    factor = lax.rsqrt(jnp.mean(values * values, 0, keepdims=True) + EPS)
    unit = values * factor
    terms = jnp.sum(incoming * unit, 1, keepdims=True)
    scaled = incoming * gain
    return factor * (scaled - unit * jnp.mean(scaled * unit, 0, keepdims=True)), terms


def forward_kernel(
    block, q_ref, kv_ref, cos_ref, sin_ref, gain_ref, row_ref, col_ref,
    o_ref, log_ref, qr_ref, kvr_ref, bias_ref
):
    head = kv_ref.shape[0] // 2
    size = kv_ref.shape[1]
    scale = head ** (-0.5)

    @pl.when(pl.program_id(0) == 0)
    def _():
        set_bias(bias_ref, row_ref, col_ref, block)

    cosine, sine = cos_ref[...], sin_ref[...]
    keys = turned(kv_ref[:head, :], gain_ref[1], cosine, sine)
    kvr_ref[:head, :] = keys.astype(jnp.bfloat16)
    keys = keys.T.astype(jnp.bfloat16)
    values = kv_ref[head:, :].astype(jnp.bfloat16)
    kvr_ref[head:, :] = values
    for which in range(q_ref.shape[0] // head):
        rows = slice(which * head, (which + 1) * head)
        query = turned(q_ref[rows, :], gain_ref[0], cosine, sine).astype(jnp.bfloat16)
        qr_ref[rows, :] = query
        for first in range(0, size, block):
            here = slice(first, first + block)
            total = jnp.zeros((1, block), jnp.float32)
            summed = jnp.zeros((head, block), jnp.float32)
            for key in range(0, first + block, block):
                there = slice(key, key + block)
                scores = jnp.dot(keys[there], query[:, here], preferred_element_type=jnp.float32)
                weight = jnp.exp(scores * scale + bias_ref[there, here])
                total += jnp.sum(weight, 0, keepdims=True)
                summed += jnp.dot(
                    values[:, there],
                    weight.astype(jnp.bfloat16),
                    preferred_element_type=jnp.float32,
                )
            o_ref[rows, here] = summed / total
            log_ref[0, which : which + 1, here] = jnp.log(total)


def backward_kernel(
    block, q_ref, kv_ref, qr_ref, kvr_ref, do_ref, o_ref, log_ref, cos_ref, sin_ref,
    gain_ref, row_ref, col_ref, dq_ref, dkv_ref, gains_ref, bias_ref, dkey_ref, dvalue_ref
):
    head = kv_ref.shape[0] // 2
    size = kv_ref.shape[1]
    scale = head ** (-0.5)

    @pl.when(pl.program_id(0) == 0)
    def _():
        set_bias(bias_ref, row_ref, col_ref, block)
        gains_ref[...] = jnp.zeros_like(gains_ref)

    cosine, sine = cos_ref[...], sin_ref[...]
    keys_t = kvr_ref[:head, :]
    keys = keys_t.astype(jnp.float32).T.astype(jnp.bfloat16)
    values = kvr_ref[head:, :].astype(jnp.float32).T.astype(jnp.bfloat16)
    dkey_ref[...] = jnp.zeros_like(dkey_ref)
    dvalue_ref[...] = jnp.zeros_like(dvalue_ref)
    found = []
    for which in range(q_ref.shape[0] // head):
        rows = slice(which * head, (which + 1) * head)
        query = qr_ref[rows, :]
        grad = do_ref[rows, :]
        delta = jnp.sum(grad.astype(jnp.float32) * o_ref[rows, :], 0, keepdims=True)
        pieces = []
        for first in range(0, size, block):
            here = slice(first, first + block)
            dquery = jnp.zeros((head, block), jnp.float32)
            for key in range(0, first + block, block):
                there = slice(key, key + block)
                scores = jnp.dot(keys[there], query[:, here], preferred_element_type=jnp.float32)
                probs = jnp.exp(
                    scores * scale + (bias_ref[there, here] - log_ref[0, which : which + 1, here])
                )
                dprobs = jnp.dot(values[there], grad[:, here], preferred_element_type=jnp.float32)
                dscores = (probs * (dprobs - delta[:, here])).astype(jnp.bfloat16)
                dquery += jnp.dot(keys_t[:, there], dscores, preferred_element_type=jnp.float32)
                dkey_ref[:, there] += nt(query[:, here], dscores)
                dvalue_ref[:, there] += nt(grad[:, here], probs.astype(jnp.bfloat16))
            pieces.append(dquery * scale)
        dquery, terms = turned_back(
            jnp.concatenate(pieces, 1), q_ref[rows, :], gain_ref[0], cosine, sine
        )
        found.append(dquery)
        gains_ref[0] += terms
    dq_ref[...] = jnp.concatenate(found, 0).T.astype(jnp.bfloat16)
    dkey, terms = turned_back(dkey_ref[...] * scale, kv_ref[:head, :], gain_ref[1], cosine, sine)
    dkv_ref[...] = jnp.concatenate([dkey, dvalue_ref[...]], 0).T.astype(jnp.bfloat16)
    gains_ref[1] += terms


def whole_spec(*shape):
    return pl.BlockSpec(shape, lambda i: (0,) * len(shape))


def attend(raw, cosine, sine, gains, segments, kv_own, head, block):
    size = raw.shape[1]
    group = raw.shape[0] // head // kv_own - 2
    query = pl.BlockSpec((group * head, size), lambda i: (i, 0))
    kv_at = group * kv_own // 2
    return pl.pallas_call(
        functools.partial(forward_kernel, block),
        grid=(kv_own,),
        in_specs=[
            query,
            pl.BlockSpec((2 * head, size), lambda i: (kv_at + i, 0)),
            whole_spec(head // 2, size),
            whole_spec(head // 2, size),
            whole_spec(2, head, 1),
            whole_spec(1, size),
            whole_spec(size, 1),
        ],
        out_specs=[
            query,
            pl.BlockSpec((1, group, size), lambda i: (i, 0, 0)),
            query,
            pl.BlockSpec((2 * head, size), lambda i: (i, 0)),
        ],
        out_shape=[
            jax.ShapeDtypeStruct((kv_own * group * head, size), jnp.float32),
            jax.ShapeDtypeStruct((kv_own, group, size), jnp.float32),
            jax.ShapeDtypeStruct((kv_own * group * head, size), jnp.bfloat16),
            jax.ShapeDtypeStruct((kv_own * 2 * head, size), jnp.bfloat16),
        ],
        scratch_shapes=[pltpu.VMEM((size, size), jnp.float32)],
        compiler_params=pltpu.CompilerParams(vmem_limit_bytes=58 * 2**20),
        cost_estimate=pl.CostEstimate(flops=10**6, bytes_accessed=0, transcendentals=0),
    )(raw, raw, cosine, sine, gains, segments[None, :], segments[:, None])


def attend_back(
    raw, turned_q, turned_kv, grad, attended, logs, cosine, sine, gains, segments,
    kv_own, head, block, begin, count
):
    size = raw.shape[1]
    group = raw.shape[0] // head // kv_own - 2
    query = pl.BlockSpec((group * head, size), lambda i: (begin + i, 0))
    kv_at = group * kv_own // 2 + begin
    return pl.pallas_call(
        functools.partial(backward_kernel, block),
        grid=(count,),
        in_specs=[
            query,
            pl.BlockSpec((2 * head, size), lambda i: (kv_at + i, 0)),
            query,
            pl.BlockSpec((2 * head, size), lambda i: (begin + i, 0)),
            query,
            query,
            pl.BlockSpec((1, group, size), lambda i: (begin + i, 0, 0)),
            whole_spec(head // 2, size),
            whole_spec(head // 2, size),
            whole_spec(2, head, 1),
            whole_spec(1, size),
            whole_spec(size, 1),
        ],
        out_specs=[
            pl.BlockSpec((size, group * head), lambda i: (0, i)),
            pl.BlockSpec((size, 2 * head), lambda i: (0, i)),
            whole_spec(2, head, 1),
        ],
        out_shape=[
            jax.ShapeDtypeStruct((size, count * group * head), jnp.bfloat16),
            jax.ShapeDtypeStruct((size, count * 2 * head), jnp.bfloat16),
            jax.ShapeDtypeStruct((2, head, 1), jnp.float32),
        ],
        scratch_shapes=[
            pltpu.VMEM((size, size), jnp.float32),
            pltpu.VMEM((head, size), jnp.float32),
            pltpu.VMEM((head, size), jnp.float32),
        ],
        compiler_params=pltpu.CompilerParams(vmem_limit_bytes=58 * 2**20),
        cost_estimate=pl.CostEstimate(flops=10**6, bytes_accessed=0, transcendentals=0),
    )(
        raw, raw, turned_q, turned_kv, grad, attended, logs, cosine, sine, gains,
        segments[None, :], segments[:, None]
    )


def on_device_fast(
    hidden_in,
    out_grad,
    segment_ids,
    doc_positions,
    attn_gain,
    head_gains,
    w_query,
    w_key,
    w_value,
    w_out,
    ffn_gain,
    w_gate,
    w_up,
    w_down,
):
    low, full = jnp.bfloat16, jnp.float32
    dp, ctx = lax.axis_index("dp"), lax.axis_index("ctx")
    ctx_count = lax.axis_size("ctx")
    core, side, high = dp % 2, dp // 2 % 2, dp // 4
    width = hidden_in.shape[-1]
    rows = w_query.shape[0]
    head = head_gains.shape[0] * lax.axis_size("dp") * ctx_count // 2
    group = w_query.shape[1] // w_key.shape[1]
    kv_own = w_key.shape[1] // head // 2
    units = w_down.shape[0] * ctx_count

    tokens = hidden_in.shape[2]
    marks = jnp.stack(
        [segment_ids[:, 0], doc_positions[:, 0] // 256, doc_positions[:, 0] % 256], 1
    ).reshape(2, 1, -1)
    marks = jnp.pad(marks, ((0, 0), (0, 15), (0, width - 3 * tokens))).astype(low)
    x_came, x_kept = spread(jnp.concatenate([hidden_in[:, 0], marks], 1))

    head_few = head_gains.shape[0]
    gains = jnp.stack([attn_gain, ffn_gain, jnp.pad(head_gains, (0, rows - head_few))])
    gains = jnp.pad(gains, ((0, rows - 3), (0, 128 - rows)))
    key_value = jnp.stack([w_key.reshape(rows, -1, 2, head), w_value.reshape(rows, -1, 2, head)], 3)
    parities = [
        jnp.concatenate(
            [
                w_query.reshape(rows, -1, 2, group * head)[:, :, which].reshape(rows, -1),
                key_value[:, :, which].reshape(rows, -1),
                gains,
            ],
            1,
        )
        for which in range(2)
    ]
    inner = parities[0].shape[1]

    tops = w_gate.shape[1] // units // 4

    def of_member(which):
        return [
            jnp.concatenate(
                [w[:, (top * 4 + which) * units : (top * 4 + which + 1) * units] for top in range(tops)],
                1,
            )
            for w in (w_gate, w_up)
        ]

    def related(zero, one, two, three):
        near, far = choose(side, zero, two), choose(side, two, zero)
        near_far, far_far = choose(side, one, three), choose(side, three, one)
        return (
            choose(core, near, near_far),
            choose(core, far, far_far),
            choose(core, near_far, near),
            choose(core, far_far, far),
        )

    members = [of_member(which) for which in range(4)]
    gate_of = related(*[member[0] for member in members])
    up_of = related(*[member[1] for member in members])
    from_core = flip(
        joined(choose(core, parities[1], parities[0]), gate_of[2], up_of[2], gate_of[3], up_of[3]),
        CORE,
    )
    block = joined(
        choose(core, parities[0], from_core[0]),
        choose(core, from_core[0], parities[1]),
        jnp.pad(w_out, ((0, 0), (0, inner - width))),
    )
    from_side = flip(joined(gate_of[1], up_of[1], from_core[3], from_core[4]), SIDE)
    blocks = [block]
    for step in range(ctx_count - 1):
        blocks.append(spin(blocks[-1]))

    def across(pair):
        return [pair, flip(pair, SIDE), flip(pair, HIGH), flip(pair, SIDE | HIGH)]

    early = across(jnp.concatenate(blocks[:2], 0))
    blocks[3], w_down_late, *early = hold(blocks[3], w_down, *early)
    late = across(jnp.concatenate(blocks[2:], 0))
    block_ffn = unit_block(
        [side * 2 + core, side * 2 + 1 - core, 2 - side * 2 + core, 2 - side * 2 + 1 - core],
        joined(gate_of[0], up_of[0]), from_core, from_side, w_down_late,
    )
    block_ffn, *x_came = hold(block_ffn, *x_came)
    ffn_blocks = [block_ffn, spin(block_ffn)]
    x_half = order(ctx // 2, *settled(x_came, x_kept))
    x_other = flip(x_half, CORE)
    block_ffn, out_late, *late = hold(block_ffn, out_grad, *late)
    ffn_far = [flip(block_ffn, HIGH)]
    df_came, df_kept = spread(out_late[:, 0])
    pieces = [
        pair[3 * part : 3 * part + 3] for pairs in (early, late) for part in range(2) for pair in pairs
    ]

    slots = []
    for step in range(ctx_count):
        place = (ctx - step) % ctx_count
        for far in range(4):
            up = 1 - high if far >= 2 else high
            across_to = 1 - side if far % 2 == 1 else side
            chip = up * 2 + across_to
            slots += [(chip * 2 + c) * ctx_count + place for c in range(2)]
            slots += [chip * ctx_count + place]
    w_in, w_mine = placed(pieces, (0, 0, 1), slots, (8 * ctx_count, 4 * ctx_count))
    w_in, w_mine = w_in.reshape(-1, inner), w_mine.reshape(-1, inner)[:, :width]
    w_in, w_mine, x_other = hold(w_in, w_mine, x_other)
    w_theirs = flip(w_mine, CORE)
    features = inner - 128
    gains_all = w_in[:, features:].reshape(-1, rows, 128)[:, :3, :rows].astype(full)
    w_in = w_in[:, :features]
    attn_gain_all, ffn_gain_all = gains_all[:, 0].reshape(-1), gains_all[:, 1].reshape(-1)
    head_gains_all = gains_all[:, 2, :head_few].reshape(2, head, 1)

    x_all = order(core, x_half, x_other)
    marks = x_all[:, :, tokens, : 3 * tokens].reshape(-1, 3, tokens)
    x_all, x_half = x_all[:, :, :tokens].reshape(-1, width), x_half[:, :tokens].reshape(-1, width)
    segments = marks[:, 0].reshape(-1).astype(jnp.int32)
    places = (256.0 * marks[:, 1].astype(full) + marks[:, 2].astype(full)).reshape(-1)
    normed, _, _ = norm_forward(x_all.astype(full), attn_gain_all)
    a_low = normed.astype(low)
    raw = lax.dot_general(w_in, a_low, (((0,), (1,)), ((), ())), preferred_element_type=full)
    raw, ffn_blocks[1], ffn_far[0], w_theirs = hold(raw, ffn_blocks[1], ffn_far[0], w_theirs)
    ffn_blocks.append(spin(ffn_blocks[1]))
    ffn_far.append(flip(ffn_blocks[1], HIGH))
    freq = THETA ** (-(jnp.arange(head // 2, dtype=full) * 2.0 / head))
    turn = freq[:, None] * places[None, :]
    cosine, sine = jnp.cos(turn), jnp.sin(turn)
    attended, logs, turned_q, turned_kv = attend(
        raw, cosine, sine, head_gains_all, segments, kv_own, head, 256
    )
    attended_low = attended.astype(low)
    o_theirs = flip(half_of(1 - core, attended_low, 1), CORE)
    o_theirs, ffn_blocks[2], ffn_far[1], *df_came = hold(
        o_theirs, ffn_blocks[2], ffn_far[1], *df_came
    )
    df = order(ctx // 2, *settled(df_came, df_kept)).reshape(-1, width)
    df_side, df_core = flip(df, SIDE), flip(df, CORE)
    ffn_blocks.append(spin(ffn_blocks[2]))
    ffn_far.append(flip(ffn_blocks[2], HIGH))
    hidden = (
        x_half.astype(full)
        + left_trans(half_of(core, attended_low, 1), w_mine)
        + left_trans(o_theirs, w_theirs)
    )
    normed_two, h_unit, h_factor = norm_forward(hidden, ffn_gain_all)
    b_own = swap_halves(high, normed_two.astype(low), 1)
    b_own, df_core, ffn_blocks[3], ffn_far[2] = hold(b_own, df_core, ffn_blocks[3], ffn_far[2])
    b_side, b_core = flip(b_own, SIDE), flip(b_own, CORE)
    ffn_far.append(flip(ffn_blocks[3], HIGH))
    b_side, b_core, df_side, ffn_far[3] = hold(b_side, b_core, df_side, ffn_far[3])
    b_both, df_both = flip(b_side, CORE), flip(df_side, CORE)

    units_of = functools.partial(
        feed_forward,
        [(ctx - step) % ctx_count for step in range(ctx_count)] + [high],
        [block for pair in zip(ffn_blocks, ffn_far) for block in pair],
        rows,
    )
    *left, db_side, db_both, out_side, out_both = units_of(
        [b_side, b_both], [df_side, df_both], 256, 2, []
    )
    got_both, got_out_both = flip(db_both, CORE), flip(out_both, CORE)
    db_far = total_low(db_side, got_both)
    block_side = total_low(out_side, got_out_both)
    db_far, block_side, b_own, b_core = hold(db_far, block_side, b_own, b_core)
    got_side = flip(db_far, SIDE)
    act, d_pre, team_b, team_df, db_own, db_core, out_own, out_core = units_of(
        [b_own, b_core], [df, df_core], 256, 0, left
    )
    db_core, d_pre, act, block_side, got_side = hold(db_core, d_pre, act, block_side, got_side)
    got_core, got_out_core, got_block = flip(db_core, CORE), flip(out_core, CORE), flip(block_side, SIDE)

    def behind(step):
        return (ctx - 1 - step) % ctx_count

    g_down = left_trans(act, team_df).astype(low)
    g_down, team_b, got_core = hold(g_down, team_b, got_core)

    db = db_own.astype(full) + got_core.astype(full) + got_side.astype(full)
    db = swap_halves(high, db, 1)
    d_hidden, ffn_terms = norm_backward(db, h_unit, h_factor, ffn_gain_all)
    d_hidden = df.astype(full) + d_hidden
    dz = d_hidden.astype(low)
    dz, team_b = hold(dz, team_b)
    dz_other = flip(dz, CORE)
    g_ffn = left_trans(team_b, d_pre).astype(low)
    g_ffn, dz_other = hold(g_ffn, dz_other)
    dz_all = order(core, dz, dz_other).reshape(-1, width)
    d_attended = right_trans(w_mine, dz_all).astype(low)
    g_out = matmul(attended_low, dz_all).astype(low).reshape(2, 2, ctx_count, -1, width)
    g_out = jnp.stack([pick(g_out, behind(step), 2) for step in range(ctx_count)], 2)
    terms = spread_units(
        [behind(step) for step in range(ctx_count)] + [high], g_ffn, g_down, rows, ctx_count
    )
    *terms, d_attended, g_out, got_out_core, got_block = hold(
        *terms, d_attended, g_out, got_out_core, got_block
    )
    block_out = hidden + out_own.astype(full) + got_out_core.astype(full) + got_block.astype(full)
    block_came, block_kept = unspread(block_out.astype(low).reshape(2, -1, width))
    near_terms = terms[:ctx_count]
    far_got = [flip(term, HIGH) for term in terms[ctx_count:-1]]

    def side_square(array):
        near = jnp.where(side == 0, array[:, 0], array[:, 1])
        far = jnp.where(side == 0, array[:, 1], array[:, 0])
        near = joined(pick(near, high), pick(near, 1 - high))
        return near, flip(joined(pick(far, high), pick(far, 1 - high)), SIDE)

    def high_square(near, got):
        sums = near.astype(full) + got.astype(full)
        return sums[0], flip(sums[1].astype(low), HIGH)

    def total(terms):
        return functools.reduce(lambda a, b: a + b, [term.astype(full) for term in terms])

    back = functools.partial(
        attend_back, raw, turned_q, turned_kv, attended=attended, logs=logs, cosine=cosine,
        sine=sine, gains=head_gains_all, segments=segments, kv_own=kv_own, head=head, block=256
    )
    out_near, out_got = side_square(g_out)
    dq_one, dkv_one, g_heads_one = back(grad=d_attended, begin=0, count=kv_own // 2)
    dq_one, out_got, far_got[0], d_attended, *block_came = hold(
        dq_one, out_got, far_got[0], d_attended, *block_came
    )
    unit_total = total_low(near_terms[0], far_got[0])
    out_near, out_got = high_square(out_near, out_got)
    d_attended, unit_total = hold(d_attended, unit_total)
    unit_ring = spin(unit_total)
    dq_two, dkv_two, g_heads_two = back(
        grad=d_attended, begin=kv_own // 2, count=kv_own - kv_own // 2
    )
    g_heads = g_heads_one + g_heads_two
    dq_two, unit_ring, far_got[1], out_got, last_term = hold(
        dq_two, unit_ring, far_got[1], out_got, terms[-1]
    )
    far_got.append(flip(last_term, HIGH))
    unit_total = total_low(unit_ring, total_low(near_terms[1], far_got[1]))
    dq_two, unit_total = hold(dq_two, unit_total)
    unit_ring = spin(unit_total)
    d_raw = jnp.concatenate([dq_one, dq_two, dkv_one, dkv_two], 1)
    d_theirs = right_trans(half_of(1 - core, d_raw, 0), w_in).astype(low)
    d_theirs, d_raw = hold(d_theirs, d_raw)
    d_from = flip(d_theirs, CORE)
    d_inner = right_trans(half_of(core, d_raw, 0), w_in)
    d_inner, d_raw = hold(d_inner, d_raw)
    g_in = left_trans(a_low, d_raw).astype(low).reshape(2, 2, 2, ctx_count, rows, features)
    g_in, d_inner, d_from = hold(g_in, d_inner, d_from)
    d_inner = d_inner + d_from.astype(full)
    _, x_unit, x_factor = norm_forward(x_half.astype(full), attn_gain_all)
    d_input, attn_terms = norm_backward(d_inner, x_unit, x_factor, attn_gain_all)
    in_grad = (d_hidden + d_input).astype(low)

    g_gains = jnp.concatenate(
        [
            jnp.sum(attn_terms, 0).reshape(2, 2, 2, ctx_count, rows),
            jnp.sum(ffn_terms, 0).reshape(2, 2, 2, ctx_count, rows),
            g_heads.reshape(2, 2, 2, ctx_count, head_few),
        ],
        -1,
    ).astype(low)
    blank = ((0, 0), (0, 0), (0, 0), (0, 14), (0, width - g_gains.shape[-1]))
    g_gains = jnp.pad(jnp.moveaxis(g_gains, 2, 3), blank)
    g_in = jnp.moveaxis(g_in, 3, 2).reshape(2, 2, ctx_count, 2 * rows, features)
    g_in = jnp.concatenate([g_in, g_gains], 3)
    g_in = jnp.stack([pick(g_in, behind(step), 2) for step in range(ctx_count)], 2)
    g_in, in_grad = hold(g_in, in_grad)
    early_near, early_got = side_square(g_in[:, :, :2])
    late_near, late_got = side_square(g_in[:, :, 2:])
    in_came, in_kept = unspread(in_grad.reshape(2, -1, width))
    out_total = out_near + out_got.astype(full)
    unit_total = total_low(unit_ring, total_low(near_terms[2], far_got[2]))
    unit_ring = spin(unit_total)
    early_near, early_got = high_square(early_near, early_got)
    early_got, late_got, unit_ring, far_got[3] = hold(early_got, late_got, unit_ring, far_got[3])
    unit_total = total_low(unit_ring, total_low(near_terms[3], far_got[3]))
    ffn_total = jnp.concatenate(
        [unit_total[: 4 * rows], unit_total[4 * rows : 8 * rows]], 1
    ).reshape(2, 2, rows, -1)
    g_down = unit_total[8 * rows :, :width]

    found = [
        pick(pick(ffn_total, side), core),
        flip(pick(pick(ffn_total, side), 1 - core), CORE),
        flip(pick(pick(ffn_total, 1 - side), core), SIDE),
        flip(pick(pick(ffn_total, 1 - side), 1 - core), SIDE | CORE),
    ]
    late_near, late_got = high_square(late_near, late_got)

    def terms_of(near, got, first):
        terms = near + got.astype(full)
        return [jnp.concatenate([terms[at], out_total[first + at]], 0) for at in range(2)]

    in_terms = terms_of(early_near, early_got, 0)
    in_ring = spin(in_terms[0].astype(low))
    in_ring, late_got = hold(in_ring, late_got)
    in_terms += terms_of(late_near, late_got, 2)
    in_ring = spin((in_ring.astype(full) + in_terms[1]).astype(low))
    in_ring, *found = hold(in_ring, *found)
    in_ring = spin((in_ring.astype(full) + in_terms[2]).astype(low))
    in_ring, *in_came = hold(in_ring, *in_came)
    found = related(*found)
    found = (found[0], found[2], found[1], found[3])

    def to_columns(first):
        return jnp.concatenate(
            [
                found[which][:, (first + top) * units : (first + top + 1) * units].astype(full)
                for top in range(tops)
                for which in range(4)
            ],
            1,
        )

    g_gate, g_up = to_columns(0), to_columns(tops)

    in_sum = in_ring.astype(full) + in_terms[3]
    g_in, g_out = in_sum[: 2 * rows].astype(low).reshape(2, rows, width), in_sum[2 * rows + 16 :]
    g_gains = in_sum[2 * rows : 2 * rows + 16]
    g_in, *block_came = hold(g_in, *block_came)
    in_grad = order(ctx % 2, *settled(in_came, in_kept))
    block_out = order(ctx % 2, *settled(block_came, block_kept))
    own = pick(g_in, core).astype(full)
    got = flip(jnp.concatenate([pick(g_in, 1 - core), g_gains.astype(low)], 0), CORE).astype(full)
    g_gains = pick(g_gains[:2] + got[rows : rows + 2], core)
    got = got[:rows]
    even, odd = choose(core, own, got), choose(core, got, own)
    first = group * head * kv_own

    def mixed(start, stop, step, size):
        return jnp.concatenate(
            [part[:, at : at + size] for at in range(start, stop, step) for part in (even, odd)], 1
        )

    return (
        block_out[:, None],
        in_grad[:, None],
        g_gains[:rows],
        g_gains[2 * rows : 2 * rows + head_few],
        mixed(0, first, group * head, group * head),
        mixed(first, features, 2 * head, head),
        mixed(first + head, features, 2 * head, head),
        g_out,
        g_gains[rows : 2 * rows],
        g_gate,
        g_up,
        g_down.astype(full),
    )


def solution(mesh):
    placed = (
        P(None, "dp", "ctx", None),
        P(None, "dp", "ctx", None),
        P(None, "dp", "ctx"),
        P(None, "dp", "ctx"),
        P(("dp", "ctx")),
        P(("dp", "ctx")),
        P(("dp", "ctx"), None),
        P(("dp", "ctx"), None),
        P(("dp", "ctx"), None),
        P(("dp", "ctx"), None),
        P(("dp", "ctx")),
        P(("dp", "ctx"), None),
        P(("dp", "ctx"), None),
        P(("dp", "ctx"), None),
    )
    fits = mesh.shape["dp"] == 8 and mesh.shape["ctx"] == 4
    return jax.shard_map(
        on_device_fast if fits else on_device,
        mesh=mesh,
        in_specs=placed,
        out_specs=(
            P(None, "dp", "ctx", None),
            P(None, "dp", "ctx", None),
            P(("dp", "ctx")),
            P(("dp", "ctx")),
            P(("dp", "ctx"), None),
            P(("dp", "ctx"), None),
            P(("dp", "ctx"), None),
            P(("dp", "ctx"), None),
            P(("dp", "ctx")),
            P(("dp", "ctx"), None),
            P(("dp", "ctx"), None),
            P(("dp", "ctx"), None),
        ),
        check_vma=False,
    )
```
